128 devices in a mesh: group: 4 (over y), ctx: 4 (over x), tp: 8 (over z, core).
Axes of the slice: x: 4, y: 4, z: 4, core: 2. Of those that a mesh axis runs over, the one named last changes fastest.
Arguments:
- tokens: bfloat16 [2048, 8192], P('group', 'ctx'), may hold values from -200 to 200, as said below
- norm_gain: float32 [8192], P('ctx'), may hold values from 0.5 to 2
- w_query: bfloat16 [8192, 8192], P('ctx', 'tp'), may hold values from -0.25 to 0.25
- w_key: bfloat16 [8192, 1024], P('ctx', 'tp'), may hold values from -0.03125 to 0.03125
- w_value: bfloat16 [8192, 1024], P('ctx', 'tp'), may hold values from -0.03125 to 0.03125
- w_out: bfloat16 [8192, 8192], P('tp', 'ctx'), may hold values from -0.09375 to 0.09375
- kv_pool: bfloat16 [1024, 2, 8, 128, 128], P(('group', 'ctx'), None, 'tp'), may hold values from -80 to 80, as said below
- block_table: int32 [8, 256], replicated, may hold values from 0 to 1023, as said below
- prefix_len: int32 [8], replicated, may hold values from 8192 to 32768, as said below
- write_slot: int32 [8, 2], replicated, may hold values from 0 to 1023, as said below
Outputs:
- attention_out: bfloat16 [2048, 8192], P('group', ('ctx', 'tp'))
- new_pool: bfloat16 [1024, 2, 8, 128, 128], P(('group', 'ctx'), None, 'tp')
The draws below stay inside these ranges and needn't reach their ends.
Inputs may be any that keep to these rules, and one draw needn't show every extreme that they name: `tokens`: hidden states of order one to some hundreds. `kv_pool`: keys and values mostly of order one, a few up to some tens. `block_table`: entry = o * 64 + j: pool block j of the device at index o // (size of ctx) of group and o % (size of ctx) of ctx. The list slots handled by one device, those of the 2 sessions of its group index with slot number b such that b modulo the size of ctx equals its ctx index, lie exactly 8 on each pool device. Blocks may be shared by several slots and sessions. `prefix_len`: some session has 32768 prefix tokens and some has 8192. `write_slot`: all entries are distinct.
All inputs are finite; a program needn't handle non-finite values.
Results may differ from the reference program's by a relative error of at most 0.02.
The reference program's roundings to bfloat16 on the way count: a program that leaves them out, or rounds other values in their place, can miss the bound.
Values may be sent and summed in bfloat16 or wider, within the bound.
No kernel may reach another device: no remote copies, remote signals or barrier semaphores. Data moves between devices by JAX's collectives and lax.ppermute only.
A program may use at most 128 MiB of HBM per device.

```python
import math
import jax
import jax.numpy as jnp
from jax import lax

D = 8192
HEADS = 64
KVH = 8
HD = 128
NEW = 256
BLK = 128
MAXB = 256
SESS_GRP = 2
POOL = 64
SESSIONS = 8
TOKENS = 2048
POOL_ALL = 1024
NEWB = 2
N_GROUP = 4
N_CTX = 4
N_TP = 8


def draw_tokens(key, part):
    key = jax.random.fold_in(key, 11)
    base_key, row_key, col_key = jax.random.split(key, 3)
    trend = 3.0 ** (jnp.arange(D, dtype=jnp.float32) / D)
    base = jnp.clip(jax.random.normal(base_key, (TOKENS, D), jnp.float32), -6.0, 6.0)
    row_scales = jnp.exp(jax.random.uniform(row_key, (TOKENS, 1), jnp.float32, 0.0, jnp.log(10.0)))
    col_scales = trend[None, :] * jnp.exp(jax.random.uniform(col_key, (1, D), jnp.float32, 0.0, jnp.log(10.0)))
    return (base * row_scales * col_scales * 0.1).astype(jnp.bfloat16)


def draw_kv_pool(key, part):
    key = jax.random.fold_in(key, 12)
    base_key = jax.random.fold_in(key, 0)
    shape = (POOL_ALL, 2, KVH, BLK, HD)
    base = jnp.clip(jax.random.normal(base_key, shape, jnp.float32), -6.0, 6.0)
    return (0.6 * base).astype(jnp.bfloat16)


def draw_block_table(key, part):
    key = jax.random.fold_in(key, 13)
    owner_key, slot_key = jax.random.split(key)
    owners_count = N_GROUP * N_CTX
    per_device = SESS_GRP * MAXB // N_CTX
    base = jnp.repeat(jnp.arange(owners_count, dtype=jnp.int32), per_device // owners_count)
    shuffled = jax.vmap(lambda one_key: jax.random.permutation(one_key, base))(jax.random.split(owner_key, owners_count))
    owner_of = shuffled.reshape(N_GROUP, N_CTX, SESS_GRP, MAXB // N_CTX).transpose(0, 2, 3, 1).reshape(SESSIONS, MAXB)
    local_slot = jax.random.randint(slot_key, (SESSIONS, MAXB), 0, POOL)
    return (owner_of * POOL + local_slot).astype(jnp.int32)


def draw_prefix_len(key, part):
    key = jax.random.fold_in(key, 14)
    length_key, order_key = jax.random.split(key)
    shortest = MAXB * BLK // 4
    longest = MAXB * BLK
    drawn = jax.random.randint(length_key, (SESSIONS,), shortest, longest + 1)
    ordering = jax.random.permutation(order_key, SESSIONS)
    drawn = drawn.at[ordering[0]].set(longest).at[ordering[1]].set(shortest)
    return drawn.astype(jnp.int32)


def draw_write_slot(key, part):
    key = jax.random.fold_in(key, 15)
    chosen = jax.random.permutation(key, POOL_ALL)[:SESSIONS * NEWB]
    return chosen.reshape(SESSIONS, NEWB).astype(jnp.int32)


def with_spikes(values, key, source, target, blocks, factor):
    owner, partner = [(jnp.arange(values.shape[position]) // (values.shape[position] // blocks)).reshape([-1 if axis == position else 1 for axis in range(values.ndim)]) for position in (source, target)]
    chosen = jax.random.permutation(key, blocks)[partner]
    strong = (owner == chosen) | (owner == (partner + blocks // 2) % blocks)
    return jnp.where(strong, factor * values, values)


def shard_levels(rng, extent, pieces, low, largest):
    def one(dim, parts):
        steps = jax.random.uniform(jax.random.fold_in(jax.random.fold_in(rng, 6), dim), (parts,), jnp.float32, low / len(pieces), largest / len(pieces))
        return jnp.repeat(jnp.exp(steps), extent[dim] // parts).reshape((-1,) + (1,) * (len(extent) - dim - 1))

    factor_of = one(*pieces[0])
    for cut in pieces[1:]:
        factor_of = factor_of * one(*cut)
    return factor_of


def bell_draw(stream_key, extent, spread, limit, shards=(), kind=jnp.bfloat16):
    entries = jax.random.normal(stream_key, extent, jnp.float32) * spread
    if len(shards) > 0:
        entries = shard_levels(stream_key, extent, shards, -0.22, 0.18) * entries
    return jnp.clip(entries, min=-limit, max=limit).astype(kind)


def noise_with(stream_key, shape, width, bound, cuts, heavy, held_as=jnp.bfloat16):
    values = width * jax.random.normal(stream_key, shape, jnp.float32)
    if cuts:
        values = values * shard_levels(stream_key, shape, cuts, -0.22, 0.18)
    return jnp.clip(with_spikes(values, jax.random.fold_in(stream_key, 3), *heavy), -bound, bound).astype(held_as)


def setup_inputs(seed: int = 0) -> dict:
    key_list = jax.random.split(jax.random.key(seed), 11)
    tokens = draw_tokens(jax.random.fold_in(key_list[10], 71), 0)
    norm_gain = jnp.clip(jnp.exp(math.log(2.0) - 1.3862944 * jax.random.uniform(key_list[1], (D,), jnp.float32) ** shard_levels(key_list[1], (D,), ((0, 4),), -0.2, 0.2)), 0.5, 2.0)
    w_query = bell_draw(key_list[2], (D, HEADS * HD), (D // 16) ** -0.5, 0.25, ((0, 4), (1, 8)))
    w_key = bell_draw(key_list[3], (D, KVH * HD), (4 * D) ** -0.5, 0.03125, ((0, 4), (1, 8)))
    w_value = bell_draw(key_list[4], (D, KVH * HD), (4 * D) ** -0.5, 0.03125, ((0, 4), (1, 8)))
    w_out = noise_with(key_list[5], (HEADS * HD, D), (HEADS * HD) ** -0.5, 0.09375, ((0, 8), (1, 4)), (0, 1, 8, 2.0))
    kv_pool = draw_kv_pool(jax.random.fold_in(key_list[10], 71), 0)
    block_table = draw_block_table(jax.random.fold_in(key_list[10], 71), 0)
    prefix_len = draw_prefix_len(jax.random.fold_in(key_list[10], 71), 0)
    write_slot = draw_write_slot(jax.random.fold_in(key_list[10], 71), 0)
    return dict(tokens=tokens, norm_gain=norm_gain, w_query=w_query, w_key=w_key, w_value=w_value, w_out=w_out, kv_pool=kv_pool, block_table=block_table, prefix_len=prefix_len, write_slot=write_slot)


NEG_FILL = -1e+30

def project_all(tokens, norm_gain, w_query, w_key, w_value):
    wide_rows = tokens.astype(jnp.float32)
    row_scale = lax.rsqrt(lax.optimization_barrier(jnp.mean(wide_rows * wide_rows, axis=1, keepdims=True)) + 1e-05)
    normalized = (wide_rows * norm_gain[None, :]).astype(jnp.bfloat16)
    queries = (row_scale * jnp.dot(normalized, w_query, preferred_element_type=jnp.float32)).astype(jnp.bfloat16)
    keys_new = (row_scale * jnp.dot(normalized, w_key, preferred_element_type=jnp.float32)).astype(jnp.bfloat16)
    values_new = (row_scale * jnp.dot(normalized, w_value, preferred_element_type=jnp.float32)).astype(jnp.bfloat16)
    return (queries, keys_new, values_new)

def attend_head(inputs):
    query_rows, prefix_keys, prefix_values, fresh_keys, fresh_values, length = inputs
    row_count = query_rows.shape[0]
    group_size = row_count // NEW
    token_of_row = jnp.arange(row_count, dtype=jnp.int32) // group_size
    prefix_live = jnp.arange(prefix_keys.shape[0], dtype=jnp.int32) < length
    fresh_live = jnp.arange(NEW, dtype=jnp.int32)[None, :] <= token_of_row[:, None]
    live_mask = jnp.concatenate([jnp.broadcast_to(prefix_live[None, :], (row_count, prefix_keys.shape[0])), fresh_live], axis=1)
    all_keys = jnp.concatenate([prefix_keys, fresh_keys], axis=0)
    all_values = jnp.concatenate([prefix_values, fresh_values], axis=0)
    scores = jnp.dot(query_rows, all_keys.T, preferred_element_type=jnp.float32) * HD ** (-0.5)
    masked = jnp.where(live_mask, scores, NEG_FILL)
    row_top = lax.optimization_barrier(jnp.max(masked, axis=1, keepdims=True))
    weights = jnp.where(live_mask, jnp.exp(masked - row_top), 0.0)
    denominator = lax.optimization_barrier(jnp.sum(weights, axis=1, keepdims=True))
    mixed_rows = jnp.dot(weights.astype(jnp.bfloat16), all_values, preferred_element_type=jnp.float32) / denominator
    return mixed_rows.astype(jnp.bfloat16)

def reference(tokens, norm_gain, w_query, w_key, w_value, w_out, kv_pool, block_table, prefix_len, write_slot):
    queries, keys_new, values_new = project_all(tokens, norm_gain, w_query, w_key, w_value)
    group_size = HEADS // KVH
    query_sets = queries.reshape(SESSIONS, NEW, KVH, group_size, HD).transpose(0, 2, 1, 3, 4).reshape(SESSIONS, KVH, NEW * group_size, HD)
    fresh_k = keys_new.reshape(SESSIONS, NEW, KVH, HD).transpose(0, 2, 1, 3)
    fresh_v = values_new.reshape(SESSIONS, NEW, KVH, HD).transpose(0, 2, 1, 3)

    def one_session(inputs):
        query_set, table_row, length, session_k, session_v = inputs
        blocks = kv_pool[table_row]
        prefix_k = blocks[:, 0].transpose(1, 0, 2, 3).reshape(KVH, MAXB * BLK, HD)
        prefix_v = blocks[:, 1].transpose(1, 0, 2, 3).reshape(KVH, MAXB * BLK, HD)
        lengths = jnp.broadcast_to(length, (KVH,))
        return lax.map(attend_head, (query_set, prefix_k, prefix_v, session_k, session_v, lengths))
    attended = lax.map(one_session, (query_sets, block_table, prefix_len, fresh_k, fresh_v))
    attended = attended.reshape(SESSIONS, KVH, NEW, group_size, HD).transpose(0, 2, 1, 3, 4).reshape(TOKENS, HEADS * HD)
    block_cols = HEADS * HD // N_TP
    summed = jnp.zeros((TOKENS, D), jnp.float32)
    for member in range(N_TP):
        term_part = jnp.dot(attended[:, member * block_cols:(member + 1) * block_cols], w_out[member * block_cols:(member + 1) * block_cols], preferred_element_type=jnp.float32).astype(jnp.bfloat16)
        term_part = lax.optimization_barrier(term_part)
        summed = summed + term_part.astype(jnp.float32)
    attention_out = summed.astype(jnp.bfloat16)
    packed = jnp.stack([keys_new, values_new], axis=1).reshape(SESSIONS * NEWB, BLK, 2, KVH, HD).transpose(0, 2, 3, 1, 4)
    new_pool = kv_pool.at[write_slot.reshape(-1)].set(packed)
    return (attention_out, new_pool)
```

```python
import jax
import jax.numpy as jnp
from jax import lax
from jax.experimental import pallas as pl
from jax.experimental.pallas import tpu as pltpu
from jax.sharding import PartitionSpec as P

NEG_FILL = -1e30
LOG2E = 1.4426950408889634
F32 = jnp.float32
BF16 = jnp.bfloat16
VMEM_BYTES = 56 * 1024 * 1024
CHUNK = 4
CTX = 4
NT = (((1,), (1,)), ((), ()))


def params():
    return pltpu.CompilerParams(vmem_limit_bytes=VMEM_BYTES)


def vmem():
    return pl.BlockSpec(memory_space=pltpu.VMEM)


def smem():
    return pl.BlockSpec(memory_space=pltpu.SMEM)


def project_kernel(tok_ref, gain_ref, wq_ref, wk_ref, wv_ref, out_ref):
    wide = tok_ref[...].astype(F32)
    normalized = (wide * gain_ref[...]).astype(BF16)
    q_cols = wq_ref.shape[1]
    for j in range(0, q_cols, 256):
        out_ref[:, j : j + 256] = jnp.dot(
            normalized, wq_ref[:, j : j + 256], preferred_element_type=F32
        )
    out_ref[:, q_cols : q_cols + 128] = jnp.dot(
        normalized, wk_ref[...], preferred_element_type=F32
    )
    out_ref[:, q_cols + 128 : q_cols + 256] = jnp.dot(
        normalized, wv_ref[...], preferred_element_type=F32
    )
    squares = jnp.sum(wide * wide, axis=1, keepdims=True)
    out_ref[:, q_cols + 256 : q_cols + 384] = jnp.broadcast_to(
        squares, (tok_ref.shape[0], 128)
    )


def project(tokens, gain, w_query, w_key, w_value):
    rows = tokens.shape[0]
    cols = w_query.shape[1] + 384
    return pl.pallas_call(
        project_kernel,
        out_shape=jax.ShapeDtypeStruct((rows, cols), F32),
        in_specs=[vmem()] * 5,
        out_specs=vmem(),
        compiler_params=params(),
        cost_estimate=pl.CostEstimate(
            flops=2 * rows * cols * tokens.shape[1], bytes_accessed=10 << 20, transcendentals=0
        ),
        name="project",
    )(tokens, gain, w_query, w_key, w_value)


def finish_kernel(features, part_ref, out_ref):
    q_cols = out_ref.shape[1]
    total = part_ref[0]
    for c in range(1, part_ref.shape[0]):
        total = total + part_ref[c]
    scale = lax.rsqrt(total[:, q_cols : q_cols + 1] / features + 1e-05)
    out_ref[...] = (total[:, :q_cols] * scale).astype(BF16)


def finish(parts, features):
    count, rows, cols = parts.shape
    return pl.pallas_call(
        lambda *refs: finish_kernel(features, *refs),
        out_shape=jax.ShapeDtypeStruct((rows, cols - 128), BF16),
        in_specs=[vmem()],
        out_specs=vmem(),
        compiler_params=params(),
        name="finish",
    )(parts)


def update(q_ref, m_ref, l_ref, acc_ref, row0, new_len, head, keys, values_ext, mask, const, zero):
    rows = pl.ds(row0, new_len)
    cols = slice(head * 128, head * 128 + 128)
    scores = lax.dot_general(q_ref[rows, cols], keys, NT, preferred_element_type=F32)
    scores = jnp.where(mask, scores, NEG_FILL)
    m_old = m_ref[head, rows, :]
    m_new = jnp.maximum(m_old, jnp.max(scores, axis=1, keepdims=True))
    shift = m_new * const
    alpha = jnp.exp2(m_old * const - shift)
    reps = scores.shape[1] // 128
    weights = jnp.exp2(scores * const - jnp.concatenate([shift] * reps, axis=1))
    if zero:
        weights = jnp.where(mask, weights, 0.0)
    mixed = jnp.dot(weights.astype(BF16), values_ext, preferred_element_type=F32)
    m_ref[head, rows, :] = m_new
    l_ref[head, rows, :] = l_ref[head, rows, :] * alpha + mixed[:, 128:]
    acc_ref[rows, cols] = acc_ref[rows, cols] * alpha + mixed[:, :128]


def prefix_part(meta_ref, base, q_ref, buf_ref, vx_ref, m_ref, l_ref, acc_ref, new_len, const):
    blocks = buf_ref.shape[0]
    heads = m_ref.shape[0]
    span = CHUNK * 128
    vx_ref[:, :128] = buf_ref[:, 1].reshape(blocks * 128, 128)
    vx_ref[:, 128:] = jnp.ones((blocks * 128, 128), BF16)
    sessions = q_ref.shape[0] // new_len
    for session in range(sessions):
        first = meta_ref[base + 2 * session]
        keys_live = meta_ref[base + 2 * session + 1]
        high = first * 128 + keys_live

        def body(step, carry, first=first, high=high, row0=session * new_len):
            wanted = first + step * CHUNK
            begin = jnp.minimum(wanted, blocks - CHUNK)
            keys = buf_ref[pl.ds(begin, CHUNK), 0].reshape(span, 128)
            values_ext = vx_ref[pl.ds(pl.multiple_of(begin * 128, 128), span), :]
            index = begin * 128 + lax.broadcasted_iota(jnp.int32, (1, span), 1)
            mask = (index >= wanted * 128) & (index < high)
            for head in range(heads):
                update(
                    q_ref, m_ref, l_ref, acc_ref, row0, new_len, head, keys, values_ext, mask,
                    const, False,
                )
            return carry

        lax.fori_loop(0, (keys_live + span - 1) // span, body, 0)


def pack_lanes(ref, rows):
    lane = lax.broadcasted_iota(jnp.int32, (rows, 128), 1)
    packed = jnp.zeros((rows, 128), F32)
    for head in range(ref.shape[0]):
        packed = jnp.where(lane == head, ref[head], packed)
    return packed


def first_kernel(
    new_len, const, meta_ref, quarter_refs, kv_refs, buf_ref, q_ref, acc_ref, mp_ref, lp_ref,
    vx_ref, m_ref, l_ref,
):
    tokens = q_ref.shape[0]
    part = quarter_refs[0].shape[0]
    rank = meta_ref[0]
    q_cols = q_ref.shape[1]
    for step, ref in enumerate(quarter_refs):
        place = lax.rem(rank + CTX - step, CTX)
        q_ref[pl.ds(pl.multiple_of(place * part, part), part), :] = ref[:, :q_cols]
    m_ref[...] = jnp.full(m_ref.shape, NEG_FILL, F32)
    l_ref[...] = jnp.zeros(l_ref.shape, F32)
    acc_ref[...] = jnp.zeros(acc_ref.shape, F32)
    own = quarter_refs[0]
    keys = own[:, q_cols : q_cols + 128]
    values_ext = jnp.concatenate(
        [own[:, q_cols + 128 : q_cols + 256], jnp.ones((part, 128), BF16)], axis=1
    )
    per_session = new_len // part
    row0 = pl.multiple_of(lax.div(rank, per_session) * new_len, new_len)
    offset = lax.rem(rank, per_session) * part
    token = lax.broadcasted_iota(jnp.int32, (new_len, part), 0)
    fresh = lax.broadcasted_iota(jnp.int32, (new_len, part), 1) + offset
    mask = fresh <= token
    for head in range(m_ref.shape[0]):
        update(
            q_ref, m_ref, l_ref, acc_ref, row0, new_len, head, keys, values_ext, mask, const, True
        )
    prefix_part(meta_ref, 1, q_ref, buf_ref, vx_ref, m_ref, l_ref, acc_ref, new_len, const)
    mp_ref[...] = pack_lanes(m_ref, tokens)
    lp_ref[...] = pack_lanes(l_ref, tokens)


def load_state(acc_in, mp_in, lp_in, acc_ref, m_ref, l_ref):
    acc_ref[...] = acc_in[...]
    shape = m_ref.shape[1:]
    for head in range(m_ref.shape[0]):
        m_ref[head] = jnp.broadcast_to(mp_in[:, head : head + 1], shape)
        l_ref[head] = jnp.broadcast_to(lp_in[:, head : head + 1], shape)


def middle_kernel(
    new_len, const, meta_ref, q_ref, buf_refs, acc_in, mp_in, lp_in, acc_ref, mp_ref, lp_ref,
    vx_ref, m_ref, l_ref,
):
    load_state(acc_in, mp_in, lp_in, acc_ref, m_ref, l_ref)
    for n, buf_ref in enumerate(buf_refs):
        prefix_part(
            meta_ref, 4 * n, q_ref, buf_ref, vx_ref, m_ref, l_ref, acc_ref, new_len, const
        )
    tokens = q_ref.shape[0]
    mp_ref[...] = pack_lanes(m_ref, tokens)
    lp_ref[...] = pack_lanes(l_ref, tokens)


def last_kernel(
    new_len, const, meta_ref, q_ref, buf_refs, acc_in, mp_in, lp_in, out_ref, vx_ref, m_ref, l_ref,
    acc_ref,
):
    load_state(acc_in, mp_in, lp_in, acc_ref, m_ref, l_ref)
    for n, buf_ref in enumerate(buf_refs):
        prefix_part(
            meta_ref, 4 * n, q_ref, buf_ref, vx_ref, m_ref, l_ref, acc_ref, new_len, const
        )
    tokens = q_ref.shape[0]
    heads = m_ref.shape[0]
    part = tokens // CTX
    for head in range(heads):
        cols = slice(head * 128, head * 128 + 128)
        total = l_ref[head]
        empty = total == 0.0
        safe = jnp.where(empty, 1.0, total)
        done = (acc_ref[:, cols] / safe).astype(BF16)
        for c in range(CTX):
            out_ref[c, :part, cols] = done[c * part : (c + 1) * part]
        m_ref[head] = jnp.where(empty, NEG_FILL, m_ref[head] * const + jnp.log2(safe))
    packed = pack_lanes(m_ref, tokens)
    row = lax.broadcasted_iota(jnp.int32, (16, heads * 128), 0)
    for c in range(CTX):
        turned = packed[c * part : (c + 1) * part].T
        line = jnp.concatenate([turned[h : h + 1] for h in range(heads)], axis=1)
        high = line.astype(BF16).astype(F32)
        rest = line - high
        mid = rest.astype(BF16).astype(F32)
        low = rest - mid
        tile = jnp.where(row == 0, high, jnp.where(row == 1, mid, jnp.where(row == 2, low, 0.0)))
        out_ref[c, part : part + 16, :] = tile.astype(BF16)


def attend_cost(blocks, tokens, heads):
    pairs = blocks * 128 * tokens // 2 * heads
    return pl.CostEstimate(flops=pairs * 512, bytes_accessed=8 << 20, transcendentals=pairs)


def scratch(tokens, heads, blocks):
    return [
        pltpu.VMEM((blocks * 128, 256), BF16),
        pltpu.VMEM((heads, tokens, 128), F32),
        pltpu.VMEM((heads, tokens, 128), F32),
    ]


def state_shapes(tokens, q_cols):
    return [
        jax.ShapeDtypeStruct((tokens, q_cols), F32),
        jax.ShapeDtypeStruct((tokens, 128), F32),
        jax.ShapeDtypeStruct((tokens, 128), F32),
    ]


def attend_first(meta, quarters, buf, new_len, const):
    part = quarters[0].shape[0]
    q_cols = quarters[0].shape[1] - 256
    tokens = part * CTX
    heads = q_cols // 128

    def kernel(meta_ref, a, b, c, d, buf_ref, q_ref, acc, mp, lp, vx, m, l):
        first_kernel(
            new_len, const, meta_ref, [a, b, c, d], None, buf_ref, q_ref, acc, mp, lp, vx, m, l
        )

    return pl.pallas_call(
        kernel,
        out_shape=[jax.ShapeDtypeStruct((tokens, q_cols), BF16)] + state_shapes(tokens, q_cols),
        in_specs=[smem()] + [vmem()] * 5,
        out_specs=[vmem()] * 4,
        scratch_shapes=scratch(tokens, heads, buf.shape[0]),
        compiler_params=params(),
        cost_estimate=attend_cost(buf.shape[0], tokens, heads),
        name="attend_own",
    )(meta, *quarters, buf)


def attend_more(meta, queries, bufs, state, new_len, const, last):
    tokens, q_cols = queries.shape
    heads = q_cols // 128
    count = len(bufs)

    def kernel(meta_ref, q_ref, *refs):
        buf_refs = refs[:count]
        acc_in, mp_in, lp_in = refs[count : count + 3]
        rest = refs[count + 3 :]
        body = last_kernel if last else middle_kernel
        body(new_len, const, meta_ref, q_ref, buf_refs, acc_in, mp_in, lp_in, *rest)

    if last:
        out_shape = jax.ShapeDtypeStruct((CTX, tokens // CTX + 16, q_cols), BF16)
        out_specs = vmem()
        more = [pltpu.VMEM((tokens, q_cols), F32)]
    else:
        out_shape = state_shapes(tokens, q_cols)
        out_specs = [vmem()] * 3
        more = []
    return pl.pallas_call(
        kernel,
        out_shape=out_shape,
        in_specs=[smem()] + [vmem()] * (4 + count),
        out_specs=out_specs,
        scratch_shapes=scratch(tokens, heads, bufs[0].shape[0]) + more,
        compiler_params=params(),
        cost_estimate=attend_cost(bufs[0].shape[0] * count, tokens, heads),
        name="attend_last" if last else "attend_near",
    )(meta, queries, *bufs, *state)


def combine_kernel(in_ref, out_ref):
    part, q_cols = out_ref.shape
    heads = q_cols // 128
    lines = []
    for c in range(CTX):
        tile = in_ref[c, part : part + 16, :].astype(F32)
        lines.append(tile[0:1] + tile[1:2] + tile[2:3])
    top = lines[0]
    for line in lines[1:]:
        top = jnp.maximum(top, line)
    shares = [jnp.exp2(line - top) for line in lines]
    total = shares[0] + shares[1] + shares[2] + shares[3]
    pieces = []
    for share in shares:
        share = share / total
        pieces += [share[:, h * 128 : h * 128 + 128] for h in range(heads)]
    pieces.append(jnp.zeros((128 - CTX * heads, 128), F32))
    turned = jnp.concatenate(pieces, axis=0).T
    for head in range(heads):
        cols = slice(head * 128, head * 128 + 128)
        mixed = jnp.zeros((part, 128), F32)
        for c in range(CTX):
            at = c * heads + head
            mixed = mixed + in_ref[c, :part, cols].astype(F32) * turned[:, at : at + 1]
        out_ref[:, cols] = mixed.astype(BF16)


def combine(arrived):
    count, rows, q_cols = arrived.shape
    return pl.pallas_call(
        combine_kernel,
        out_shape=jax.ShapeDtypeStruct((rows - 16, q_cols), BF16),
        in_specs=[vmem()],
        out_specs=vmem(),
        compiler_params=params(),
        name="combine",
    )(arrived)


def out_kernel(meta_ref, a, b, c, d, w_ref, own_ref, send_ref, rows_ref):
    rank = meta_ref[0]
    core = meta_ref[1]
    part = a.shape[0]
    half = own_ref.shape[2]

    @pl.when(pl.program_id(0) == 0)
    def _():
        for step, ref in enumerate((a, b, c, d)):
            place = lax.rem(rank + CTX - step, CTX)
            rows_ref[pl.ds(pl.multiple_of(place * part, part), part), :] = ref[...]

    product = jnp.dot(rows_ref[...], w_ref[...], preferred_element_type=F32)

    @pl.when(core == 0)
    def _():
        own_ref[0] = product[:, :half]
        send_ref[0] = product[:, half:].astype(BF16)

    @pl.when(core != 0)
    def _():
        own_ref[0] = product[:, half:]
        send_ref[0] = product[:, :half].astype(BF16)


def project_out(meta, quarters, w_out, planes):
    part, depth = quarters[0].shape
    tokens = part * CTX
    width = w_out.shape[1] // planes
    whole = pl.BlockSpec((part, depth), lambda i: (0, 0))
    return pl.pallas_call(
        out_kernel,
        grid=(planes,),
        out_shape=[
            jax.ShapeDtypeStruct((planes, tokens, width // 2), F32),
            jax.ShapeDtypeStruct((planes, tokens, width // 2), BF16),
        ],
        in_specs=[smem(), whole, whole, whole, whole, pl.BlockSpec((depth, width), lambda i: (0, i))],
        out_specs=[pl.BlockSpec((1, tokens, width // 2), lambda i: (i, 0, 0))] * 2,
        scratch_shapes=[pltpu.VMEM((tokens, depth), BF16)],
        compiler_params=params(),
        cost_estimate=pl.CostEstimate(
            flops=2 * tokens * depth * w_out.shape[1], bytes_accessed=8 << 20, transcendentals=0
        ),
        name="project_out",
    )(meta, *quarters, w_out)


def shifted(value, axis, step):
    size = lax.axis_size(axis)
    return lax.ppermute(value, axis, [(i, (i + step) % size) for i in range(size)])


def around(value, axis):
    return [value] + [shifted(value, axis, step) for step in (1, 2, 3)]


def local(
    tokens, norm_gain, w_query, w_key, w_value, w_out, kv_pool, block_table, prefix_len, write_slot
):
    groups = lax.axis_size("group")
    ranks = lax.axis_size("ctx")
    tp_size = lax.axis_size("tp")
    rank = lax.axis_index("ctx")
    group = lax.axis_index("group")
    core = lax.axis_index("tp") % 2
    pool_size = kv_pool.shape[0]
    sessions, list_len = block_table.shape
    sess_here = sessions // groups
    per_pair = sess_here * list_len // (groups * ranks)
    new_len = tokens.shape[0] // sess_here
    head_dim = kv_pool.shape[4]
    const = head_dim**-0.5 * LOG2E
    device_id = group * ranks + rank
    pool = kv_pool.reshape(pool_size, 2, head_dim, head_dim)

    table = block_table.reshape(groups, sess_here * list_len)
    steps = jnp.arange(groups, dtype=jnp.int32)
    send_table = jnp.roll(table, -group, axis=0)
    here = send_table // pool_size == device_id
    upper = jnp.triu(jnp.ones((sess_here * list_len,) * 2, BF16))
    order = jnp.dot(here.astype(BF16), upper, preferred_element_type=F32).astype(jnp.int32)
    wanted = jnp.arange(1, per_pair + 1, dtype=jnp.int32)
    picked = here[:, None, :] & (order[:, None, :] == wanted[None, :, None])
    send_index = jnp.sum(jnp.where(picked, send_table[:, None, :] % pool_size, 0), axis=2)
    blocks = [pool[send_index[step]] for step in range(groups)]
    arrived = [blocks[0]] + [shifted(blocks[step], "group", step) for step in range(1, groups)]

    mine = lax.dynamic_index_in_dim(table, group, 0, keepdims=False).reshape(sess_here, list_len)
    lengths = lax.dynamic_slice_in_dim(prefix_len, group * sess_here, sess_here)
    source = ((group - steps) % groups) * ranks + rank
    from_there = mine[None] // pool_size == source[:, None, None]
    slots = jnp.arange(list_len, dtype=jnp.int32)
    keys_in = jnp.clip(lengths[:, None] - slots[None, :] * head_dim, 0, head_dim)
    live_keys = jnp.sum(jnp.where(from_there, keys_in[None], 0), axis=2)
    counts = jnp.sum(from_there.astype(jnp.int32), axis=2)
    starts = jnp.cumsum(counts, axis=1) - counts
    meta = jnp.stack([starts, live_keys], axis=2).reshape(groups, 2 * sess_here).astype(jnp.int32)

    parts = project(tokens, norm_gain[None, :], w_query, w_key, w_value)
    part_rows = tokens.shape[0] // ranks
    parts = parts.reshape(ranks, part_rows, parts.shape[1])
    parts = lax.all_to_all(parts, "ctx", split_axis=0, concat_axis=0, tiled=True)
    fresh = finish(parts, tokens.shape[1] * ranks)
    quarters = around(fresh, "ctx")
    q_cols = w_query.shape[1]

    first_meta = jnp.concatenate([rank[None].astype(jnp.int32), meta[0]])
    queries, *state = attend_first(first_meta, quarters, arrived[0], new_len, const)
    near_meta = jnp.concatenate([meta[1], meta[3]])
    state = attend_more(
        near_meta, queries, [arrived[1], arrived[3]], state, new_len, const, False
    )
    partial = attend_more(meta[2], queries, [arrived[2]], state, new_len, const, True)
    partial = lax.all_to_all(partial, "ctx", split_axis=0, concat_axis=0, tiled=True)
    attended = combine(partial)

    planes = tp_size // 2
    out_meta = jnp.stack([rank, core]).astype(jnp.int32)
    own, send = project_out(out_meta, around(attended, "ctx"), w_out, planes)
    other = lax.ppermute(send, "tp", [(i, i ^ 1) for i in range(tp_size)])
    pair = (own + other.astype(F32)).astype(BF16)
    terms = lax.all_to_all(
        pair,
        "tp",
        split_axis=0,
        concat_axis=0,
        axis_index_groups=[[2 * z + c for z in range(planes)] for c in range(2)],
        tiled=True,
    )
    attention_out = jnp.sum(terms.astype(F32), axis=0).astype(BF16)

    block = fresh[:, q_cols:].reshape(part_rows, 2, 1, head_dim).transpose(1, 2, 0, 3)
    every = lax.all_gather(block, ("group", "ctx"))
    targets = write_slot.reshape(-1)
    placement = jnp.where(targets // pool_size == device_id, targets % pool_size, pool_size)
    new_pool = kv_pool.at[placement].set(every, mode="drop")
    return (attention_out, new_pool)


def solution(mesh):
    placed = (
        P("group", "ctx"),
        P("ctx"),
        P("ctx", "tp"),
        P("ctx", "tp"),
        P("ctx", "tp"),
        P("tp", "ctx"),
        P(("group", "ctx"), None, "tp", None, None),
        P(),
        P(),
        P(),
    )
    return jax.shard_map(
        local,
        mesh=mesh,
        in_specs=placed,
        out_specs=(P("group", ("ctx", "tp")), P(("group", "ctx"), None, "tp", None, None)),
        check_vma=False,
    )
```

```python
import jax
import jax.numpy as jnp
from jax import lax
from jax.experimental import pallas as pl
from jax.experimental.pallas import tpu as pltpu
from jax.sharding import PartitionSpec as P

NEG_FILL = -1e30
LOG2E = 1.4426950408889634
F32 = jnp.float32
BF16 = jnp.bfloat16
VMEM_BYTES = 30 * 1024 * 1024
CHUNK = 4
TAIL = 2
ROOM = 60.0
CTX = 4
NT = (((1,), (1,)), ((), ()))


def params():
    return pltpu.CompilerParams(vmem_limit_bytes=VMEM_BYTES)


def vmem():
    return pl.BlockSpec(memory_space=pltpu.VMEM)


def smem():
    return pl.BlockSpec(memory_space=pltpu.SMEM)


def anywhere():
    return pl.BlockSpec(memory_space=pl.ANY)


def project_kernel(tok_ref, gain_ref, wq_ref, wk_ref, wv_ref, out_ref):
    wide = tok_ref[...].astype(F32)
    normalized = (wide * gain_ref[...]).astype(BF16)
    q_cols = wq_ref.shape[1]
    rows = tok_ref.shape[0]
    start = pl.program_id(0) == 0

    def add(cols, value):
        @pl.when(start)
        def _():
            out_ref[:, cols] = value

        @pl.when(jnp.logical_not(start))
        def _():
            out_ref[:, cols] += value

    for j in range(0, q_cols, 512):
        add(
            slice(j, j + 512),
            jnp.dot(normalized, wq_ref[:, j : j + 512], preferred_element_type=F32),
        )
    both = jnp.concatenate([wk_ref[...], wv_ref[...]], axis=1)
    add(slice(q_cols, q_cols + 256), jnp.dot(normalized, both, preferred_element_type=F32))
    squares = jnp.sum(wide * wide, axis=1, keepdims=True)
    add(slice(q_cols + 256, q_cols + 384), jnp.broadcast_to(squares, (rows, 128)))


def project(tokens, gain, w_query, w_key, w_value):
    rows, features = tokens.shape
    cols = w_query.shape[1] + 384
    deep = features // 4
    return pl.pallas_call(
        project_kernel,
        grid=(4,),
        out_shape=jax.ShapeDtypeStruct((rows, cols), F32),
        in_specs=[
            pl.BlockSpec((rows, deep), lambda i: (0, i)),
            pl.BlockSpec((1, deep), lambda i: (0, i)),
            pl.BlockSpec((deep, w_query.shape[1]), lambda i: (i, 0)),
            pl.BlockSpec((deep, 128), lambda i: (i, 0)),
            pl.BlockSpec((deep, 128), lambda i: (i, 0)),
        ],
        out_specs=pl.BlockSpec((rows, cols), lambda i: (0, 0)),
        compiler_params=params(),
        cost_estimate=pl.CostEstimate(
            flops=2 * rows * cols * features, bytes_accessed=10 << 20, transcendentals=0
        ),
        name="project",
    )(tokens, gain, w_query, w_key, w_value)


def finish_kernel(features, part_ref, out_ref, block_ref):
    q_cols = out_ref.shape[1]
    total = part_ref[0]
    for c in range(1, part_ref.shape[0]):
        total = total + part_ref[c]
    scale = lax.rsqrt(total[:, q_cols : q_cols + 1] / features + 1e-05)
    done = (total[:, :q_cols] * scale).astype(BF16)
    out_ref[...] = done
    block_ref[0] = done[:, q_cols - 256 : q_cols - 128]
    block_ref[1] = done[:, q_cols - 128 :]


def finish(parts, features):
    count, rows, cols = parts.shape
    return pl.pallas_call(
        lambda *refs: finish_kernel(features, *refs),
        out_shape=[
            jax.ShapeDtypeStruct((rows, cols - 128), BF16),
            jax.ShapeDtypeStruct((2, rows, 128), BF16),
        ],
        in_specs=[vmem()],
        out_specs=[vmem()] * 2,
        compiler_params=params(),
        name="finish",
    )(parts)


def pack_kernel(index_ref, pool_ref, out_ref, sem):
    for n in range(out_ref.shape[0]):
        pltpu.make_async_copy(pool_ref.at[index_ref[n]], out_ref.at[n], sem).start()
    pltpu.make_async_copy(out_ref, out_ref, sem).wait()


def pack(index, pool):
    count = index.shape[0]
    return pl.pallas_call(
        pack_kernel,
        out_shape=jax.ShapeDtypeStruct((count,) + pool.shape[1:], BF16),
        in_specs=[smem(), anywhere()],
        out_specs=anywhere(),
        scratch_shapes=[pltpu.SemaphoreType.DMA(())],
        compiler_params=params(),
        name="pack",
    )(index, pool)


def pack_lanes(ref, rows):
    lane = lax.broadcasted_iota(jnp.int32, (ref.shape[1], 128), 1)[: ref[0, rows, :].shape[0]]
    packed = jnp.zeros(lane.shape, F32)
    for head in range(ref.shape[0]):
        packed = jnp.where(lane == head, ref[head, rows, :], packed)
    return packed


def sweep(q_ref, rows, heads, keys, finish_head):
    pending = None
    for head in range(heads):
        cols = slice(head * 128, head * 128 + 128)
        scores = lax.dot_general(q_ref[rows, cols], keys, NT, preferred_element_type=F32)
        if pending is not None:
            finish_head(*pending)
        pending = (head, cols, scores)
    finish_head(*pending)


def moving(q_ref, m_ref, l_ref, acc_ref, rows, keys, values_ext, mask, const, zero):
    def finish_head(head, cols, scores):
        scores = jnp.where(mask, scores, NEG_FILL)
        m_old = m_ref[head, rows, :]
        m_new = jnp.maximum(m_old, jnp.max(scores, axis=1, keepdims=True) * const)
        alpha = jnp.exp2(m_old - m_new)
        reps = scores.shape[1] // 128
        weights = jnp.exp2(scores * const - jnp.concatenate([m_new] * reps, axis=1))
        if zero:
            weights = jnp.where(mask, weights, 0.0)
        mixed = jnp.dot(weights.astype(BF16), values_ext, preferred_element_type=F32)
        m_ref[head, rows, :] = m_new
        l_ref[head, rows, :] = l_ref[head, rows, :] * alpha + mixed[:, 128:]
        acc_ref[rows, cols] = acc_ref[rows, cols] * alpha + mixed[:, :128]

    sweep(q_ref, rows, m_ref.shape[0], keys, finish_head)


def steady(q_ref, m_ref, l_ref, acc_ref, rows, keys, values_ext, mask, const):
    def finish_head(head, cols, scores):
        if mask is not None:
            scores = jnp.where(mask, scores, NEG_FILL)
        reps = scores.shape[1] // 128
        shift = jnp.concatenate([m_ref[head, rows, :]] * reps, axis=1)
        weights = jnp.exp2(scores * const - shift)
        mixed = jnp.dot(weights.astype(BF16), values_ext, preferred_element_type=F32)
        l_ref[head, rows, :] += mixed[:, 128:]
        acc_ref[rows, cols] += mixed[:, :128]

    sweep(q_ref, rows, m_ref.shape[0], keys, finish_head)


def prefix_part(meta_ref, base, q_ref, qn_ref, kv_ref, vx_ref, m_ref, l_ref, acc_ref, new_len, const):
    blocks = kv_ref.shape[0]
    state = (q_ref, m_ref, l_ref, acc_ref)
    all_keys = kv_ref[:, 0].reshape(blocks * 128, 128)
    vx_ref[:, :128] = kv_ref[:, 1].reshape(blocks * 128, 128)
    vx_ref[:, 128:] = jnp.ones((blocks * 128, 128), BF16)
    norms = jnp.dot(all_keys * all_keys, jnp.ones((128, 128), BF16), preferred_element_type=F32)
    reach = jnp.sqrt(jnp.max(norms)) * (1.05 * const)

    def session_body(session, carry):
        row0 = pl.multiple_of(session * new_len, new_len)
        rows = pl.ds(row0, new_len)
        first = meta_ref[base + 2 * session]
        keys_live = meta_ref[base + 2 * session + 1]
        high = first * 128 + keys_live
        total = (keys_live + 127) // 128

        def enough():
            room = qn_ref[rows, :] * reach - pack_lanes(m_ref, rows)
            return (jnp.max(room) <= ROOM).astype(jnp.int32)

        def piece(wanted, count, masked):
            span = count * 128
            begin = jnp.minimum(wanted, blocks - count)
            keys = kv_ref[pl.ds(begin, count), 0].reshape(span, 128)
            values_ext = vx_ref[pl.ds(pl.multiple_of(begin * 128, 128), span), :]
            if not masked:
                return keys, values_ext, None
            index = begin * 128 + lax.broadcasted_iota(jnp.int32, (1, span), 1)
            return keys, values_ext, (index >= wanted * 128) & (index < high)

        def slow_more(now):
            return (now[0] < total) & (now[1] == 0)

        def slow(now):
            moving(*state, rows, *piece(first + now[0], CHUNK, True), const, False)
            return now[0] + CHUNK, enough()

        done, _ = lax.while_loop(slow_more, slow, (0, enough()))
        full = jnp.maximum(keys_live - done * 128, 0) // (CHUNK * 128)

        def fast(step, carry):
            steady(*state, rows, *piece(first + done + step * CHUNK, CHUNK, False), const)
            return carry

        lax.fori_loop(0, full, fast, 0)
        done = done + full * CHUNK

        def tail(step, carry):
            steady(*state, rows, *piece(first + done + step * TAIL, TAIL, True), const)
            return carry

        lax.fori_loop(0, (jnp.maximum(total - done, 0) + TAIL - 1) // TAIL, tail, 0)
        return carry

    lax.fori_loop(0, q_ref.shape[0] // new_len, session_body, 0)


def first_kernel(
    new_len, const, meta_ref, index_ref, a, b, c, d, pool_ref,
    q_ref, qn_ref, acc_ref, mp_ref, lp_ref, kv_ref, vx_ref, m_ref, l_ref, sem,
):
    blocks = kv_ref.shape[0]
    for n in range(blocks):
        pltpu.make_async_copy(pool_ref.at[index_ref[n]], kv_ref.at[n], sem).start()
    tokens, q_cols = q_ref.shape
    part = a.shape[0]
    heads = m_ref.shape[0]
    rank = meta_ref[0]
    for step, ref in enumerate((a, b, c, d)):
        place = lax.rem(rank + CTX - step, CTX)
        q_ref[pl.ds(pl.multiple_of(place * part, part), part), :] = ref[:, :q_cols]
    m_ref[...] = jnp.full(m_ref.shape, NEG_FILL, F32)
    l_ref[...] = jnp.zeros(l_ref.shape, F32)
    acc_ref[...] = jnp.zeros(acc_ref.shape, F32)
    lane = lax.broadcasted_iota(jnp.int32, (tokens, 128), 1)
    squares = jnp.zeros((tokens, 128), F32)
    for head in range(heads):
        wide = q_ref[:, head * 128 : head * 128 + 128].astype(F32)
        squares = jnp.where(lane == head, jnp.sum(wide * wide, axis=1, keepdims=True), squares)
    qn_ref[...] = jnp.sqrt(squares)
    keys = a[:, q_cols : q_cols + 128]
    values_ext = jnp.concatenate(
        [a[:, q_cols + 128 : q_cols + 256], jnp.ones((part, 128), BF16)], axis=1
    )
    per_session = new_len // part
    rows = pl.ds(pl.multiple_of(lax.div(rank, per_session) * new_len, new_len), new_len)
    offset = lax.rem(rank, per_session) * part
    token = lax.broadcasted_iota(jnp.int32, (new_len, part), 0)
    fresh = lax.broadcasted_iota(jnp.int32, (new_len, part), 1) + offset
    moving(q_ref, m_ref, l_ref, acc_ref, rows, keys, values_ext, fresh <= token, const, True)
    pltpu.make_async_copy(kv_ref, kv_ref, sem).wait()
    prefix_part(
        meta_ref, 1, q_ref, qn_ref, kv_ref, vx_ref, m_ref, l_ref, acc_ref, new_len, const
    )
    mp_ref[...] = pack_lanes(m_ref, slice(None))
    lp_ref[...] = pack_lanes(l_ref, slice(None))


def load_state(mp_in, lp_in, m_ref, l_ref):
    shape = m_ref.shape[1:]
    for head in range(m_ref.shape[0]):
        m_ref[head] = jnp.broadcast_to(mp_in[:, head : head + 1], shape)
        l_ref[head] = jnp.broadcast_to(lp_in[:, head : head + 1], shape)


def sources(
    new_len, const, meta_ref, q_ref, qn_ref, bufs, acc_in, mp_in, lp_in,
    acc_ref, kv_ref, vx_ref, m_ref, l_ref, sems,
):
    copies = []
    for n, buf in enumerate(bufs):
        copies.append(pltpu.make_async_copy(buf, kv_ref.at[n], sems.at[n]))
        copies[-1].start()
    acc_ref[...] = acc_in[...]
    load_state(mp_in, lp_in, m_ref, l_ref)
    for n, copy in enumerate(copies):
        copy.wait()
        prefix_part(
            meta_ref, 4 * n, q_ref, qn_ref, kv_ref.at[n], vx_ref, m_ref, l_ref, acc_ref, new_len,
            const,
        )


def near_kernel(
    new_len, const, meta_ref, q_ref, qn_ref, acc_in, mp_in, lp_in, buf_a, buf_b, pool_ref,
    acc_ref, mp_ref, lp_ref, pool_out, kv_ref, vx_ref, m_ref, l_ref, sems, pool_sem,
):
    keep = pltpu.make_async_copy(pool_ref, pool_out, pool_sem)
    keep.start()
    sources(
        new_len, const, meta_ref, q_ref, qn_ref, (buf_a, buf_b), acc_in, mp_in, lp_in,
        acc_ref, kv_ref, vx_ref, m_ref, l_ref, sems,
    )
    mp_ref[...] = pack_lanes(m_ref, slice(None))
    lp_ref[...] = pack_lanes(l_ref, slice(None))
    keep.wait()


def last_kernel(
    new_len, const, meta_ref, place_ref, q_ref, qn_ref, acc_in, mp_in, lp_in, buf,
    new_a, new_b, new_c, new_d, pool_in, out_ref, pool_out,
    acc_ref, kv_ref, vx_ref, m_ref, l_ref, sems, new_sems,
):
    def place(act):
        count = new_a.shape[0]
        for n, ref in enumerate((new_a, new_b, new_c, new_d)):
            for i in range(count):
                at = n * count + i
                slot = place_ref[at]

                @pl.when(slot >= 0)
                def _(ref=ref, i=i, at=at, slot=slot):
                    act(pltpu.make_async_copy(ref.at[i], pool_out.at[slot], new_sems.at[at]))

    place(lambda copy: copy.start())
    sources(
        new_len, const, meta_ref, q_ref, qn_ref, (buf,), acc_in, mp_in, lp_in,
        acc_ref, kv_ref, vx_ref, m_ref, l_ref, sems,
    )
    tokens = q_ref.shape[0]
    heads = m_ref.shape[0]
    part = tokens // CTX
    for head in range(heads):
        cols = slice(head * 128, head * 128 + 128)
        total = l_ref[head]
        empty = total == 0.0
        safe = jnp.where(empty, 1.0, total)
        done = (acc_ref[:, cols] / safe).astype(BF16)
        for c in range(CTX):
            out_ref[c, :part, cols] = done[c * part : (c + 1) * part]
        m_ref[head] = jnp.where(empty, NEG_FILL, m_ref[head] + jnp.log2(safe))
    packed = pack_lanes(m_ref, slice(None))
    row = lax.broadcasted_iota(jnp.int32, (16, heads * 128), 0)
    for c in range(CTX):
        turned = packed[c * part : (c + 1) * part].T
        line = jnp.concatenate([turned[h : h + 1] for h in range(heads)], axis=1)
        high = line.astype(BF16).astype(F32)
        rest = line - high
        mid = rest.astype(BF16).astype(F32)
        low = rest - mid
        tile = jnp.where(row == 0, high, jnp.where(row == 1, mid, jnp.where(row == 2, low, 0.0)))
        out_ref[c, part : part + 16, :] = tile.astype(BF16)
    place(lambda copy: copy.wait())


def attend_cost(blocks, tokens, heads):
    pairs = blocks * 128 * tokens // 2 * heads
    return pl.CostEstimate(flops=pairs * 512, bytes_accessed=8 << 20, transcendentals=pairs)


def scratch(tokens, heads, blocks, lead=()):
    return [
        pltpu.VMEM(lead + (blocks, 2, 128, 128), BF16),
        pltpu.VMEM((blocks * 128, 256), BF16),
        pltpu.VMEM((heads, tokens, 128), F32),
        pltpu.VMEM((heads, tokens, 128), F32),
    ]


def state_shapes(tokens, q_cols):
    return [
        jax.ShapeDtypeStruct((tokens, q_cols), F32),
        jax.ShapeDtypeStruct((tokens, 128), F32),
        jax.ShapeDtypeStruct((tokens, 128), F32),
    ]


def attend_own(meta, index, quarters, pool, new_len, const):
    part = quarters[0].shape[0]
    q_cols = quarters[0].shape[1] - 256
    tokens = part * CTX
    heads = q_cols // 128
    blocks = index.shape[0]
    return pl.pallas_call(
        lambda *refs: first_kernel(new_len, const, *refs),
        out_shape=[
            jax.ShapeDtypeStruct((tokens, q_cols), BF16),
            jax.ShapeDtypeStruct((tokens, 128), F32),
        ]
        + state_shapes(tokens, q_cols),
        in_specs=[smem(), smem()] + [vmem()] * 4 + [anywhere()],
        out_specs=[vmem()] * 5,
        scratch_shapes=scratch(tokens, heads, blocks) + [pltpu.SemaphoreType.DMA(())],
        compiler_params=params(),
        cost_estimate=attend_cost(blocks, tokens, heads),
        name="attend_own",
    )(meta, index, *quarters, pool)


def attend_near(meta, queries, norms, state, bufs, pool, new_len, const):
    tokens, q_cols = queries.shape
    heads = q_cols // 128
    blocks = bufs[0].shape[0]
    return pl.pallas_call(
        lambda *refs: near_kernel(new_len, const, *refs),
        out_shape=state_shapes(tokens, q_cols) + [jax.ShapeDtypeStruct(pool.shape, BF16)],
        in_specs=[smem()] + [vmem()] * 5 + [anywhere()] * 3,
        out_specs=[vmem()] * 3 + [anywhere()],
        scratch_shapes=scratch(tokens, heads, blocks, (2,))
        + [pltpu.SemaphoreType.DMA((2,)), pltpu.SemaphoreType.DMA(())],
        compiler_params=params(),
        cost_estimate=attend_cost(2 * blocks, tokens, heads),
        name="attend_near",
    )(meta, queries, norms, *state, *bufs, pool)


def attend_last(meta, places, queries, norms, state, buf, news, pool, new_len, const):
    tokens, q_cols = queries.shape
    heads = q_cols // 128
    blocks = buf.shape[0]
    return pl.pallas_call(
        lambda *refs: last_kernel(new_len, const, *refs),
        out_shape=[
            jax.ShapeDtypeStruct((CTX, tokens // CTX + 16, q_cols), BF16),
            jax.ShapeDtypeStruct(pool.shape, BF16),
        ],
        in_specs=[smem(), smem()] + [vmem()] * 5 + [anywhere()] * 6,
        out_specs=[vmem(), anywhere()],
        scratch_shapes=[pltpu.VMEM((tokens, q_cols), F32)]
        + scratch(tokens, heads, blocks, (1,))
        + [pltpu.SemaphoreType.DMA((1,)), pltpu.SemaphoreType.DMA((places.shape[0],))],
        input_output_aliases={12: 1},
        compiler_params=params(),
        cost_estimate=attend_cost(blocks, tokens, heads),
        name="attend_last",
    )(meta, places, queries, norms, *state, buf, *news, pool)


def combine_kernel(in_ref, out_ref):
    part, q_cols = out_ref.shape
    heads = q_cols // 128
    lines = []
    for c in range(CTX):
        tile = in_ref[c, part : part + 16, :].astype(F32)
        lines.append(tile[0:1] + tile[1:2] + tile[2:3])
    top = lines[0]
    for line in lines[1:]:
        top = jnp.maximum(top, line)
    shares = [jnp.exp2(line - top) for line in lines]
    total = shares[0] + shares[1] + shares[2] + shares[3]
    pieces = []
    for share in shares:
        share = share / total
        pieces += [share[:, h * 128 : h * 128 + 128] for h in range(heads)]
    pieces.append(jnp.zeros((128 - CTX * heads, 128), F32))
    turned = jnp.concatenate(pieces, axis=0).T
    for head in range(heads):
        cols = slice(head * 128, head * 128 + 128)
        mixed = jnp.zeros((part, 128), F32)
        for c in range(CTX):
            at = c * heads + head
            mixed = mixed + in_ref[c, :part, cols].astype(F32) * turned[:, at : at + 1]
        out_ref[:, cols] = mixed.astype(BF16)


def combine(arrived):
    count, rows, q_cols = arrived.shape
    return pl.pallas_call(
        combine_kernel,
        out_shape=jax.ShapeDtypeStruct((rows - 16, q_cols), BF16),
        in_specs=[vmem()],
        out_specs=vmem(),
        compiler_params=params(),
        name="combine",
    )(arrived)


def out_kernel(meta_ref, a, b, c, d, w_ref, own_ref, send_ref, rows_ref):
    rank = meta_ref[0]
    core = meta_ref[1]
    part = a.shape[0]
    half = own_ref.shape[2]

    @pl.when(pl.program_id(0) == 0)
    def _():
        for step, ref in enumerate((a, b, c, d)):
            place = lax.rem(rank + CTX - step, CTX)
            rows_ref[pl.ds(pl.multiple_of(place * part, part), part), :] = ref[...]

    product = jnp.dot(rows_ref[...], w_ref[...], preferred_element_type=F32)

    @pl.when(core == 0)
    def _():
        own_ref[0] = product[:, :half]
        send_ref[0] = product[:, half:].astype(BF16)

    @pl.when(core != 0)
    def _():
        own_ref[0] = product[:, half:]
        send_ref[0] = product[:, :half].astype(BF16)


def project_out(meta, quarters, w_out, planes):
    part, depth = quarters[0].shape
    tokens = part * CTX
    width = w_out.shape[1] // planes
    whole = pl.BlockSpec((part, depth), lambda i: (0, 0))
    return pl.pallas_call(
        out_kernel,
        grid=(planes,),
        out_shape=[
            jax.ShapeDtypeStruct((planes, tokens, width // 2), F32),
            jax.ShapeDtypeStruct((planes, tokens, width // 2), BF16),
        ],
        in_specs=[smem(), whole, whole, whole, whole, pl.BlockSpec((depth, width), lambda i: (0, i))],
        out_specs=[pl.BlockSpec((1, tokens, width // 2), lambda i: (i, 0, 0))] * 2,
        scratch_shapes=[pltpu.VMEM((tokens, depth), BF16)],
        compiler_params=params(),
        cost_estimate=pl.CostEstimate(
            flops=2 * tokens * depth * w_out.shape[1], bytes_accessed=8 << 20, transcendentals=0
        ),
        name="project_out",
    )(meta, *quarters, w_out)


def shifted(value, axis, step):
    size = lax.axis_size(axis)
    return lax.ppermute(value, axis, [(i, (i + step) % size) for i in range(size)])


def around(value, axis):
    return [value] + [shifted(value, axis, step) for step in (1, 2, 3)]


def local(
    tokens, norm_gain, w_query, w_key, w_value, w_out, kv_pool, block_table, prefix_len, write_slot
):
    groups = lax.axis_size("group")
    ranks = lax.axis_size("ctx")
    tp_size = lax.axis_size("tp")
    rank = lax.axis_index("ctx")
    group = lax.axis_index("group")
    core = lax.axis_index("tp") % 2
    pool_size = kv_pool.shape[0]
    sessions, list_len = block_table.shape
    sess_here = sessions // groups
    per_pair = sess_here * list_len // (groups * ranks)
    new_len = tokens.shape[0] // sess_here
    head_dim = kv_pool.shape[4]
    const = head_dim**-0.5 * LOG2E
    device_id = group * ranks + rank
    pool = kv_pool.reshape(pool_size, 2, head_dim, head_dim)

    table = block_table.reshape(groups, sess_here * list_len)
    steps = jnp.arange(groups, dtype=jnp.int32)
    send_table = jnp.roll(table, -group, axis=0)
    here = send_table // pool_size == device_id
    upper = jnp.triu(jnp.ones((sess_here * list_len,) * 2, BF16))
    order = jnp.dot(here.astype(BF16), upper, preferred_element_type=F32).astype(jnp.int32)
    wanted = jnp.arange(1, per_pair + 1, dtype=jnp.int32)
    picked = here[:, None, :] & (order[:, None, :] == wanted[None, :, None])
    send_index = jnp.sum(jnp.where(picked, send_table[:, None, :] % pool_size, 0), axis=2)
    blocks = {step: pack(send_index[step], pool) for step in (1, 3, 2)}
    arrived = {step: shifted(blocks[step], "group", step) for step in (1, 3, 2)}

    mine = lax.dynamic_index_in_dim(table, group, 0, keepdims=False).reshape(sess_here, list_len)
    lengths = lax.dynamic_slice_in_dim(prefix_len, group * sess_here, sess_here)
    source = ((group - steps) % groups) * ranks + rank
    from_there = mine[None] // pool_size == source[:, None, None]
    slots = jnp.arange(list_len, dtype=jnp.int32)
    keys_in = jnp.clip(lengths[:, None] - slots[None, :] * head_dim, 0, head_dim)
    live_keys = jnp.sum(jnp.where(from_there, keys_in[None], 0), axis=2)
    counts = jnp.sum(from_there.astype(jnp.int32), axis=2)
    starts = jnp.cumsum(counts, axis=1) - counts
    meta = jnp.stack([starts, live_keys], axis=2).reshape(groups, 2 * sess_here).astype(jnp.int32)

    tokens, _ = lax.optimization_barrier((tokens, blocks))
    parts = project(tokens, norm_gain[None, :], w_query, w_key, w_value)
    part_rows = tokens.shape[0] // ranks
    parts = parts.reshape(ranks, part_rows, parts.shape[1])
    parts = lax.all_to_all(parts, "ctx", split_axis=0, concat_axis=0, tiled=True)
    fresh, block = finish(parts, tokens.shape[1] * ranks)
    quarters = around(fresh, "ctx")
    news = around(jnp.stack(around(block, "group")), "ctx")
    targets = write_slot.reshape(groups, ranks)
    targets = jnp.stack(
        [targets[(group - g) % groups, (rank - c) % ranks] for c in range(ranks) for g in range(groups)]
    )
    places = jnp.where(targets // pool_size == device_id, targets % pool_size, -1)

    first_meta = jnp.concatenate([rank[None].astype(jnp.int32), meta[0]])
    queries, norms, *state = attend_own(
        first_meta, send_index[0], quarters, pool, new_len, const
    )
    near_meta = jnp.concatenate([meta[1], meta[3]])
    *state, new_pool = attend_near(
        near_meta, queries, norms, state, [arrived[1], arrived[3]], pool, new_len, const
    )
    partial, new_pool = attend_last(
        meta[2], places, queries, norms, state, arrived[2], news, new_pool, new_len, const
    )
    partial = lax.all_to_all(partial, "ctx", split_axis=0, concat_axis=0, tiled=True)
    attended = combine(partial)

    planes = tp_size // 2
    out_meta = jnp.stack([rank, core]).astype(jnp.int32)
    own, send = project_out(out_meta, around(attended, "ctx"), w_out, planes)
    other = lax.ppermute(send, "tp", [(i, i ^ 1) for i in range(tp_size)])
    pair = (own + other.astype(F32)).astype(BF16)
    terms = lax.all_to_all(
        pair,
        "tp",
        split_axis=0,
        concat_axis=0,
        axis_index_groups=[[2 * z + c for z in range(planes)] for c in range(2)],
        tiled=True,
    )
    attention_out = jnp.sum(terms.astype(F32), axis=0).astype(BF16)

    new_pool = new_pool.reshape(kv_pool.shape)
    return (attention_out, new_pool)


def solution(mesh):
    placed = (
        P("group", "ctx"),
        P("ctx"),
        P("ctx", "tp"),
        P("ctx", "tp"),
        P("ctx", "tp"),
        P("tp", "ctx"),
        P(("group", "ctx"), None, "tp", None, None),
        P(),
        P(),
        P(),
    )
    return jax.shard_map(
        local,
        mesh=mesh,
        in_specs=placed,
        out_specs=(P("group", ("ctx", "tp")), P(("group", "ctx"), None, "tp", None, None)),
        check_vma=False,
    )
```

```python
import jax
import jax.numpy as jnp
from jax import lax
from jax.experimental import pallas as pl
from jax.experimental.pallas import tpu as pltpu
from jax.sharding import PartitionSpec as P

NEG_FILL = -1e30
LOG2E = 1.4426950408889634
F32 = jnp.float32
BF16 = jnp.bfloat16
VMEM_BYTES = 30 * 1024 * 1024
CHUNK = 4
TAIL = 2
ROOM = 60.0
NO_COST = pl.CostEstimate(flops=1, bytes_accessed=1, transcendentals=0)
CTX = 4
NT = (((1,), (1,)), ((), ()))


def params():
    return pltpu.CompilerParams(vmem_limit_bytes=VMEM_BYTES)


def vmem():
    return pl.BlockSpec(memory_space=pltpu.VMEM)


def smem():
    return pl.BlockSpec(memory_space=pltpu.SMEM)


def anywhere():
    return pl.BlockSpec(memory_space=pl.ANY)


def project_kernel(tok_ref, gain_ref, wq_ref, wk_ref, wv_ref, out_ref):
    wide = tok_ref[...].astype(F32)
    normalized = (wide * gain_ref[...]).astype(BF16)
    q_cols = wq_ref.shape[1]
    rows = tok_ref.shape[0]
    start = pl.program_id(0) == 0

    def add(cols, value):
        @pl.when(start)
        def _():
            out_ref[:, cols] = value

        @pl.when(jnp.logical_not(start))
        def _():
            out_ref[:, cols] += value

    for j in range(0, q_cols, 512):
        add(
            slice(j, j + 512),
            jnp.dot(normalized, wq_ref[:, j : j + 512], preferred_element_type=F32),
        )
    both = jnp.concatenate([wk_ref[...], wv_ref[...]], axis=1)
    add(slice(q_cols, q_cols + 256), jnp.dot(normalized, both, preferred_element_type=F32))
    squares = jnp.sum(wide * wide, axis=1, keepdims=True)
    add(slice(q_cols + 256, q_cols + 384), jnp.broadcast_to(squares, (rows, 128)))


def project(tokens, gain, w_query, w_key, w_value):
    rows, features = tokens.shape
    cols = w_query.shape[1] + 384
    deep = features // 4
    return pl.pallas_call(
        project_kernel,
        grid=(4,),
        out_shape=jax.ShapeDtypeStruct((rows, cols), F32),
        in_specs=[
            pl.BlockSpec((rows, deep), lambda i: (0, i)),
            pl.BlockSpec((1, deep), lambda i: (0, i)),
            pl.BlockSpec((deep, w_query.shape[1]), lambda i: (i, 0)),
            pl.BlockSpec((deep, 128), lambda i: (i, 0)),
            pl.BlockSpec((deep, 128), lambda i: (i, 0)),
        ],
        out_specs=pl.BlockSpec((rows, cols), lambda i: (0, 0)),
        compiler_params=params(),
        cost_estimate=NO_COST,
        name="project",
    )(tokens, gain, w_query, w_key, w_value)


def finish_kernel(features, part_ref, out_ref):
    q_cols = out_ref.shape[1]
    total = part_ref[0]
    for c in range(1, part_ref.shape[0]):
        total = total + part_ref[c]
    scale = lax.rsqrt(total[:, q_cols : q_cols + 1] / features + 1e-05)
    out_ref[...] = (total[:, :q_cols] * scale).astype(BF16)


def finish(parts, features):
    count, rows, cols = parts.shape
    return pl.pallas_call(
        lambda *refs: finish_kernel(features, *refs),
        out_shape=jax.ShapeDtypeStruct((rows, cols - 128), BF16),
        in_specs=[vmem()],
        out_specs=vmem(),
        compiler_params=params(),
        cost_estimate=NO_COST,
        name="finish",
    )(parts)


def pack_kernel(index_ref, pool_ref, out_ref):
    for n in range(out_ref.shape[0]):
        out_ref[n] = pool_ref[index_ref[n]]


def pack(index, pool):
    count = index.shape[0]
    return pl.pallas_call(
        pack_kernel,
        out_shape=jax.ShapeDtypeStruct((count,) + pool.shape[1:], BF16),
        in_specs=[smem(), vmem()],
        out_specs=vmem(),
        compiler_params=pltpu.CompilerParams(vmem_limit_bytes=20 * 1024 * 1024),
        cost_estimate=NO_COST,
        name="pack",
    )(index, pool)


def pack_lanes(ref, rows):
    lane = lax.broadcasted_iota(jnp.int32, (ref.shape[1], 128), 1)[: ref[0, rows, :].shape[0]]
    packed = jnp.zeros(lane.shape, F32)
    for head in range(ref.shape[0]):
        packed = jnp.where(lane == head, ref[head, rows, :], packed)
    return packed


def sweep(q_ref, rows, heads, keys, finish_head):
    pending = None
    for head in range(heads):
        cols = slice(head * 128, head * 128 + 128)
        scores = lax.dot_general(q_ref[rows, cols], keys, NT, preferred_element_type=F32)
        if pending is not None:
            finish_head(*pending)
        pending = (head, cols, scores)
    finish_head(*pending)


def moving(q_ref, m_ref, l_ref, acc_ref, rows, keys, values_ext, mask, const, zero):
    def finish_head(head, cols, scores):
        scores = jnp.where(mask, scores, NEG_FILL)
        m_old = m_ref[head, rows, :]
        m_new = jnp.maximum(m_old, jnp.max(scores, axis=1, keepdims=True) * const)
        alpha = jnp.exp2(m_old - m_new)
        reps = scores.shape[1] // 128
        weights = jnp.exp2(scores * const - jnp.concatenate([m_new] * reps, axis=1))
        if zero:
            weights = jnp.where(mask, weights, 0.0)
        mixed = jnp.dot(weights.astype(BF16), values_ext, preferred_element_type=F32)
        m_ref[head, rows, :] = m_new
        l_ref[head, rows, :] = l_ref[head, rows, :] * alpha + mixed[:, 128:]
        acc_ref[rows, cols] = acc_ref[rows, cols] * alpha + mixed[:, :128]

    sweep(q_ref, rows, m_ref.shape[0], keys, finish_head)


def steady(q_ref, m_ref, l_ref, acc_ref, rows, keys, values_ext, mask, const):
    def finish_head(head, cols, scores):
        if mask is not None:
            scores = jnp.where(mask, scores, NEG_FILL)
        reps = scores.shape[1] // 128
        shift = jnp.concatenate([m_ref[head, rows, :]] * reps, axis=1)
        weights = jnp.exp2(scores * const - shift)
        mixed = jnp.dot(weights.astype(BF16), values_ext, preferred_element_type=F32)
        l_ref[head, rows, :] += mixed[:, 128:]
        acc_ref[rows, cols] += mixed[:, :128]

    sweep(q_ref, rows, m_ref.shape[0], keys, finish_head)


def prefix_part(meta_ref, base, q_ref, qn_ref, kv_ref, vx_ref, m_ref, l_ref, acc_ref, new_len, const):
    blocks = kv_ref.shape[0]
    state = (q_ref, m_ref, l_ref, acc_ref)
    all_keys = kv_ref[:, 0].reshape(blocks * 128, 128)
    vx_ref[:, :128] = kv_ref[:, 1].reshape(blocks * 128, 128)
    vx_ref[:, 128:] = jnp.ones((blocks * 128, 128), BF16)
    norms = jnp.dot(all_keys * all_keys, jnp.ones((128, 128), BF16), preferred_element_type=F32)
    reach = jnp.sqrt(jnp.max(norms)) * (1.05 * const)

    def session_body(session, carry):
        row0 = pl.multiple_of(session * new_len, new_len)
        rows = pl.ds(row0, new_len)
        first = meta_ref[base + 2 * session]
        keys_live = meta_ref[base + 2 * session + 1]
        high = first * 128 + keys_live
        total = (keys_live + 127) // 128

        def enough():
            room = qn_ref[rows, :] * reach - pack_lanes(m_ref, rows)
            return (jnp.max(room) <= ROOM).astype(jnp.int32)

        def piece(wanted, count, masked):
            span = count * 128
            begin = jnp.minimum(wanted, blocks - count)
            keys = kv_ref[pl.ds(begin, count), 0].reshape(span, 128)
            values_ext = vx_ref[pl.ds(pl.multiple_of(begin * 128, 128), span), :]
            if not masked:
                return keys, values_ext, None
            index = begin * 128 + lax.broadcasted_iota(jnp.int32, (1, span), 1)
            return keys, values_ext, (index >= wanted * 128) & (index < high)

        def slow_more(now):
            return (now[0] < total) & (now[1] == 0)

        def slow(now):
            moving(*state, rows, *piece(first + now[0], CHUNK, True), const, False)
            return now[0] + CHUNK, enough()

        done, _ = lax.while_loop(slow_more, slow, (0, enough()))
        full = jnp.maximum(keys_live - done * 128, 0) // (CHUNK * 128)

        def fast(step, carry):
            steady(*state, rows, *piece(first + done + step * CHUNK, CHUNK, False), const)
            return carry

        lax.fori_loop(0, full, fast, 0)
        done = done + full * CHUNK

        def tail(step, carry):
            steady(*state, rows, *piece(first + done + step * TAIL, TAIL, True), const)
            return carry

        lax.fori_loop(0, (jnp.maximum(total - done, 0) + TAIL - 1) // TAIL, tail, 0)
        return carry

    lax.fori_loop(0, q_ref.shape[0] // new_len, session_body, 0)


def first_kernel(
    new_len, const, meta_ref, a, b, c, d, buf,
    q_ref, qn_ref, acc_ref, mp_ref, lp_ref, new_ref, kv_ref, vx_ref, m_ref, l_ref, sem,
):
    fetch = pltpu.make_async_copy(buf, kv_ref, sem)
    fetch.start()
    tokens, q_cols = q_ref.shape
    part = a.shape[0]
    heads = m_ref.shape[0]
    rank = meta_ref[0]
    for step, ref in enumerate((a, b, c, d)):
        place = lax.rem(rank + CTX - step, CTX)
        q_ref[pl.ds(pl.multiple_of(place * part, part), part), :] = ref[:, :q_cols]
        new_ref[place, 0] = ref[:, q_cols : q_cols + 128]
        new_ref[place, 1] = ref[:, q_cols + 128 :]
    m_ref[...] = jnp.full(m_ref.shape, NEG_FILL, F32)
    l_ref[...] = jnp.zeros(l_ref.shape, F32)
    acc_ref[...] = jnp.zeros(acc_ref.shape, F32)
    lane = lax.broadcasted_iota(jnp.int32, (tokens, 128), 1)
    squares = jnp.zeros((tokens, 128), F32)
    for head in range(heads):
        wide = q_ref[:, head * 128 : head * 128 + 128].astype(F32)
        squares = jnp.where(lane == head, jnp.sum(wide * wide, axis=1, keepdims=True), squares)
    qn_ref[...] = jnp.sqrt(squares)
    keys = a[:, q_cols : q_cols + 128]
    values_ext = jnp.concatenate(
        [a[:, q_cols + 128 : q_cols + 256], jnp.ones((part, 128), BF16)], axis=1
    )
    per_session = new_len // part
    rows = pl.ds(pl.multiple_of(lax.div(rank, per_session) * new_len, new_len), new_len)
    offset = lax.rem(rank, per_session) * part
    token = lax.broadcasted_iota(jnp.int32, (new_len, part), 0)
    fresh = lax.broadcasted_iota(jnp.int32, (new_len, part), 1) + offset
    moving(q_ref, m_ref, l_ref, acc_ref, rows, keys, values_ext, fresh <= token, const, True)
    fetch.wait()
    prefix_part(
        meta_ref, 1, q_ref, qn_ref, kv_ref, vx_ref, m_ref, l_ref, acc_ref, new_len, const
    )
    mp_ref[...] = pack_lanes(m_ref, slice(None))
    lp_ref[...] = pack_lanes(l_ref, slice(None))


def load_state(mp_in, lp_in, m_ref, l_ref):
    shape = m_ref.shape[1:]
    for head in range(m_ref.shape[0]):
        m_ref[head] = jnp.broadcast_to(mp_in[:, head : head + 1], shape)
        l_ref[head] = jnp.broadcast_to(lp_in[:, head : head + 1], shape)


def sources(
    new_len, const, meta_ref, q_ref, qn_ref, bufs, acc_in, mp_in, lp_in,
    acc_ref, kv_ref, vx_ref, m_ref, l_ref, sems,
):
    copies = []
    for n, buf in enumerate(bufs):
        copies.append(pltpu.make_async_copy(buf, kv_ref.at[n], sems.at[n]))
        copies[-1].start()
    acc_ref[...] = acc_in[...]
    load_state(mp_in, lp_in, m_ref, l_ref)
    for n, copy in enumerate(copies):
        copy.wait()
        prefix_part(
            meta_ref, 4 * n, q_ref, qn_ref, kv_ref.at[n], vx_ref, m_ref, l_ref, acc_ref, new_len,
            const,
        )


def near_kernel(
    new_len, const, meta_ref, q_ref, qn_ref, acc_in, mp_in, lp_in, buf_a, buf_b, pool_ref,
    acc_ref, mp_ref, lp_ref, pool_out, kv_ref, vx_ref, m_ref, l_ref, sems, pool_sem,
):
    keep = pltpu.make_async_copy(pool_ref, pool_out, pool_sem)
    keep.start()
    sources(
        new_len, const, meta_ref, q_ref, qn_ref, (buf_a, buf_b), acc_in, mp_in, lp_in,
        acc_ref, kv_ref, vx_ref, m_ref, l_ref, sems,
    )
    mp_ref[...] = pack_lanes(m_ref, slice(None))
    lp_ref[...] = pack_lanes(l_ref, slice(None))
    keep.wait()


def last_kernel(
    new_len, const, meta_ref, q_ref, qn_ref, acc_in, mp_in, lp_in, buf, out_ref,
    acc_ref, kv_ref, vx_ref, m_ref, l_ref, sems,
):
    sources(
        new_len, const, meta_ref, q_ref, qn_ref, (buf,), acc_in, mp_in, lp_in,
        acc_ref, kv_ref, vx_ref, m_ref, l_ref, sems,
    )
    tokens = q_ref.shape[0]
    heads = m_ref.shape[0]
    part = tokens // CTX
    for head in range(heads):
        cols = slice(head * 128, head * 128 + 128)
        total = l_ref[head]
        empty = total == 0.0
        safe = jnp.where(empty, 1.0, total)
        done = (acc_ref[:, cols] / safe).astype(BF16)
        for c in range(CTX):
            out_ref[c, :part, cols] = done[c * part : (c + 1) * part]
        m_ref[head] = jnp.where(empty, NEG_FILL, m_ref[head] + jnp.log2(safe))
    packed = pack_lanes(m_ref, slice(None))
    row = lax.broadcasted_iota(jnp.int32, (16, heads * 128), 0)
    for c in range(CTX):
        turned = packed[c * part : (c + 1) * part].T
        line = jnp.concatenate([turned[h : h + 1] for h in range(heads)], axis=1)
        high = line.astype(BF16).astype(F32)
        rest = line - high
        mid = rest.astype(BF16).astype(F32)
        low = rest - mid
        tile = jnp.where(row == 0, high, jnp.where(row == 1, mid, jnp.where(row == 2, low, 0.0)))
        out_ref[c, part : part + 16, :] = tile.astype(BF16)


def scratch(tokens, heads, blocks, lead=()):
    return [
        pltpu.VMEM(lead + (blocks, 2, 128, 128), BF16),
        pltpu.VMEM((blocks * 128, 256), BF16),
        pltpu.VMEM((heads, tokens, 128), F32),
        pltpu.VMEM((heads, tokens, 128), F32),
    ]


def state_shapes(tokens, q_cols):
    return [
        jax.ShapeDtypeStruct((tokens, q_cols), F32),
        jax.ShapeDtypeStruct((tokens, 128), F32),
        jax.ShapeDtypeStruct((tokens, 128), F32),
    ]


def attend_own(meta, quarters, buf, new_len, const):
    part = quarters[0].shape[0]
    q_cols = quarters[0].shape[1] - 256
    tokens = part * CTX
    heads = q_cols // 128
    blocks = buf.shape[0]
    return pl.pallas_call(
        lambda *refs: first_kernel(new_len, const, *refs),
        out_shape=[
            jax.ShapeDtypeStruct((tokens, q_cols), BF16),
            jax.ShapeDtypeStruct((tokens, 128), F32),
        ]
        + state_shapes(tokens, q_cols)
        + [jax.ShapeDtypeStruct((CTX, 2, part, 128), BF16)],
        in_specs=[smem()] + [vmem()] * 4 + [anywhere()],
        out_specs=[vmem()] * 6,
        scratch_shapes=scratch(tokens, heads, blocks) + [pltpu.SemaphoreType.DMA(())],
        compiler_params=params(),
        cost_estimate=NO_COST,
        name="attend_own",
    )(meta, *quarters, buf)


def attend_near(meta, queries, norms, state, bufs, pool, new_len, const):
    tokens, q_cols = queries.shape
    heads = q_cols // 128
    blocks = bufs[0].shape[0]
    return pl.pallas_call(
        lambda *refs: near_kernel(new_len, const, *refs),
        out_shape=state_shapes(tokens, q_cols) + [jax.ShapeDtypeStruct(pool.shape, BF16)],
        in_specs=[smem()] + [vmem()] * 5 + [anywhere()] * 3,
        out_specs=[vmem()] * 3 + [anywhere()],
        scratch_shapes=scratch(tokens, heads, blocks, (2,))
        + [pltpu.SemaphoreType.DMA((2,)), pltpu.SemaphoreType.DMA(())],
        compiler_params=params(),
        cost_estimate=NO_COST,
        name="attend_near",
    )(meta, queries, norms, *state, *bufs, pool)


def attend_last(meta, queries, norms, state, buf, new_len, const):
    tokens, q_cols = queries.shape
    heads = q_cols // 128
    blocks = buf.shape[0]
    return pl.pallas_call(
        lambda *refs: last_kernel(new_len, const, *refs),
        out_shape=jax.ShapeDtypeStruct((CTX, tokens // CTX + 16, q_cols), BF16),
        in_specs=[smem()] + [vmem()] * 5 + [anywhere()],
        out_specs=vmem(),
        scratch_shapes=[pltpu.VMEM((tokens, q_cols), F32)]
        + scratch(tokens, heads, blocks, (1,))
        + [pltpu.SemaphoreType.DMA((1,))],
        compiler_params=params(),
        cost_estimate=NO_COST,
        name="attend_last",
    )(meta, queries, norms, *state, buf)


def combine_kernel(in_ref, out_ref):
    part, q_cols = out_ref.shape
    heads = q_cols // 128
    lines = []
    for c in range(CTX):
        tile = in_ref[c, part : part + 16, :].astype(F32)
        lines.append(tile[0:1] + tile[1:2] + tile[2:3])
    top = lines[0]
    for line in lines[1:]:
        top = jnp.maximum(top, line)
    shares = [jnp.exp2(line - top) for line in lines]
    total = shares[0] + shares[1] + shares[2] + shares[3]
    pieces = []
    for share in shares:
        share = share / total
        pieces += [share[:, h * 128 : h * 128 + 128] for h in range(heads)]
    pieces.append(jnp.zeros((128 - CTX * heads, 128), F32))
    turned = jnp.concatenate(pieces, axis=0).T
    for head in range(heads):
        cols = slice(head * 128, head * 128 + 128)
        mixed = jnp.zeros((part, 128), F32)
        for c in range(CTX):
            at = c * heads + head
            mixed = mixed + in_ref[c, :part, cols].astype(F32) * turned[:, at : at + 1]
        out_ref[:, cols] = mixed.astype(BF16)


def combine(arrived):
    count, rows, q_cols = arrived.shape
    return pl.pallas_call(
        combine_kernel,
        out_shape=jax.ShapeDtypeStruct((rows - 16, q_cols), BF16),
        in_specs=[vmem()],
        out_specs=vmem(),
        compiler_params=params(),
        cost_estimate=NO_COST,
        name="combine",
    )(arrived)


def out_kernel(
    meta_ref, place_ref, a, b, c, d, w_ref, new_a, new_b, new_c, new_d, pool_in,
    own_ref, send_ref, pool_out, rows_ref, sems,
):
    rank = meta_ref[0]
    core = meta_ref[1]
    part = a.shape[0]
    half = own_ref.shape[2]

    def place_blocks(act):
        count = new_a.shape[0]
        for n, ref in enumerate((new_a, new_b, new_c, new_d)):
            for i in range(count):
                at = n * count + i
                slot = place_ref[at]

                @pl.when(slot >= 0)
                def _(ref=ref, i=i, at=at, slot=slot):
                    act(pltpu.make_async_copy(ref.at[i], pool_out.at[slot], sems.at[at]))

    @pl.when(pl.program_id(0) == 0)
    def _():
        place_blocks(lambda copy: copy.start())
        for step, ref in enumerate((a, b, c, d)):
            place = lax.rem(rank + CTX - step, CTX)
            rows_ref[pl.ds(pl.multiple_of(place * part, part), part), :] = ref[...]

    product = jnp.dot(rows_ref[...], w_ref[...], preferred_element_type=F32)

    @pl.when(core == 0)
    def _():
        own_ref[0] = product[:, :half]
        send_ref[0] = product[:, half:].astype(BF16)

    @pl.when(core != 0)
    def _():
        own_ref[0] = product[:, half:]
        send_ref[0] = product[:, :half].astype(BF16)

    @pl.when(pl.program_id(0) == pl.num_programs(0) - 1)
    def _():
        place_blocks(lambda copy: copy.wait())


def project_out(meta, places, quarters, w_out, news, pool, planes):
    part, depth = quarters[0].shape
    tokens = part * CTX
    width = w_out.shape[1] // planes
    whole = pl.BlockSpec((part, depth), lambda i: (0, 0))
    return pl.pallas_call(
        out_kernel,
        grid=(planes,),
        out_shape=[
            jax.ShapeDtypeStruct((planes, tokens, width // 2), F32),
            jax.ShapeDtypeStruct((planes, tokens, width // 2), BF16),
            jax.ShapeDtypeStruct(pool.shape, BF16),
        ],
        in_specs=[smem(), smem()]
        + [whole] * 4
        + [pl.BlockSpec((depth, width), lambda i: (0, i))]
        + [anywhere()] * 5,
        out_specs=[pl.BlockSpec((1, tokens, width // 2), lambda i: (i, 0, 0))] * 2 + [anywhere()],
        scratch_shapes=[
            pltpu.VMEM((tokens, depth), BF16),
            pltpu.SemaphoreType.DMA((places.shape[0],)),
        ],
        input_output_aliases={11: 2},
        compiler_params=params(),
        cost_estimate=NO_COST,
        name="project_out",
    )(meta, places, *quarters, w_out, *news, pool)


def shifted(value, axis, step):
    size = lax.axis_size(axis)
    return lax.ppermute(value, axis, [(i, (i + step) % size) for i in range(size)])


def around(value, axis):
    return [value] + [shifted(value, axis, step) for step in (1, 2, 3)]


def local(
    tokens, norm_gain, w_query, w_key, w_value, w_out, kv_pool, block_table, prefix_len, write_slot
):
    groups = lax.axis_size("group")
    ranks = lax.axis_size("ctx")
    tp_size = lax.axis_size("tp")
    rank = lax.axis_index("ctx")
    group = lax.axis_index("group")
    core = lax.axis_index("tp") % 2
    pool_size = kv_pool.shape[0]
    sessions, list_len = block_table.shape
    sess_here = sessions // groups
    per_pair = sess_here * list_len // (groups * ranks)
    new_len = tokens.shape[0] // sess_here
    head_dim = kv_pool.shape[4]
    const = head_dim**-0.5 * LOG2E
    device_id = group * ranks + rank
    pool = kv_pool.reshape(pool_size, 2, head_dim, head_dim)

    table = block_table.reshape(groups, sess_here * list_len)
    steps = jnp.arange(groups, dtype=jnp.int32)
    send_table = jnp.roll(table, -group, axis=0)
    here = send_table // pool_size == device_id
    upper = jnp.triu(jnp.ones((sess_here * list_len,) * 2, BF16))
    order = jnp.dot(here.astype(BF16), upper, preferred_element_type=F32).astype(jnp.int32)
    wanted = jnp.arange(1, per_pair + 1, dtype=jnp.int32)
    picked = here[:, None, :] & (order[:, None, :] == wanted[None, :, None])
    send_index = jnp.sum(jnp.where(picked, send_table[:, None, :] % pool_size, 0), axis=2)
    blocks = {step: pack(send_index[step], pool) for step in (1, 3, 2, 0)}
    arrived = {step: shifted(blocks[step], "group", step) for step in (1, 3, 2)}

    mine = lax.dynamic_index_in_dim(table, group, 0, keepdims=False).reshape(sess_here, list_len)
    lengths = lax.dynamic_slice_in_dim(prefix_len, group * sess_here, sess_here)
    source = ((group - steps) % groups) * ranks + rank
    from_there = mine[None] // pool_size == source[:, None, None]
    slots = jnp.arange(list_len, dtype=jnp.int32)
    keys_in = jnp.clip(lengths[:, None] - slots[None, :] * head_dim, 0, head_dim)
    live_keys = jnp.sum(jnp.where(from_there, keys_in[None], 0), axis=2)
    counts = jnp.sum(from_there.astype(jnp.int32), axis=2)
    starts = jnp.cumsum(counts, axis=1) - counts
    meta = jnp.stack([starts, live_keys], axis=2).reshape(groups, 2 * sess_here).astype(jnp.int32)

    tokens, _ = lax.optimization_barrier((tokens, [blocks[step] for step in (1, 2, 3)]))
    parts = project(tokens, norm_gain[None, :], w_query, w_key, w_value)
    part_rows = tokens.shape[0] // ranks
    parts = parts.reshape(ranks, part_rows, parts.shape[1])
    parts = lax.all_to_all(parts, "ctx", split_axis=0, concat_axis=0, tiled=True)
    fresh = finish(parts, tokens.shape[1] * ranks)
    quarters = around(fresh, "ctx")

    first_meta = jnp.concatenate([rank[None].astype(jnp.int32), meta[0]])
    queries, norms, *state, block = attend_own(first_meta, quarters, blocks[0], new_len, const)
    near_meta = jnp.concatenate([meta[1], meta[3]])
    *state, new_pool = attend_near(
        near_meta, queries, norms, state, [arrived[1], arrived[3]], pool, new_len, const
    )
    partial = attend_last(meta[2], queries, norms, state, arrived[2], new_len, const)
    partial = lax.all_to_all(partial, "ctx", split_axis=0, concat_axis=0, tiled=True)
    attended = combine(partial)

    planes = tp_size // 2
    out_meta = jnp.stack([rank, core]).astype(jnp.int32)
    news = around(block, "group")
    targets = jnp.roll(write_slot.reshape(groups, ranks)[::-1], group + 1, axis=0).reshape(-1)
    places = jnp.where(targets // pool_size == device_id, targets % pool_size, -1)
    own, send, new_pool = project_out(
        out_meta, places, around(attended, "ctx"), w_out, news, new_pool, planes
    )
    other = lax.ppermute(send, "tp", [(i, i ^ 1) for i in range(tp_size)])
    pair = (own + other.astype(F32)).astype(BF16)
    terms = lax.all_to_all(
        pair,
        "tp",
        split_axis=0,
        concat_axis=0,
        axis_index_groups=[[2 * z + c for z in range(planes)] for c in range(2)],
        tiled=True,
    )
    attention_out = jnp.sum(terms.astype(F32), axis=0).astype(BF16)

    new_pool = new_pool.reshape(kv_pool.shape)
    return (attention_out, new_pool)


def solution(mesh):
    placed = (
        P("group", "ctx"),
        P("ctx"),
        P("ctx", "tp"),
        P("ctx", "tp"),
        P("ctx", "tp"),
        P("tp", "ctx"),
        P(("group", "ctx"), None, "tp", None, None),
        P(),
        P(),
        P(),
    )
    return jax.shard_map(
        local,
        mesh=mesh,
        in_specs=placed,
        out_specs=(P("group", ("ctx", "tp")), P(("group", "ctx"), None, "tp", None, None)),
        check_vma=False,
    )
```

```python
import jax
import jax.numpy as jnp
from jax import lax
from jax.experimental import pallas as pl
from jax.experimental.pallas import tpu as pltpu
from jax.sharding import PartitionSpec as P

NEG_FILL = -1e30
LOG2E = 1.4426950408889634
F32 = jnp.float32
BF16 = jnp.bfloat16
VMEM_BYTES = 30 * 1024 * 1024
VMEM_MOST = 58 * 1024 * 1024
CHUNK = 4
TAIL = 2
ROOM = 60.0
NO_COST = pl.CostEstimate(flops=1, bytes_accessed=1, transcendentals=0)
CTX = 4
NT = (((1,), (1,)), ((), ()))


def params(size=VMEM_BYTES):
    return pltpu.CompilerParams(vmem_limit_bytes=size)


def vmem():
    return pl.BlockSpec(memory_space=pltpu.VMEM)


def smem():
    return pl.BlockSpec(memory_space=pltpu.SMEM)


def anywhere():
    return pl.BlockSpec(memory_space=pl.ANY)


def project_kernel(
    tok_ref, gain_ref, wq_ref, wk_ref, wv_ref, out_ref, tok, wq, wkv, norm, total, in_sems, out_sems
):
    rows, features = tok.shape
    q_cols = wq.shape[1]
    step = 256
    count = q_cols // step
    half = rows // 2
    fetch_tok = [
        pltpu.make_async_copy(
            tok_ref.at[pl.ds(n * half, half)], tok.at[pl.ds(n * half, half)], in_sems.at[n]
        )
        for n in range(2)
    ]
    fetch_w = [
        pltpu.make_async_copy(
            wq_ref.at[:, pl.ds(n * step, step)], wq.at[:, pl.ds(n * step, step)], in_sems.at[2 + n]
        )
        for n in range(count)
    ]
    fetch_kv = [
        pltpu.make_async_copy(ref, wkv.at[:, pl.ds(n * 128, 128)], in_sems.at[2 + count + n])
        for n, ref in enumerate((wk_ref, wv_ref))
    ]
    for copy in fetch_tok + fetch_w + fetch_kv:
        copy.start()
    sent = []

    def send(first, width):
        cols = pl.ds(first, width)
        sent.append(
            pltpu.make_async_copy(total.at[:, cols], out_ref.at[:, cols], out_sems.at[len(sent)])
        )
        sent[-1].start()

    for n, copy in enumerate(fetch_tok):
        copy.wait()
        part = slice(n * half, n * half + half)
        wide = tok[part].astype(F32)
        norm[part] = (wide * gain_ref[...]).astype(BF16)
        squares = jnp.sum(wide * wide, axis=1, keepdims=True)
        total[part, q_cols + 256 :] = jnp.broadcast_to(squares, (half, 128))
    send(q_cols + 256, 128)
    for n, copy in enumerate(fetch_w):
        copy.wait()
        cols = slice(n * step, n * step + step)
        total[:, cols] = jnp.dot(norm[...], wq[:, cols], preferred_element_type=F32)
        send(n * step, step)
    for copy in fetch_kv:
        copy.wait()
    total[:, q_cols : q_cols + 256] = jnp.dot(norm[...], wkv[...], preferred_element_type=F32)
    send(q_cols, 256)
    for copy in sent:
        copy.wait()


def project(tokens, gain, w_query, w_key, w_value):
    rows, features = tokens.shape
    q_cols = w_query.shape[1]
    cols = q_cols + 384
    return pl.pallas_call(
        project_kernel,
        out_shape=jax.ShapeDtypeStruct((rows, cols), F32),
        in_specs=[anywhere(), vmem(), anywhere(), anywhere(), anywhere()],
        out_specs=anywhere(),
        scratch_shapes=[
            pltpu.VMEM((rows, features), BF16),
            pltpu.VMEM((features, q_cols), BF16),
            pltpu.VMEM((features, 256), BF16),
            pltpu.VMEM((rows, features), BF16),
            pltpu.VMEM((rows, cols), F32),
            pltpu.SemaphoreType.DMA((4 + q_cols // 256,)),
            pltpu.SemaphoreType.DMA((2 + q_cols // 256,)),
        ],
        compiler_params=params(VMEM_MOST),
        cost_estimate=NO_COST,
        name="project",
    )(tokens, gain, w_query, w_key, w_value)


def finish_kernel(features, part_ref, out_ref, block_ref):
    q_cols = out_ref.shape[1]
    total = part_ref[0]
    for c in range(1, part_ref.shape[0]):
        total = total + part_ref[c]
    scale = lax.rsqrt(total[:, q_cols : q_cols + 1] / features + 1e-05)
    done = (total[:, :q_cols] * scale).astype(BF16)
    out_ref[...] = done
    block_ref[0] = done[:, q_cols - 256 : q_cols - 128]
    block_ref[1] = done[:, q_cols - 128 :]


def finish(parts, features):
    count, rows, cols = parts.shape
    return pl.pallas_call(
        lambda *refs: finish_kernel(features, *refs),
        out_shape=[
            jax.ShapeDtypeStruct((rows, cols - 128), BF16),
            jax.ShapeDtypeStruct((2, rows, 128), BF16),
        ],
        in_specs=[vmem()],
        out_specs=[vmem()] * 2,
        compiler_params=params(),
        cost_estimate=NO_COST,
        name="finish",
    )(parts)


def pack_kernel(index_ref, pool_ref, *refs):
    steps = index_ref.shape[0]
    outs = refs[:steps]
    pool_out, pool, held, sems = refs[steps:]
    fetch = pltpu.make_async_copy(pool_ref, pool, sems.at[steps])
    fetch.start()
    fetch.wait()
    copies = []
    for step in range(steps):
        for n in range(held.shape[1]):
            held[step, n] = pool[index_ref[step, n]]
        copies.append(pltpu.make_async_copy(held.at[step], outs[step], sems.at[step]))
        copies[-1].start()
    copies.append(pltpu.make_async_copy(pool, pool_out, sems.at[steps]))
    copies[-1].start()
    for copy in copies:
        copy.wait()


def pack(index, pool):
    steps, count = index.shape
    block = pool.shape[1:]
    return pl.pallas_call(
        pack_kernel,
        out_shape=[jax.ShapeDtypeStruct((count,) + block, BF16)] * steps
        + [jax.ShapeDtypeStruct(pool.shape, BF16)],
        in_specs=[smem(), anywhere()],
        out_specs=[anywhere()] * (steps + 1),
        scratch_shapes=[
            pltpu.VMEM(pool.shape, BF16),
            pltpu.VMEM((steps, count) + block, BF16),
            pltpu.SemaphoreType.DMA((steps + 1,)),
        ],
        compiler_params=params(VMEM_MOST),
        cost_estimate=NO_COST,
        name="pack",
    )(index, pool)


def pack_lanes(ref, rows):
    lane = lax.broadcasted_iota(jnp.int32, (ref.shape[1], 128), 1)[: ref[0, rows, :].shape[0]]
    packed = jnp.zeros(lane.shape, F32)
    for head in range(ref.shape[0]):
        packed = jnp.where(lane == head, ref[head, rows, :], packed)
    return packed


def sweep(q_ref, rows, heads, keys, finish_head):
    pending = None
    for head in range(heads):
        cols = slice(head * 128, head * 128 + 128)
        scores = lax.dot_general(q_ref[rows, cols], keys, NT, preferred_element_type=F32)
        if pending is not None:
            finish_head(*pending)
        pending = (head, cols, scores)
    finish_head(*pending)


def moving(q_ref, m_ref, l_ref, acc_ref, rows, keys, values_ext, mask, const, zero):
    def finish_head(head, cols, scores):
        scores = jnp.where(mask, scores, NEG_FILL)
        m_old = m_ref[head, rows, :]
        m_new = jnp.maximum(m_old, jnp.max(scores, axis=1, keepdims=True) * const)
        alpha = jnp.exp2(m_old - m_new)
        reps = scores.shape[1] // 128
        weights = jnp.exp2(scores * const - jnp.concatenate([m_new] * reps, axis=1))
        if zero:
            weights = jnp.where(mask, weights, 0.0)
        mixed = jnp.dot(weights.astype(BF16), values_ext, preferred_element_type=F32)
        m_ref[head, rows, :] = m_new
        l_ref[head, rows, :] = l_ref[head, rows, :] * alpha + mixed[:, 128:]
        acc_ref[rows, cols] = acc_ref[rows, cols] * alpha + mixed[:, :128]

    sweep(q_ref, rows, m_ref.shape[0], keys, finish_head)


def steady(q_ref, m_ref, l_ref, acc_ref, rows, keys, values_ext, mask, const):
    def finish_head(head, cols, scores):
        if mask is not None:
            scores = jnp.where(mask, scores, NEG_FILL)
        reps = scores.shape[1] // 128
        shift = jnp.concatenate([m_ref[head, rows, :]] * reps, axis=1)
        weights = jnp.exp2(scores * const - shift)
        mixed = jnp.dot(weights.astype(BF16), values_ext, preferred_element_type=F32)
        l_ref[head, rows, :] += mixed[:, 128:]
        acc_ref[rows, cols] += mixed[:, :128]

    sweep(q_ref, rows, m_ref.shape[0], keys, finish_head)


def prefix_part(meta_ref, base, q_ref, qn_ref, kv_ref, vx_ref, m_ref, l_ref, acc_ref, new_len, const):
    blocks = kv_ref.shape[0]
    state = (q_ref, m_ref, l_ref, acc_ref)
    all_keys = kv_ref[:, 0].reshape(blocks * 128, 128)
    vx_ref[:, :128] = kv_ref[:, 1].reshape(blocks * 128, 128)
    vx_ref[:, 128:] = jnp.ones((blocks * 128, 128), BF16)
    norms = jnp.dot(all_keys * all_keys, jnp.ones((128, 128), BF16), preferred_element_type=F32)
    reach = jnp.sqrt(jnp.max(norms)) * (1.05 * const)

    def session_body(session, carry):
        row0 = pl.multiple_of(session * new_len, new_len)
        rows = pl.ds(row0, new_len)
        first = meta_ref[base + 2 * session]
        keys_live = meta_ref[base + 2 * session + 1]
        high = first * 128 + keys_live
        total = (keys_live + 127) // 128

        def enough():
            room = qn_ref[rows, :] * reach - pack_lanes(m_ref, rows)
            return (jnp.max(room) <= ROOM).astype(jnp.int32)

        def piece(wanted, count, masked):
            span = count * 128
            begin = jnp.minimum(wanted, blocks - count)
            keys = kv_ref[pl.ds(begin, count), 0].reshape(span, 128)
            values_ext = vx_ref[pl.ds(pl.multiple_of(begin * 128, 128), span), :]
            if not masked:
                return keys, values_ext, None
            index = begin * 128 + lax.broadcasted_iota(jnp.int32, (1, span), 1)
            return keys, values_ext, (index >= wanted * 128) & (index < high)

        def slow_more(now):
            return (now[0] < total) & (now[1] == 0)

        def slow(now):
            moving(*state, rows, *piece(first + now[0], CHUNK, True), const, False)
            return now[0] + CHUNK, enough()

        done, _ = lax.while_loop(slow_more, slow, (0, enough()))
        full = jnp.maximum(keys_live - done * 128, 0) // (CHUNK * 128)

        def fast(step, carry):
            steady(*state, rows, *piece(first + done + step * CHUNK, CHUNK, False), const)
            return carry

        lax.fori_loop(0, full, fast, 0)
        done = done + full * CHUNK

        def tail(step, carry):
            steady(*state, rows, *piece(first + done + step * TAIL, TAIL, True), const)
            return carry

        lax.fori_loop(0, (jnp.maximum(total - done, 0) + TAIL - 1) // TAIL, tail, 0)
        return carry

    lax.fori_loop(0, q_ref.shape[0] // new_len, session_body, 0)


def first_kernel(
    new_len, const, meta_ref, a, b, c, d, buf,
    q_ref, qn_ref, acc_ref, mp_ref, lp_ref, kv_ref, vx_ref, m_ref, l_ref, sem,
):
    fetch = pltpu.make_async_copy(buf, kv_ref, sem)
    fetch.start()
    tokens, q_cols = q_ref.shape
    part = a.shape[0]
    heads = m_ref.shape[0]
    rank = meta_ref[0]
    for step, ref in enumerate((a, b, c, d)):
        place = lax.rem(rank + CTX - step, CTX)
        q_ref[pl.ds(pl.multiple_of(place * part, part), part), :] = ref[:, :q_cols]
    m_ref[...] = jnp.full(m_ref.shape, NEG_FILL, F32)
    l_ref[...] = jnp.zeros(l_ref.shape, F32)
    acc_ref[...] = jnp.zeros(acc_ref.shape, F32)
    lane = lax.broadcasted_iota(jnp.int32, (tokens, 128), 1)
    squares = jnp.zeros((tokens, 128), F32)
    for head in range(heads):
        wide = q_ref[:, head * 128 : head * 128 + 128].astype(F32)
        squares = jnp.where(lane == head, jnp.sum(wide * wide, axis=1, keepdims=True), squares)
    qn_ref[...] = jnp.sqrt(squares)
    keys = a[:, q_cols : q_cols + 128]
    values_ext = jnp.concatenate(
        [a[:, q_cols + 128 : q_cols + 256], jnp.ones((part, 128), BF16)], axis=1
    )
    per_session = new_len // part
    rows = pl.ds(pl.multiple_of(lax.div(rank, per_session) * new_len, new_len), new_len)
    offset = lax.rem(rank, per_session) * part
    token = lax.broadcasted_iota(jnp.int32, (new_len, part), 0)
    fresh = lax.broadcasted_iota(jnp.int32, (new_len, part), 1) + offset
    moving(q_ref, m_ref, l_ref, acc_ref, rows, keys, values_ext, fresh <= token, const, True)
    fetch.wait()
    prefix_part(
        meta_ref, 1, q_ref, qn_ref, kv_ref, vx_ref, m_ref, l_ref, acc_ref, new_len, const
    )
    mp_ref[...] = pack_lanes(m_ref, slice(None))
    lp_ref[...] = pack_lanes(l_ref, slice(None))


def load_state(mp_in, lp_in, m_ref, l_ref):
    shape = m_ref.shape[1:]
    for head in range(m_ref.shape[0]):
        m_ref[head] = jnp.broadcast_to(mp_in[:, head : head + 1], shape)
        l_ref[head] = jnp.broadcast_to(lp_in[:, head : head + 1], shape)


def sources(
    new_len, const, meta_ref, q_ref, qn_ref, bufs, acc_in, mp_in, lp_in,
    acc_ref, kv_ref, vx_ref, m_ref, l_ref, sems,
):
    copies = []
    for n, buf in enumerate(bufs):
        copies.append(pltpu.make_async_copy(buf, kv_ref.at[n], sems.at[n]))
        copies[-1].start()
    acc_ref[...] = acc_in[...]
    load_state(mp_in, lp_in, m_ref, l_ref)
    for n, copy in enumerate(copies):
        copy.wait()
        prefix_part(
            meta_ref, 4 * n, q_ref, qn_ref, kv_ref.at[n], vx_ref, m_ref, l_ref, acc_ref, new_len,
            const,
        )


def near_kernel(
    new_len, const, meta_ref, q_ref, qn_ref, acc_in, mp_in, lp_in, buf_a, buf_b,
    acc_ref, mp_ref, lp_ref, kv_ref, vx_ref, m_ref, l_ref, sems,
):
    sources(
        new_len, const, meta_ref, q_ref, qn_ref, (buf_a, buf_b), acc_in, mp_in, lp_in,
        acc_ref, kv_ref, vx_ref, m_ref, l_ref, sems,
    )
    mp_ref[...] = pack_lanes(m_ref, slice(None))
    lp_ref[...] = pack_lanes(l_ref, slice(None))


def last_kernel(
    new_len, const, meta_ref, place_ref, q_ref, qn_ref, acc_in, mp_in, lp_in, buf, new_ref, pool_in,
    out_a, out_b, out_c, out_d, pool_out, acc_ref, kv_ref, vx_ref, m_ref, l_ref, sems, new_sems,
):
    def place_blocks(act):
        for n in range(new_ref.shape[0]):
            slot = place_ref[n]

            @pl.when(slot >= 0)
            def _(n=n, slot=slot):
                act(pltpu.make_async_copy(new_ref.at[n], pool_out.at[slot], new_sems.at[n]))

    place_blocks(lambda copy: copy.start())
    sources(
        new_len, const, meta_ref, q_ref, qn_ref, (buf,), acc_in, mp_in, lp_in,
        acc_ref, kv_ref, vx_ref, m_ref, l_ref, sems,
    )
    tokens = q_ref.shape[0]
    heads = m_ref.shape[0]
    part = tokens // CTX
    rank = meta_ref[4]
    row = lax.broadcasted_iota(jnp.int32, (16, heads * 128), 0)
    for step, out_ref in enumerate((out_a, out_b, out_c, out_d)):
        place = lax.rem(rank + step, CTX)
        rows = pl.ds(pl.multiple_of(place * part, part), part)
        for head in range(heads):
            cols = slice(head * 128, head * 128 + 128)
            total = l_ref[head, rows, :]
            empty = total == 0.0
            safe = jnp.where(empty, 1.0, total)
            out_ref[:part, cols] = (acc_ref[rows, cols] / safe).astype(BF16)
            m_ref[head, rows, :] = jnp.where(
                empty, NEG_FILL, m_ref[head, rows, :] + jnp.log2(safe)
            )
        turned = pack_lanes(m_ref, rows).T
        line = jnp.concatenate([turned[h : h + 1] for h in range(heads)], axis=1)
        high = line.astype(BF16).astype(F32)
        rest = line - high
        mid = rest.astype(BF16).astype(F32)
        low = rest - mid
        tile = jnp.where(row == 0, high, jnp.where(row == 1, mid, jnp.where(row == 2, low, 0.0)))
        out_ref[part : part + 16, :] = tile.astype(BF16)
    place_blocks(lambda copy: copy.wait())


def scratch(tokens, heads, blocks, lead=()):
    return [
        pltpu.VMEM(lead + (blocks, 2, 128, 128), BF16),
        pltpu.VMEM((blocks * 128, 256), BF16),
        pltpu.VMEM((heads, tokens, 128), F32),
        pltpu.VMEM((heads, tokens, 128), F32),
    ]


def state_shapes(tokens, q_cols):
    return [
        jax.ShapeDtypeStruct((tokens, q_cols), F32),
        jax.ShapeDtypeStruct((tokens, 128), F32),
        jax.ShapeDtypeStruct((tokens, 128), F32),
    ]


def attend_own(meta, quarters, buf, new_len, const):
    part = quarters[0].shape[0]
    q_cols = quarters[0].shape[1] - 256
    tokens = part * CTX
    heads = q_cols // 128
    blocks = buf.shape[0]
    return pl.pallas_call(
        lambda *refs: first_kernel(new_len, const, *refs),
        out_shape=[
            jax.ShapeDtypeStruct((tokens, q_cols), BF16),
            jax.ShapeDtypeStruct((tokens, 128), F32),
        ]
        + state_shapes(tokens, q_cols),
        in_specs=[smem()] + [vmem()] * 4 + [anywhere()],
        out_specs=[vmem()] * 5,
        scratch_shapes=scratch(tokens, heads, blocks) + [pltpu.SemaphoreType.DMA(())],
        compiler_params=params(),
        cost_estimate=NO_COST,
        name="attend_own",
    )(meta, *quarters, buf)


def attend_near(meta, queries, norms, state, bufs, new_len, const):
    tokens, q_cols = queries.shape
    heads = q_cols // 128
    blocks = bufs[0].shape[0]
    return pl.pallas_call(
        lambda *refs: near_kernel(new_len, const, *refs),
        out_shape=state_shapes(tokens, q_cols),
        in_specs=[smem()] + [vmem()] * 5 + [anywhere()] * 2,
        out_specs=[vmem()] * 3,
        scratch_shapes=scratch(tokens, heads, blocks, (2,))
        + [pltpu.SemaphoreType.DMA((2,))],
        compiler_params=params(),
        cost_estimate=NO_COST,
        name="attend_near",
    )(meta, queries, norms, *state, *bufs)


def attend_last(meta, places, queries, norms, state, buf, news, pool, new_len, const):
    tokens, q_cols = queries.shape
    heads = q_cols // 128
    blocks = buf.shape[0]
    return pl.pallas_call(
        lambda *refs: last_kernel(new_len, const, *refs),
        out_shape=[jax.ShapeDtypeStruct((tokens // CTX + 16, q_cols), BF16)] * CTX
        + [jax.ShapeDtypeStruct(pool.shape, BF16)],
        in_specs=[smem(), smem()] + [vmem()] * 5 + [anywhere()] * 3,
        out_specs=[vmem()] * CTX + [anywhere()],
        scratch_shapes=[pltpu.VMEM((tokens, q_cols), F32)]
        + scratch(tokens, heads, blocks, (1,))
        + [pltpu.SemaphoreType.DMA((1,)), pltpu.SemaphoreType.DMA((places.shape[0],))],
        input_output_aliases={9: CTX},
        compiler_params=params(),
        cost_estimate=NO_COST,
        name="attend_last",
    )(meta, places, queries, norms, *state, buf, news, pool)


def combine_kernel(*refs):
    in_refs, out_ref = refs[:CTX], refs[CTX]
    part, q_cols = out_ref.shape
    heads = q_cols // 128
    lines = []
    for c in range(CTX):
        tile = in_refs[c][part : part + 16, :].astype(F32)
        lines.append(tile[0:1] + tile[1:2] + tile[2:3])
    top = lines[0]
    for line in lines[1:]:
        top = jnp.maximum(top, line)
    shares = [jnp.exp2(line - top) for line in lines]
    total = shares[0] + shares[1] + shares[2] + shares[3]
    pieces = []
    for share in shares:
        share = share / total
        pieces += [share[:, h * 128 : h * 128 + 128] for h in range(heads)]
    pieces.append(jnp.zeros((128 - CTX * heads, 128), F32))
    turned = jnp.concatenate(pieces, axis=0).T
    for head in range(heads):
        cols = slice(head * 128, head * 128 + 128)
        mixed = jnp.zeros((part, 128), F32)
        for c in range(CTX):
            at = c * heads + head
            mixed = mixed + in_refs[c][:part, cols].astype(F32) * turned[:, at : at + 1]
        out_ref[:, cols] = mixed.astype(BF16)


def combine(arrived):
    rows, q_cols = arrived[0].shape
    return pl.pallas_call(
        combine_kernel,
        out_shape=jax.ShapeDtypeStruct((rows - 16, q_cols), BF16),
        in_specs=[vmem()] * CTX,
        out_specs=vmem(),
        compiler_params=params(),
        cost_estimate=NO_COST,
        name="combine",
    )(*arrived)


def out_kernel(meta_ref, a, b, c, d, w_ref, own_ref, send_ref, rows_ref):
    rank = meta_ref[0]
    core = meta_ref[1]
    part = a.shape[0]
    half = own_ref.shape[2]

    @pl.when(pl.program_id(0) == 0)
    def _():
        for step, ref in enumerate((a, b, c, d)):
            place = lax.rem(rank + CTX - step, CTX)
            rows_ref[pl.ds(pl.multiple_of(place * part, part), part), :] = ref[...]

    product = jnp.dot(rows_ref[...], w_ref[...], preferred_element_type=F32)

    @pl.when(core == 0)
    def _():
        own_ref[0] = product[:, :half]
        send_ref[0] = product[:, half:].astype(BF16)

    @pl.when(core != 0)
    def _():
        own_ref[0] = product[:, half:]
        send_ref[0] = product[:, :half].astype(BF16)


def project_out(meta, quarters, w_out, planes):
    part, depth = quarters[0].shape
    tokens = part * CTX
    width = w_out.shape[1] // planes
    whole = pl.BlockSpec((part, depth), lambda i, meta: (0, 0))
    out = pl.BlockSpec((1, tokens, width // 2), lambda i, meta: (i, 0, 0))
    return pl.pallas_call(
        out_kernel,
        grid_spec=pltpu.PrefetchScalarGridSpec(
            num_scalar_prefetch=1,
            grid=(planes,),
            in_specs=[whole] * 4
            + [pl.BlockSpec((depth, width), lambda i, meta: (0, lax.rem(meta[2] + i, planes)))],
            out_specs=[out] * 2,
            scratch_shapes=[pltpu.VMEM((tokens, depth), BF16)],
        ),
        out_shape=[
            jax.ShapeDtypeStruct((planes, tokens, width // 2), F32),
            jax.ShapeDtypeStruct((planes, tokens, width // 2), BF16),
        ],
        compiler_params=params(VMEM_MOST),
        cost_estimate=NO_COST,
        name="project_out",
    )(meta, *quarters, w_out)


def shifted(value, axis, step):
    size = lax.axis_size(axis)
    return lax.ppermute(value, axis, [(i, (i + step) % size) for i in range(size)])


def around(value, axis):
    return [value] + [shifted(value, axis, step) for step in (1, 2, 3)]


def local(
    tokens, norm_gain, w_query, w_key, w_value, w_out, kv_pool, block_table, prefix_len, write_slot
):
    groups = lax.axis_size("group")
    ranks = lax.axis_size("ctx")
    tp_size = lax.axis_size("tp")
    rank = lax.axis_index("ctx")
    group = lax.axis_index("group")
    core = lax.axis_index("tp") % 2
    plane = lax.axis_index("tp") // 2
    pool_size = kv_pool.shape[0]
    sessions, list_len = block_table.shape
    sess_here = sessions // groups
    per_pair = sess_here * list_len // (groups * ranks)
    new_len = tokens.shape[0] // sess_here
    head_dim = kv_pool.shape[4]
    const = head_dim**-0.5 * LOG2E
    device_id = group * ranks + rank
    pool = kv_pool.reshape(pool_size, 2, head_dim, head_dim)

    table = block_table.reshape(groups, sess_here * list_len)
    steps = jnp.arange(groups, dtype=jnp.int32)
    send_table = jnp.roll(table, -group, axis=0)
    here = send_table // pool_size == device_id
    upper = jnp.triu(jnp.ones((sess_here * list_len,) * 2, BF16))
    order = jnp.dot(here.astype(BF16), upper, preferred_element_type=F32).astype(jnp.int32)
    wanted = jnp.arange(1, per_pair + 1, dtype=jnp.int32)
    picked = here[:, None, :] & (order[:, None, :] == wanted[None, :, None])
    send_index = jnp.sum(jnp.where(picked, send_table[:, None, :] % pool_size, 0), axis=2)
    *blocks, new_pool = pack(send_index, pool)
    arrived = {step: shifted(blocks[step], "group", step) for step in (1, 3, 2)}

    mine = lax.dynamic_index_in_dim(table, group, 0, keepdims=False).reshape(sess_here, list_len)
    lengths = lax.dynamic_slice_in_dim(prefix_len, group * sess_here, sess_here)
    source = ((group - steps) % groups) * ranks + rank
    from_there = mine[None] // pool_size == source[:, None, None]
    slots = jnp.arange(list_len, dtype=jnp.int32)
    keys_in = jnp.clip(lengths[:, None] - slots[None, :] * head_dim, 0, head_dim)
    live_keys = jnp.sum(jnp.where(from_there, keys_in[None], 0), axis=2)
    counts = jnp.sum(from_there.astype(jnp.int32), axis=2)
    starts = jnp.cumsum(counts, axis=1) - counts
    meta = jnp.stack([starts, live_keys], axis=2).reshape(groups, 2 * sess_here).astype(jnp.int32)

    parts = project(tokens, norm_gain[None, :], w_query, w_key, w_value)
    part_rows = tokens.shape[0] // ranks
    parts = parts.reshape(ranks, part_rows, parts.shape[1])
    parts = lax.all_to_all(parts, "ctx", split_axis=0, concat_axis=0, tiled=True)
    fresh, block = finish(parts, tokens.shape[1] * ranks)
    news = lax.all_gather(block, ("group", "ctx"))
    targets = write_slot.reshape(-1)
    places = jnp.where(targets // pool_size == device_id, targets % pool_size, -1)
    quarters = around(fresh, "ctx")

    rank_only = rank[None].astype(jnp.int32)
    first_meta = jnp.concatenate([rank_only, meta[0]])
    queries, norms, *state = attend_own(first_meta, quarters, blocks[0], new_len, const)
    near_meta = jnp.concatenate([meta[1], meta[3]])
    state = attend_near(
        near_meta, queries, norms, state, [arrived[1], arrived[3]], new_len, const
    )
    last_meta = jnp.concatenate([meta[2], rank_only])
    *partial, new_pool = attend_last(
        last_meta, places, queries, norms, state, arrived[2], news, new_pool, new_len, const
    )
    partial = [partial[0]] + [shifted(partial[step], "ctx", step) for step in (1, 2, 3)]
    attended = combine(partial)

    planes = tp_size // 2
    out_meta = jnp.stack([rank, core, plane]).astype(jnp.int32)
    own, send = project_out(out_meta, around(attended, "ctx"), w_out, planes)
    other = lax.ppermute(send, "tp", [(i, i ^ 1) for i in range(tp_size)])
    total = own[0] + other[0].astype(F32)
    for step in range(1, planes):
        pair = (own[step] + other[step].astype(F32)).astype(BF16)
        total = total + shifted(pair, "tp", 2 * step).astype(F32)
    return (total.astype(BF16), new_pool.reshape(kv_pool.shape))


def solution(mesh):
    placed = (
        P("group", "ctx"),
        P("ctx"),
        P("ctx", "tp"),
        P("ctx", "tp"),
        P("ctx", "tp"),
        P("tp", "ctx"),
        P(("group", "ctx"), None, "tp", None, None),
        P(),
        P(),
        P(),
    )
    return jax.shard_map(
        local,
        mesh=mesh,
        in_specs=placed,
        out_specs=(P("group", ("ctx", "tp")), P(("group", "ctx"), None, "tp", None, None)),
        check_vma=False,
    )
```

```python
import jax
import jax.numpy as jnp
from jax import lax
from jax.experimental import pallas as pl
from jax.experimental.pallas import tpu as pltpu
from jax.sharding import PartitionSpec as P

NEG_FILL = -1e30
LOG2E = 1.4426950408889634
F32 = jnp.float32
BF16 = jnp.bfloat16
VMEM_BYTES = 30 * 1024 * 1024
VMEM_MOST = 58 * 1024 * 1024
CHUNK = 4
TAIL = 2
ROOM = 60.0
NO_COST = pl.CostEstimate(flops=1, bytes_accessed=1, transcendentals=0)
CTX = 4
NT = (((1,), (1,)), ((), ()))


def params(size=VMEM_BYTES):
    return pltpu.CompilerParams(vmem_limit_bytes=size)


def vmem():
    return pl.BlockSpec(memory_space=pltpu.VMEM)


def smem():
    return pl.BlockSpec(memory_space=pltpu.SMEM)


def anywhere():
    return pl.BlockSpec(memory_space=pl.ANY)


def project_kernel(
    meta_ref, tok_ref, gain_ref, wq_ref, wk_ref, wv_ref, *refs
):
    out_refs = refs[:CTX]
    tok, wq, wkv, norm, total, in_sems, out_sems = refs[CTX:]
    rows, features = tok.shape
    q_cols = wq.shape[1]
    deep = features // 4
    part = rows // CTX
    rank = meta_ref[0]
    fetch_tok = pltpu.make_async_copy(tok_ref, tok, in_sems.at[0])
    fetch_w = [
        pltpu.make_async_copy(
            wq_ref.at[pl.ds(n * deep, deep)], wq.at[pl.ds(n * deep, deep)], in_sems.at[1 + n]
        )
        for n in range(4)
    ]
    fetch_kv = [
        pltpu.make_async_copy(ref, wkv.at[:, pl.ds(n * 128, 128)], in_sems.at[5 + n])
        for n, ref in enumerate((wk_ref, wv_ref))
    ]
    for copy in [fetch_tok] + fetch_kv + fetch_w:
        copy.start()
    fetch_tok.wait()
    for first in range(0, rows, part):
        some = slice(first, first + part)
        wide = tok[some].astype(F32)
        norm[some] = (wide * gain_ref[...]).astype(BF16)
        squares = jnp.sum(wide * wide, axis=1, keepdims=True)
        total[some, q_cols + 256 :] = jnp.broadcast_to(squares, (part, 128))
    for copy in fetch_kv:
        copy.wait()
    total[:, q_cols : q_cols + 256] = jnp.dot(norm[...], wkv[...], preferred_element_type=F32)
    half = 2 * deep
    for n in range(2):
        fetch_w[2 * n].wait()
        fetch_w[2 * n + 1].wait()
        depth = slice(n * half, n * half + half)
        for first in range(0, q_cols, 256):
            cols = slice(first, first + 256)
            value = jnp.dot(norm[:, depth], wq[depth, cols], preferred_element_type=F32)
            if n == 0:
                total[:, cols] = value
            else:
                total[:, cols] += value
    copies = []
    for step in range(CTX):
        place = lax.rem(rank + step, CTX)
        source = total.at[pl.ds(pl.multiple_of(place * part, part), part)]
        copies.append(pltpu.make_async_copy(source, out_refs[step], out_sems.at[step]))
        copies[-1].start()
    for copy in copies:
        copy.wait()


def project(meta, tokens, gain, w_query, w_key, w_value):
    rows, features = tokens.shape
    q_cols = w_query.shape[1]
    cols = q_cols + 384
    return pl.pallas_call(
        project_kernel,
        out_shape=[jax.ShapeDtypeStruct((rows // CTX, cols), F32)] * CTX,
        in_specs=[smem(), anywhere(), vmem(), anywhere(), anywhere(), anywhere()],
        out_specs=[anywhere()] * CTX,
        scratch_shapes=[
            pltpu.VMEM((rows, features), BF16),
            pltpu.VMEM((features, q_cols), BF16),
            pltpu.VMEM((features, 256), BF16),
            pltpu.VMEM((rows, features), BF16),
            pltpu.VMEM((rows, cols), F32),
            pltpu.SemaphoreType.DMA((7,)),
            pltpu.SemaphoreType.DMA((CTX,)),
        ],
        compiler_params=params(VMEM_MOST),
        cost_estimate=NO_COST,
        name="project",
    )(meta, tokens, gain, w_query, w_key, w_value)


def finish_kernel(features, *refs):
    part_refs, out_ref = refs[:CTX], refs[CTX]
    q_cols = out_ref.shape[1]
    total = part_refs[0][...]
    for ref in part_refs[1:]:
        total = total + ref[...]
    scale = lax.rsqrt(total[:, q_cols : q_cols + 1] / features + 1e-05)
    out_ref[...] = (total[:, :q_cols] * scale).astype(BF16)


def finish(parts, features):
    rows, cols = parts[0].shape
    return pl.pallas_call(
        lambda *refs: finish_kernel(features, *refs),
        out_shape=jax.ShapeDtypeStruct((rows, cols - 128), BF16),
        in_specs=[vmem()] * CTX,
        out_specs=vmem(),
        compiler_params=params(),
        cost_estimate=NO_COST,
        name="finish",
    )(*parts)


def pack_kernel(index_ref, pool_ref, *refs):
    steps = index_ref.shape[0]
    outs = refs[:steps]
    pool, held, sems = refs[steps:]
    fetch = pltpu.make_async_copy(pool_ref, pool, sems.at[steps])
    fetch.start()
    fetch.wait()
    copies = []
    for step in range(steps):
        for n in range(held.shape[1]):
            held[step, n] = pool[index_ref[step, n]]
        copies.append(pltpu.make_async_copy(held.at[step], outs[step], sems.at[step]))
        copies[-1].start()
    for copy in copies:
        copy.wait()


def pack(index, pool):
    steps, count = index.shape
    block = pool.shape[1:]
    return pl.pallas_call(
        pack_kernel,
        out_shape=[jax.ShapeDtypeStruct((count,) + block, BF16)] * steps,
        in_specs=[smem(), anywhere()],
        out_specs=[anywhere()] * steps,
        scratch_shapes=[
            pltpu.VMEM(pool.shape, BF16),
            pltpu.VMEM((steps, count) + block, BF16),
            pltpu.SemaphoreType.DMA((steps + 1,)),
        ],
        compiler_params=params(VMEM_MOST),
        cost_estimate=NO_COST,
        name="pack",
    )(index, pool)


def pack_lanes(ref, rows):
    lane = lax.broadcasted_iota(jnp.int32, (ref.shape[1], 128), 1)[: ref[0, rows, :].shape[0]]
    packed = jnp.zeros(lane.shape, F32)
    for head in range(ref.shape[0]):
        packed = jnp.where(lane == head, ref[head, rows, :], packed)
    return packed


def sweep(q_ref, rows, heads, keys, finish_head):
    pending = None
    for head in range(heads):
        cols = slice(head * 128, head * 128 + 128)
        scores = lax.dot_general(q_ref[rows, cols], keys, NT, preferred_element_type=F32)
        if pending is not None:
            finish_head(*pending)
        pending = (head, cols, scores)
    finish_head(*pending)


def moving(q_ref, m_ref, l_ref, acc_ref, rows, keys, values_ext, mask, const, zero):
    def finish_head(head, cols, scores):
        scores = jnp.where(mask, scores, NEG_FILL)
        m_old = m_ref[head, rows, :]
        m_new = jnp.maximum(m_old, jnp.max(scores, axis=1, keepdims=True) * const)
        alpha = jnp.exp2(m_old - m_new)
        reps = scores.shape[1] // 128
        weights = jnp.exp2(scores * const - jnp.concatenate([m_new] * reps, axis=1))
        if zero:
            weights = jnp.where(mask, weights, 0.0)
        mixed = jnp.dot(weights.astype(BF16), values_ext, preferred_element_type=F32)
        m_ref[head, rows, :] = m_new
        l_ref[head, rows, :] = l_ref[head, rows, :] * alpha + mixed[:, 128:]
        acc_ref[rows, cols] = acc_ref[rows, cols] * alpha + mixed[:, :128]

    sweep(q_ref, rows, m_ref.shape[0], keys, finish_head)


def steady(q_ref, m_ref, l_ref, acc_ref, rows, keys, values_ext, mask, const):
    def finish_head(head, cols, scores):
        if mask is not None:
            scores = jnp.where(mask, scores, NEG_FILL)
        reps = scores.shape[1] // 128
        shift = jnp.concatenate([m_ref[head, rows, :]] * reps, axis=1)
        weights = jnp.exp2(scores * const - shift)
        mixed = jnp.dot(weights.astype(BF16), values_ext, preferred_element_type=F32)
        l_ref[head, rows, :] += mixed[:, 128:]
        acc_ref[rows, cols] += mixed[:, :128]

    sweep(q_ref, rows, m_ref.shape[0], keys, finish_head)


def prefix_part(meta_ref, base, q_ref, qn_ref, kv_ref, vx_ref, m_ref, l_ref, acc_ref, new_len, const):
    blocks = kv_ref.shape[0]
    state = (q_ref, m_ref, l_ref, acc_ref)
    all_keys = kv_ref[:, 0].reshape(blocks * 128, 128)
    vx_ref[:, :128] = kv_ref[:, 1].reshape(blocks * 128, 128)
    vx_ref[:, 128:] = jnp.ones((blocks * 128, 128), BF16)
    norms = jnp.dot(all_keys * all_keys, jnp.ones((128, 128), BF16), preferred_element_type=F32)
    reach = jnp.sqrt(jnp.max(norms)) * (1.05 * const)

    def session_body(session, carry):
        row0 = pl.multiple_of(session * new_len, new_len)
        rows = pl.ds(row0, new_len)
        first = meta_ref[base + 2 * session]
        keys_live = meta_ref[base + 2 * session + 1]
        high = first * 128 + keys_live
        total = (keys_live + 127) // 128

        def enough():
            room = qn_ref[rows, :] * reach - pack_lanes(m_ref, rows)
            return (jnp.max(room) <= ROOM).astype(jnp.int32)

        def piece(wanted, count, masked):
            span = count * 128
            begin = jnp.minimum(wanted, blocks - count)
            keys = kv_ref[pl.ds(begin, count), 0].reshape(span, 128)
            values_ext = vx_ref[pl.ds(pl.multiple_of(begin * 128, 128), span), :]
            if not masked:
                return keys, values_ext, None
            index = begin * 128 + lax.broadcasted_iota(jnp.int32, (1, span), 1)
            return keys, values_ext, (index >= wanted * 128) & (index < high)

        def slow_more(now):
            return (now[0] < total) & (now[1] == 0)

        def slow(now):
            moving(*state, rows, *piece(first + now[0], CHUNK, True), const, False)
            return now[0] + CHUNK, enough()

        done, _ = lax.while_loop(slow_more, slow, (0, enough()))
        full = jnp.maximum(keys_live - done * 128, 0) // (CHUNK * 128)

        def fast(step, carry):
            steady(*state, rows, *piece(first + done + step * CHUNK, CHUNK, False), const)
            return carry

        lax.fori_loop(0, full, fast, 0)
        done = done + full * CHUNK

        def tail(step, carry):
            steady(*state, rows, *piece(first + done + step * TAIL, TAIL, True), const)
            return carry

        lax.fori_loop(0, (jnp.maximum(total - done, 0) + TAIL - 1) // TAIL, tail, 0)
        return carry

    lax.fori_loop(0, q_ref.shape[0] // new_len, session_body, 0)


def first_kernel(
    new_len, const, meta_ref, a, b, c, d, buf, pool_ref,
    q_ref, qn_ref, acc_ref, mp_ref, lp_ref, new_ref, pool_out,
    kv_ref, vx_ref, m_ref, l_ref, sem, pool_sem,
):
    fetch = pltpu.make_async_copy(buf, kv_ref, sem)
    fetch.start()
    keep = pltpu.make_async_copy(pool_ref, pool_out, pool_sem)
    keep.start()
    tokens, q_cols = q_ref.shape
    part = a.shape[0]
    heads = m_ref.shape[0]
    rank = meta_ref[0]
    for step, ref in enumerate((a, b, c, d)):
        place = lax.rem(rank + CTX - step, CTX)
        q_ref[pl.ds(pl.multiple_of(place * part, part), part), :] = ref[:, :q_cols]
        new_ref[place, 0] = ref[:, q_cols : q_cols + 128]
        new_ref[place, 1] = ref[:, q_cols + 128 :]
    m_ref[...] = jnp.full(m_ref.shape, NEG_FILL, F32)
    l_ref[...] = jnp.zeros(l_ref.shape, F32)
    acc_ref[...] = jnp.zeros(acc_ref.shape, F32)
    lane = lax.broadcasted_iota(jnp.int32, (tokens, 128), 1)
    squares = jnp.zeros((tokens, 128), F32)
    for head in range(heads):
        wide = q_ref[:, head * 128 : head * 128 + 128].astype(F32)
        squares = jnp.where(lane == head, jnp.sum(wide * wide, axis=1, keepdims=True), squares)
    qn_ref[...] = jnp.sqrt(squares)
    keys = a[:, q_cols : q_cols + 128]
    values_ext = jnp.concatenate(
        [a[:, q_cols + 128 : q_cols + 256], jnp.ones((part, 128), BF16)], axis=1
    )
    per_session = new_len // part
    rows = pl.ds(pl.multiple_of(lax.div(rank, per_session) * new_len, new_len), new_len)
    offset = lax.rem(rank, per_session) * part
    token = lax.broadcasted_iota(jnp.int32, (new_len, part), 0)
    fresh = lax.broadcasted_iota(jnp.int32, (new_len, part), 1) + offset
    moving(q_ref, m_ref, l_ref, acc_ref, rows, keys, values_ext, fresh <= token, const, True)
    fetch.wait()
    prefix_part(
        meta_ref, 1, q_ref, qn_ref, kv_ref, vx_ref, m_ref, l_ref, acc_ref, new_len, const
    )
    mp_ref[...] = pack_lanes(m_ref, slice(None))
    lp_ref[...] = pack_lanes(l_ref, slice(None))
    keep.wait()


def load_state(mp_in, lp_in, m_ref, l_ref):
    shape = m_ref.shape[1:]
    for head in range(m_ref.shape[0]):
        m_ref[head] = jnp.broadcast_to(mp_in[:, head : head + 1], shape)
        l_ref[head] = jnp.broadcast_to(lp_in[:, head : head + 1], shape)


def sources(
    new_len, const, meta_ref, q_ref, qn_ref, bufs, acc_in, mp_in, lp_in,
    acc_ref, kv_ref, vx_ref, m_ref, l_ref, sems,
):
    copies = []
    for n, buf in enumerate(bufs):
        copies.append(pltpu.make_async_copy(buf, kv_ref.at[n], sems.at[n]))
        copies[-1].start()
    acc_ref[...] = acc_in[...]
    load_state(mp_in, lp_in, m_ref, l_ref)
    for n, copy in enumerate(copies):
        copy.wait()
        prefix_part(
            meta_ref, 4 * n, q_ref, qn_ref, kv_ref.at[n], vx_ref, m_ref, l_ref, acc_ref, new_len,
            const,
        )


def near_kernel(
    new_len, const, meta_ref, q_ref, qn_ref, acc_in, mp_in, lp_in, buf_a, buf_b,
    acc_ref, mp_ref, lp_ref, kv_ref, vx_ref, m_ref, l_ref, sems,
):
    sources(
        new_len, const, meta_ref, q_ref, qn_ref, (buf_a, buf_b), acc_in, mp_in, lp_in,
        acc_ref, kv_ref, vx_ref, m_ref, l_ref, sems,
    )
    mp_ref[...] = pack_lanes(m_ref, slice(None))
    lp_ref[...] = pack_lanes(l_ref, slice(None))


def last_kernel(
    new_len, const, meta_ref, q_ref, qn_ref, acc_in, mp_in, lp_in, buf,
    out_a, out_b, out_c, out_d, acc_ref, kv_ref, vx_ref, m_ref, l_ref, sems,
):
    sources(
        new_len, const, meta_ref, q_ref, qn_ref, (buf,), acc_in, mp_in, lp_in,
        acc_ref, kv_ref, vx_ref, m_ref, l_ref, sems,
    )
    tokens = q_ref.shape[0]
    heads = m_ref.shape[0]
    part = tokens // CTX
    rank = meta_ref[4]
    row = lax.broadcasted_iota(jnp.int32, (16, heads * 128), 0)
    for step, out_ref in enumerate((out_a, out_b, out_c, out_d)):
        place = lax.rem(rank + step, CTX)
        rows = pl.ds(pl.multiple_of(place * part, part), part)
        for head in range(heads):
            cols = slice(head * 128, head * 128 + 128)
            total = l_ref[head, rows, :]
            empty = total == 0.0
            safe = jnp.where(empty, 1.0, total)
            out_ref[:part, cols] = (acc_ref[rows, cols] / safe).astype(BF16)
            m_ref[head, rows, :] = jnp.where(
                empty, NEG_FILL, m_ref[head, rows, :] + jnp.log2(safe)
            )
        turned = pack_lanes(m_ref, rows).T
        line = jnp.concatenate([turned[h : h + 1] for h in range(heads)], axis=1)
        high = line.astype(BF16).astype(F32)
        rest = line - high
        mid = rest.astype(BF16).astype(F32)
        low = rest - mid
        tile = jnp.where(row == 0, high, jnp.where(row == 1, mid, jnp.where(row == 2, low, 0.0)))
        out_ref[part : part + 16, :] = tile.astype(BF16)


def scratch(tokens, heads, blocks, lead=()):
    return [
        pltpu.VMEM(lead + (blocks, 2, 128, 128), BF16),
        pltpu.VMEM((blocks * 128, 256), BF16),
        pltpu.VMEM((heads, tokens, 128), F32),
        pltpu.VMEM((heads, tokens, 128), F32),
    ]


def state_shapes(tokens, q_cols):
    return [
        jax.ShapeDtypeStruct((tokens, q_cols), F32),
        jax.ShapeDtypeStruct((tokens, 128), F32),
        jax.ShapeDtypeStruct((tokens, 128), F32),
    ]


def attend_own(meta, quarters, buf, pool, new_len, const):
    part = quarters[0].shape[0]
    q_cols = quarters[0].shape[1] - 256
    tokens = part * CTX
    heads = q_cols // 128
    blocks = buf.shape[0]
    return pl.pallas_call(
        lambda *refs: first_kernel(new_len, const, *refs),
        out_shape=[
            jax.ShapeDtypeStruct((tokens, q_cols), BF16),
            jax.ShapeDtypeStruct((tokens, 128), F32),
        ]
        + state_shapes(tokens, q_cols)
        + [
            jax.ShapeDtypeStruct((CTX, 2, part, 128), BF16),
            jax.ShapeDtypeStruct(pool.shape, BF16),
        ],
        in_specs=[smem()] + [vmem()] * 4 + [anywhere()] * 2,
        out_specs=[vmem()] * 6 + [anywhere()],
        scratch_shapes=scratch(tokens, heads, blocks)
        + [pltpu.SemaphoreType.DMA(()), pltpu.SemaphoreType.DMA(())],
        compiler_params=params(VMEM_MOST),
        cost_estimate=NO_COST,
        name="attend_own",
    )(meta, *quarters, buf, pool)


def attend_near(meta, queries, norms, state, bufs, new_len, const):
    tokens, q_cols = queries.shape
    heads = q_cols // 128
    blocks = bufs[0].shape[0]
    return pl.pallas_call(
        lambda *refs: near_kernel(new_len, const, *refs),
        out_shape=state_shapes(tokens, q_cols),
        in_specs=[smem()] + [vmem()] * 5 + [anywhere()] * 2,
        out_specs=[vmem()] * 3,
        scratch_shapes=scratch(tokens, heads, blocks, (2,))
        + [pltpu.SemaphoreType.DMA((2,))],
        compiler_params=params(),
        cost_estimate=NO_COST,
        name="attend_near",
    )(meta, queries, norms, *state, *bufs)


def attend_last(meta, queries, norms, state, buf, new_len, const):
    tokens, q_cols = queries.shape
    heads = q_cols // 128
    blocks = buf.shape[0]
    pairs = blocks * 128 * tokens // 2 * heads
    return pl.pallas_call(
        lambda *refs: last_kernel(new_len, const, *refs),
        out_shape=[jax.ShapeDtypeStruct((tokens // CTX + 16, q_cols), BF16)] * CTX,
        in_specs=[smem()] + [vmem()] * 5 + [anywhere()],
        out_specs=[vmem()] * CTX,
        scratch_shapes=[pltpu.VMEM((tokens, q_cols), F32)]
        + scratch(tokens, heads, blocks, (1,))
        + [pltpu.SemaphoreType.DMA((1,))],
        compiler_params=params(),
        cost_estimate=pl.CostEstimate(
            flops=pairs * 512, bytes_accessed=8 << 20, transcendentals=pairs
        ),
        name="attend_last",
    )(meta, queries, norms, *state, buf)


def combine_kernel(*refs):
    in_refs, out_ref = refs[:CTX], refs[CTX]
    part, q_cols = out_ref.shape
    heads = q_cols // 128
    lines = []
    for c in range(CTX):
        tile = in_refs[c][part : part + 16, :].astype(F32)
        lines.append(tile[0:1] + tile[1:2] + tile[2:3])
    top = lines[0]
    for line in lines[1:]:
        top = jnp.maximum(top, line)
    shares = [jnp.exp2(line - top) for line in lines]
    total = shares[0] + shares[1] + shares[2] + shares[3]
    pieces = []
    for share in shares:
        share = share / total
        pieces += [share[:, h * 128 : h * 128 + 128] for h in range(heads)]
    pieces.append(jnp.zeros((128 - CTX * heads, 128), F32))
    turned = jnp.concatenate(pieces, axis=0).T
    for head in range(heads):
        cols = slice(head * 128, head * 128 + 128)
        mixed = jnp.zeros((part, 128), F32)
        for c in range(CTX):
            at = c * heads + head
            mixed = mixed + in_refs[c][:part, cols].astype(F32) * turned[:, at : at + 1]
        out_ref[:, cols] = mixed.astype(BF16)


def combine(arrived):
    rows, q_cols = arrived[0].shape
    return pl.pallas_call(
        combine_kernel,
        out_shape=jax.ShapeDtypeStruct((rows - 16, q_cols), BF16),
        in_specs=[vmem()] * CTX,
        out_specs=vmem(),
        compiler_params=params(),
        cost_estimate=NO_COST,
        name="combine",
    )(*arrived)


def out_kernel(
    meta_ref, place_ref, a, b, c, d, w_ref, new_a, new_b, new_c, new_d, pool_in,
    own_ref, send_ref, pool_out, rows_ref, sems,
):
    rank = meta_ref[0]
    core = meta_ref[1]
    part = a.shape[0]
    half = own_ref.shape[2]

    def place_blocks(act):
        count = new_a.shape[0]
        for n, ref in enumerate((new_a, new_b, new_c, new_d)):
            for i in range(count):
                at = n * count + i
                slot = place_ref[at]

                @pl.when(slot >= 0)
                def _(ref=ref, i=i, at=at, slot=slot):
                    act(pltpu.make_async_copy(ref.at[i], pool_out.at[slot], sems.at[at]))

    @pl.when(pl.program_id(0) == 0)
    def _():
        place_blocks(lambda copy: copy.start())
        for step, ref in enumerate((a, b, c, d)):
            place = lax.rem(rank + CTX - step, CTX)
            rows_ref[pl.ds(pl.multiple_of(place * part, part), part), :] = ref[...]

    product = jnp.dot(rows_ref[...], w_ref[...], preferred_element_type=F32)

    @pl.when(core == 0)
    def _():
        own_ref[0] = product[:, :half]
        send_ref[0] = product[:, half:].astype(BF16)

    @pl.when(core != 0)
    def _():
        own_ref[0] = product[:, half:]
        send_ref[0] = product[:, :half].astype(BF16)

    @pl.when(pl.program_id(0) == pl.num_programs(0) - 1)
    def _():
        place_blocks(lambda copy: copy.wait())


def project_out(meta, places, quarters, w_out, news, pool, planes):
    part, depth = quarters[0].shape
    tokens = part * CTX
    width = w_out.shape[1] // planes
    whole = pl.BlockSpec((part, depth), lambda i, *_: (0, 0))
    out = pl.BlockSpec((1, tokens, width // 2), lambda i, *_: (i, 0, 0))
    return pl.pallas_call(
        out_kernel,
        grid_spec=pltpu.PrefetchScalarGridSpec(
            num_scalar_prefetch=2,
            grid=(planes,),
            in_specs=[whole] * 4
            + [pl.BlockSpec((depth, width), lambda i, meta, _: (0, lax.rem(meta[2] + i, planes)))]
            + [anywhere()] * 5,
            out_specs=[out] * 2 + [anywhere()],
            scratch_shapes=[
                pltpu.VMEM((tokens, depth), BF16),
                pltpu.SemaphoreType.DMA((places.shape[0],)),
            ],
        ),
        out_shape=[
            jax.ShapeDtypeStruct((planes, tokens, width // 2), F32),
            jax.ShapeDtypeStruct((planes, tokens, width // 2), BF16),
            jax.ShapeDtypeStruct(pool.shape, BF16),
        ],
        input_output_aliases={11: 2},
        compiler_params=params(),
        cost_estimate=NO_COST,
        name="project_out",
    )(meta, places, *quarters, w_out, *news, pool)


def shifted(value, axis, step):
    size = lax.axis_size(axis)
    return lax.ppermute(value, axis, [(i, (i + step) % size) for i in range(size)])


def around(value, axis):
    return [value] + [shifted(value, axis, step) for step in (1, 2, 3)]


def local(
    tokens, norm_gain, w_query, w_key, w_value, w_out, kv_pool, block_table, prefix_len, write_slot
):
    groups = lax.axis_size("group")
    ranks = lax.axis_size("ctx")
    tp_size = lax.axis_size("tp")
    rank = lax.axis_index("ctx")
    group = lax.axis_index("group")
    core = lax.axis_index("tp") % 2
    plane = lax.axis_index("tp") // 2
    pool_size = kv_pool.shape[0]
    sessions, list_len = block_table.shape
    sess_here = sessions // groups
    per_pair = sess_here * list_len // (groups * ranks)
    new_len = tokens.shape[0] // sess_here
    head_dim = kv_pool.shape[4]
    const = head_dim**-0.5 * LOG2E
    device_id = group * ranks + rank
    pool = kv_pool.reshape(pool_size, 2, head_dim, head_dim)

    table = block_table.reshape(groups, sess_here * list_len)
    steps = jnp.arange(groups, dtype=jnp.int32)
    send_table = jnp.roll(table, -group, axis=0)
    here = send_table // pool_size == device_id
    upper = jnp.triu(jnp.ones((sess_here * list_len,) * 2, BF16))
    order = jnp.dot(here.astype(BF16), upper, preferred_element_type=F32).astype(jnp.int32)
    wanted = jnp.arange(1, per_pair + 1, dtype=jnp.int32)
    picked = here[:, None, :] & (order[:, None, :] == wanted[None, :, None])
    send_index = jnp.sum(jnp.where(picked, send_table[:, None, :] % pool_size, 0), axis=2)
    blocks = pack(send_index[1:], pool)
    near = [shifted(blocks[0], "group", 1), shifted(blocks[2], "group", 3)]

    mine = lax.dynamic_index_in_dim(table, group, 0, keepdims=False).reshape(sess_here, list_len)
    lengths = lax.dynamic_slice_in_dim(prefix_len, group * sess_here, sess_here)
    source = ((group - steps) % groups) * ranks + rank
    from_there = mine[None] // pool_size == source[:, None, None]
    slots = jnp.arange(list_len, dtype=jnp.int32)
    keys_in = jnp.clip(lengths[:, None] - slots[None, :] * head_dim, 0, head_dim)
    live_keys = jnp.sum(jnp.where(from_there, keys_in[None], 0), axis=2)
    counts = jnp.sum(from_there.astype(jnp.int32), axis=2)
    starts = jnp.cumsum(counts, axis=1) - counts
    meta = jnp.stack([starts, live_keys], axis=2).reshape(groups, 2 * sess_here).astype(jnp.int32)

    rank_only = rank[None].astype(jnp.int32)
    tokens, _ = lax.optimization_barrier((tokens, blocks))
    parts = project(rank_only, tokens, norm_gain[None, :], w_query, w_key, w_value)
    parts = [parts[0]] + [shifted(parts[step], "ctx", step) for step in (1, 3, 2)]
    fresh = finish(parts, tokens.shape[1] * ranks)
    own_index, _ = lax.optimization_barrier((send_index[:1], parts[0]))
    own_blocks = pack(own_index, pool)[0]
    far, fresh = lax.optimization_barrier((blocks[1], fresh))
    far = shifted(far, "group", 2)
    quarters = around(fresh, "ctx")

    first_meta = jnp.concatenate([rank_only, meta[0]])
    queries, norms, *state, block, new_pool = attend_own(
        first_meta, quarters, own_blocks, pool, new_len, const
    )
    near_meta = jnp.concatenate([meta[1], meta[3]])
    state = attend_near(near_meta, queries, norms, state, near, new_len, const)
    last_meta = jnp.concatenate([meta[2], rank_only])
    partial = attend_last(last_meta, queries, norms, state, far, new_len, const)
    partial = [partial[0]] + [shifted(partial[step], "ctx", step) for step in (1, 2, 3)]
    attended = combine(partial)

    planes = tp_size // 2
    out_meta = jnp.stack([rank, core, plane]).astype(jnp.int32)
    news = around(block, "group")
    targets = jnp.roll(write_slot.reshape(groups, ranks)[::-1], group + 1, axis=0).reshape(-1)
    places = jnp.where(targets // pool_size == device_id, targets % pool_size, -1)
    own, send, new_pool = project_out(
        out_meta, places, around(attended, "ctx"), w_out, news, new_pool, planes
    )
    other = lax.ppermute(send, "tp", [(i, i ^ 1) for i in range(tp_size)])
    total = own[0] + other[0].astype(F32)
    for step in range(1, planes):
        pair = (own[step] + other[step].astype(F32)).astype(BF16)
        total = total + shifted(pair, "tp", 2 * step).astype(F32)
    return (total.astype(BF16), new_pool.reshape(kv_pool.shape))


def solution(mesh):
    placed = (
        P("group", "ctx"),
        P("ctx"),
        P("ctx", "tp"),
        P("ctx", "tp"),
        P("ctx", "tp"),
        P("tp", "ctx"),
        P(("group", "ctx"), None, "tp", None, None),
        P(),
        P(),
        P(),
    )
    return jax.shard_map(
        local,
        mesh=mesh,
        in_specs=placed,
        out_specs=(P("group", ("ctx", "tp")), P(("group", "ctx"), None, "tp", None, None)),
        check_vma=False,
    )
```

```python
import jax
import jax.numpy as jnp
from jax import lax
from jax.experimental import pallas as pl
from jax.experimental.pallas import tpu as pltpu
from jax.sharding import PartitionSpec as P

NEG_FILL = -1e30
LOG2E = 1.4426950408889634
F32 = jnp.float32
BF16 = jnp.bfloat16
VMEM_BYTES = 30 * 1024 * 1024
VMEM_MOST = 58 * 1024 * 1024
CHUNK = 4
TAIL = 2
ROOM = 60.0
NO_COST = pl.CostEstimate(flops=1, bytes_accessed=1, transcendentals=0)
CTX = 4
NT = (((1,), (1,)), ((), ()))


def params(size=VMEM_BYTES):
    return pltpu.CompilerParams(vmem_limit_bytes=size)


def vmem():
    return pl.BlockSpec(memory_space=pltpu.VMEM)


def smem():
    return pl.BlockSpec(memory_space=pltpu.SMEM)


def anywhere():
    return pl.BlockSpec(memory_space=pl.ANY)


def gather_blocks(index_ref, pool, held, outs, sems):
    copies = []
    for step in range(held.shape[0]):
        for n in range(held.shape[1]):
            held[step, n] = pool[index_ref[step, n]]
        copies.append(pltpu.make_async_copy(held.at[step], outs[step], sems.at[step]))
        copies[-1].start()
    return copies


def project_kernel(
    meta_ref, index_ref, pool_ref, tok_ref, gain_ref, wq_ref, wk_ref, wv_ref, *refs
):
    steps = index_ref.shape[0]
    out_refs, block_refs = refs[:CTX], refs[CTX : CTX + steps]
    pool, held, tok, wq, wkv, norm, total, in_sems, out_sems, block_sems = refs[CTX + steps :]
    rows, features = tok.shape
    q_cols = wq.shape[1]
    deep = features // 4
    part = rows // CTX
    rank = meta_ref[0]
    fetch_tok = pltpu.make_async_copy(tok_ref, tok, in_sems.at[0])
    fetch_w = [
        pltpu.make_async_copy(
            wq_ref.at[pl.ds(n * deep, deep)], wq.at[pl.ds(n * deep, deep)], in_sems.at[1 + n]
        )
        for n in range(4)
    ]
    fetch_kv = [
        pltpu.make_async_copy(ref, wkv.at[:, pl.ds(n * 128, 128)], in_sems.at[5 + n])
        for n, ref in enumerate((wk_ref, wv_ref))
    ]
    fetch_pool = pltpu.make_async_copy(pool_ref, pool, block_sems.at[steps])
    for copy in [fetch_pool, fetch_tok] + fetch_kv + fetch_w:
        copy.start()
    fetch_pool.wait()
    sent = gather_blocks(index_ref, pool, held, block_refs, block_sems)
    fetch_tok.wait()
    for first in range(0, rows, part):
        some = slice(first, first + part)
        wide = tok[some].astype(F32)
        norm[some] = (wide * gain_ref[...]).astype(BF16)
        squares = jnp.sum(wide * wide, axis=1, keepdims=True)
        total[some, q_cols + 256 :] = jnp.broadcast_to(squares, (part, 128))
    for copy in fetch_kv:
        copy.wait()
    total[:, q_cols : q_cols + 256] = jnp.dot(norm[...], wkv[...], preferred_element_type=F32)
    half = 2 * deep
    for n in range(2):
        fetch_w[2 * n].wait()
        fetch_w[2 * n + 1].wait()
        depth = slice(n * half, n * half + half)
        for first in range(0, q_cols, 256):
            cols = slice(first, first + 256)
            value = jnp.dot(norm[:, depth], wq[depth, cols], preferred_element_type=F32)
            if n == 0:
                total[:, cols] = value
            else:
                total[:, cols] += value
    copies = []
    for step in range(CTX):
        place = lax.rem(rank + step, CTX)
        source = total.at[pl.ds(pl.multiple_of(place * part, part), part)]
        copies.append(pltpu.make_async_copy(source, out_refs[step], out_sems.at[step]))
        copies[-1].start()
    for copy in sent + copies:
        copy.wait()


def project(meta, index, pool, tokens, gain, w_query, w_key, w_value):
    steps, count = index.shape
    block = pool.shape[1:]
    rows, features = tokens.shape
    q_cols = w_query.shape[1]
    cols = q_cols + 384
    return pl.pallas_call(
        project_kernel,
        out_shape=[jax.ShapeDtypeStruct((rows // CTX, cols), F32)] * CTX
        + [jax.ShapeDtypeStruct((count,) + block, BF16)] * steps,
        in_specs=[smem(), smem(), anywhere(), anywhere(), vmem()] + [anywhere()] * 3,
        out_specs=[anywhere()] * (CTX + steps),
        scratch_shapes=[
            pltpu.VMEM(pool.shape, BF16),
            pltpu.VMEM((steps, count) + block, BF16),
            pltpu.VMEM((rows, features), BF16),
            pltpu.VMEM((features, q_cols), BF16),
            pltpu.VMEM((features, 256), BF16),
            pltpu.VMEM((rows, features), BF16),
            pltpu.VMEM((rows, cols), F32),
            pltpu.SemaphoreType.DMA((7,)),
            pltpu.SemaphoreType.DMA((CTX,)),
            pltpu.SemaphoreType.DMA((steps + 1,)),
        ],
        compiler_params=params(VMEM_MOST),
        cost_estimate=NO_COST,
        name="project",
    )(meta, index, pool, tokens, gain, w_query, w_key, w_value)


def finish_kernel(features, *refs):
    part_refs, out_ref = refs[:CTX], refs[CTX]
    q_cols = out_ref.shape[1]
    total = part_refs[0][...]
    for ref in part_refs[1:]:
        total = total + ref[...]
    scale = lax.rsqrt(total[:, q_cols : q_cols + 1] / features + 1e-05)
    out_ref[...] = (total[:, :q_cols] * scale).astype(BF16)


def finish(parts, features):
    rows, cols = parts[0].shape
    return pl.pallas_call(
        lambda *refs: finish_kernel(features, *refs),
        out_shape=jax.ShapeDtypeStruct((rows, cols - 128), BF16),
        in_specs=[vmem()] * CTX,
        out_specs=vmem(),
        compiler_params=params(),
        cost_estimate=NO_COST,
        name="finish",
    )(*parts)


def pack_kernel(index_ref, pool_ref, *refs):
    steps = index_ref.shape[0]
    outs = refs[:steps]
    pool_out, pool, held, sems = refs[steps:]
    fetch = pltpu.make_async_copy(pool_ref, pool, sems.at[steps])
    fetch.start()
    fetch.wait()
    keep = pltpu.make_async_copy(pool, pool_out, sems.at[steps])
    keep.start()
    for copy in gather_blocks(index_ref, pool, held, outs, sems) + [keep]:
        copy.wait()


def pack(index, pool):
    steps, count = index.shape
    block = pool.shape[1:]
    return pl.pallas_call(
        pack_kernel,
        out_shape=[jax.ShapeDtypeStruct((count,) + block, BF16)] * steps
        + [jax.ShapeDtypeStruct(pool.shape, BF16)],
        in_specs=[smem(), anywhere()],
        out_specs=[anywhere()] * (steps + 1),
        scratch_shapes=[
            pltpu.VMEM(pool.shape, BF16),
            pltpu.VMEM((steps, count) + block, BF16),
            pltpu.SemaphoreType.DMA((steps + 1,)),
        ],
        compiler_params=params(VMEM_MOST),
        cost_estimate=NO_COST,
        name="pack",
    )(index, pool)


def pack_lanes(ref, rows):
    lane = lax.broadcasted_iota(jnp.int32, (ref.shape[1], 128), 1)[: ref[0, rows, :].shape[0]]
    packed = jnp.zeros(lane.shape, F32)
    for head in range(ref.shape[0]):
        packed = jnp.where(lane == head, ref[head, rows, :], packed)
    return packed


def sweep(q_ref, rows, heads, keys, finish_head):
    pending = None
    for head in range(heads):
        cols = slice(head * 128, head * 128 + 128)
        scores = lax.dot_general(q_ref[rows, cols], keys, NT, preferred_element_type=F32)
        if pending is not None:
            finish_head(*pending)
        pending = (head, cols, scores)
    finish_head(*pending)


def moving(q_ref, m_ref, l_ref, acc_ref, rows, keys, values_ext, mask, const, zero):
    def finish_head(head, cols, scores):
        scores = jnp.where(mask, scores, NEG_FILL)
        m_old = m_ref[head, rows, :]
        m_new = jnp.maximum(m_old, jnp.max(scores, axis=1, keepdims=True) * const)
        alpha = jnp.exp2(m_old - m_new)
        reps = scores.shape[1] // 128
        weights = jnp.exp2(scores * const - jnp.concatenate([m_new] * reps, axis=1))
        if zero:
            weights = jnp.where(mask, weights, 0.0)
        mixed = jnp.dot(weights.astype(BF16), values_ext, preferred_element_type=F32)
        m_ref[head, rows, :] = m_new
        l_ref[head, rows, :] = l_ref[head, rows, :] * alpha + mixed[:, 128:]
        acc_ref[rows, cols] = acc_ref[rows, cols] * alpha + mixed[:, :128]

    sweep(q_ref, rows, m_ref.shape[0], keys, finish_head)


def steady(q_ref, m_ref, l_ref, acc_ref, rows, keys, values_ext, mask, const):
    def finish_head(head, cols, scores):
        if mask is not None:
            scores = jnp.where(mask, scores, NEG_FILL)
        reps = scores.shape[1] // 128
        shift = jnp.concatenate([m_ref[head, rows, :]] * reps, axis=1)
        weights = jnp.exp2(scores * const - shift)
        mixed = jnp.dot(weights.astype(BF16), values_ext, preferred_element_type=F32)
        l_ref[head, rows, :] += mixed[:, 128:]
        acc_ref[rows, cols] += mixed[:, :128]

    sweep(q_ref, rows, m_ref.shape[0], keys, finish_head)


def prefix_part(meta_ref, base, q_ref, qn_ref, kv_ref, vx_ref, m_ref, l_ref, acc_ref, new_len, const):
    blocks = kv_ref.shape[0]
    state = (q_ref, m_ref, l_ref, acc_ref)
    all_keys = kv_ref[:, 0].reshape(blocks * 128, 128)
    vx_ref[:, :128] = kv_ref[:, 1].reshape(blocks * 128, 128)
    vx_ref[:, 128:] = jnp.ones((blocks * 128, 128), BF16)
    norms = jnp.dot(all_keys * all_keys, jnp.ones((128, 128), BF16), preferred_element_type=F32)
    reach = jnp.sqrt(jnp.max(norms)) * (1.05 * const)

    def session_body(session, carry):
        row0 = pl.multiple_of(session * new_len, new_len)
        rows = pl.ds(row0, new_len)
        first = meta_ref[base + 2 * session]
        keys_live = meta_ref[base + 2 * session + 1]
        high = first * 128 + keys_live
        total = (keys_live + 127) // 128

        def enough():
            room = qn_ref[rows, :] * reach - pack_lanes(m_ref, rows)
            return (jnp.max(room) <= ROOM).astype(jnp.int32)

        def piece(wanted, count, masked):
            span = count * 128
            begin = jnp.minimum(wanted, blocks - count)
            keys = kv_ref[pl.ds(begin, count), 0].reshape(span, 128)
            values_ext = vx_ref[pl.ds(pl.multiple_of(begin * 128, 128), span), :]
            if not masked:
                return keys, values_ext, None
            index = begin * 128 + lax.broadcasted_iota(jnp.int32, (1, span), 1)
            return keys, values_ext, (index >= wanted * 128) & (index < high)

        def slow_more(now):
            return (now[0] < total) & (now[1] == 0)

        def slow(now):
            moving(*state, rows, *piece(first + now[0], CHUNK, True), const, False)
            return now[0] + CHUNK, enough()

        done, _ = lax.while_loop(slow_more, slow, (0, enough()))
        full = jnp.maximum(keys_live - done * 128, 0) // (CHUNK * 128)

        def fast(step, carry):
            steady(*state, rows, *piece(first + done + step * CHUNK, CHUNK, False), const)
            return carry

        lax.fori_loop(0, full, fast, 0)
        done = done + full * CHUNK

        def tail(step, carry):
            steady(*state, rows, *piece(first + done + step * TAIL, TAIL, True), const)
            return carry

        lax.fori_loop(0, (jnp.maximum(total - done, 0) + TAIL - 1) // TAIL, tail, 0)
        return carry

    lax.fori_loop(0, q_ref.shape[0] // new_len, session_body, 0)


def first_kernel(
    new_len, const, meta_ref, a, b, c, d, buf,
    q_ref, qn_ref, acc_ref, mp_ref, lp_ref, new_ref, kv_ref, vx_ref, m_ref, l_ref, sem,
):
    fetch = pltpu.make_async_copy(buf, kv_ref, sem)
    fetch.start()
    tokens, q_cols = q_ref.shape
    part = a.shape[0]
    heads = m_ref.shape[0]
    rank = meta_ref[0]
    for step, ref in enumerate((a, b, c, d)):
        place = lax.rem(rank + CTX - step, CTX)
        q_ref[pl.ds(pl.multiple_of(place * part, part), part), :] = ref[:, :q_cols]
        new_ref[place, 0] = ref[:, q_cols : q_cols + 128]
        new_ref[place, 1] = ref[:, q_cols + 128 :]
    m_ref[...] = jnp.full(m_ref.shape, NEG_FILL, F32)
    l_ref[...] = jnp.zeros(l_ref.shape, F32)
    acc_ref[...] = jnp.zeros(acc_ref.shape, F32)
    lane = lax.broadcasted_iota(jnp.int32, (tokens, 128), 1)
    squares = jnp.zeros((tokens, 128), F32)
    for head in range(heads):
        wide = q_ref[:, head * 128 : head * 128 + 128].astype(F32)
        squares = jnp.where(lane == head, jnp.sum(wide * wide, axis=1, keepdims=True), squares)
    qn_ref[...] = jnp.sqrt(squares)
    keys = a[:, q_cols : q_cols + 128]
    values_ext = jnp.concatenate(
        [a[:, q_cols + 128 : q_cols + 256], jnp.ones((part, 128), BF16)], axis=1
    )
    per_session = new_len // part
    rows = pl.ds(pl.multiple_of(lax.div(rank, per_session) * new_len, new_len), new_len)
    offset = lax.rem(rank, per_session) * part
    token = lax.broadcasted_iota(jnp.int32, (new_len, part), 0)
    fresh = lax.broadcasted_iota(jnp.int32, (new_len, part), 1) + offset
    moving(q_ref, m_ref, l_ref, acc_ref, rows, keys, values_ext, fresh <= token, const, True)
    fetch.wait()
    prefix_part(
        meta_ref, 1, q_ref, qn_ref, kv_ref, vx_ref, m_ref, l_ref, acc_ref, new_len, const
    )
    mp_ref[...] = pack_lanes(m_ref, slice(None))
    lp_ref[...] = pack_lanes(l_ref, slice(None))


def load_state(mp_in, lp_in, m_ref, l_ref):
    shape = m_ref.shape[1:]
    for head in range(m_ref.shape[0]):
        m_ref[head] = jnp.broadcast_to(mp_in[:, head : head + 1], shape)
        l_ref[head] = jnp.broadcast_to(lp_in[:, head : head + 1], shape)


def sources(
    new_len, const, meta_ref, q_ref, qn_ref, bufs, acc_in, mp_in, lp_in,
    acc_ref, kv_ref, vx_ref, m_ref, l_ref, sems,
):
    copies = []
    for n, buf in enumerate(bufs):
        copies.append(pltpu.make_async_copy(buf, kv_ref.at[n], sems.at[n]))
        copies[-1].start()
    acc_ref[...] = acc_in[...]
    load_state(mp_in, lp_in, m_ref, l_ref)
    for n, copy in enumerate(copies):
        copy.wait()
        prefix_part(
            meta_ref, 4 * n, q_ref, qn_ref, kv_ref.at[n], vx_ref, m_ref, l_ref, acc_ref, new_len,
            const,
        )


def near_kernel(
    new_len, const, meta_ref, q_ref, qn_ref, acc_in, mp_in, lp_in, buf_a, buf_b,
    acc_ref, mp_ref, lp_ref, kv_ref, vx_ref, m_ref, l_ref, sems,
):
    sources(
        new_len, const, meta_ref, q_ref, qn_ref, (buf_a, buf_b), acc_in, mp_in, lp_in,
        acc_ref, kv_ref, vx_ref, m_ref, l_ref, sems,
    )
    mp_ref[...] = pack_lanes(m_ref, slice(None))
    lp_ref[...] = pack_lanes(l_ref, slice(None))


def last_kernel(
    new_len, const, meta_ref, q_ref, qn_ref, acc_in, mp_in, lp_in, buf,
    out_a, out_b, out_c, out_d, acc_ref, kv_ref, vx_ref, m_ref, l_ref, sems,
):
    sources(
        new_len, const, meta_ref, q_ref, qn_ref, (buf,), acc_in, mp_in, lp_in,
        acc_ref, kv_ref, vx_ref, m_ref, l_ref, sems,
    )
    tokens = q_ref.shape[0]
    heads = m_ref.shape[0]
    part = tokens // CTX
    rank = meta_ref[4]
    row = lax.broadcasted_iota(jnp.int32, (16, heads * 128), 0)
    for step, out_ref in enumerate((out_a, out_b, out_c, out_d)):
        place = lax.rem(rank + step, CTX)
        rows = pl.ds(pl.multiple_of(place * part, part), part)
        for head in range(heads):
            cols = slice(head * 128, head * 128 + 128)
            total = l_ref[head, rows, :]
            empty = total == 0.0
            safe = jnp.where(empty, 1.0, total)
            out_ref[:part, cols] = (acc_ref[rows, cols] / safe).astype(BF16)
            m_ref[head, rows, :] = jnp.where(
                empty, NEG_FILL, m_ref[head, rows, :] + jnp.log2(safe)
            )
        turned = pack_lanes(m_ref, rows).T
        line = jnp.concatenate([turned[h : h + 1] for h in range(heads)], axis=1)
        high = line.astype(BF16).astype(F32)
        rest = line - high
        mid = rest.astype(BF16).astype(F32)
        low = rest - mid
        tile = jnp.where(row == 0, high, jnp.where(row == 1, mid, jnp.where(row == 2, low, 0.0)))
        out_ref[part : part + 16, :] = tile.astype(BF16)


def scratch(tokens, heads, blocks, lead=()):
    return [
        pltpu.VMEM(lead + (blocks, 2, 128, 128), BF16),
        pltpu.VMEM((blocks * 128, 256), BF16),
        pltpu.VMEM((heads, tokens, 128), F32),
        pltpu.VMEM((heads, tokens, 128), F32),
    ]


def state_shapes(tokens, q_cols):
    return [
        jax.ShapeDtypeStruct((tokens, q_cols), F32),
        jax.ShapeDtypeStruct((tokens, 128), F32),
        jax.ShapeDtypeStruct((tokens, 128), F32),
    ]


def attend_own(meta, quarters, buf, new_len, const):
    part = quarters[0].shape[0]
    q_cols = quarters[0].shape[1] - 256
    tokens = part * CTX
    heads = q_cols // 128
    blocks = buf.shape[0]
    return pl.pallas_call(
        lambda *refs: first_kernel(new_len, const, *refs),
        out_shape=[
            jax.ShapeDtypeStruct((tokens, q_cols), BF16),
            jax.ShapeDtypeStruct((tokens, 128), F32),
        ]
        + state_shapes(tokens, q_cols)
        + [jax.ShapeDtypeStruct((CTX, 2, part, 128), BF16)],
        in_specs=[smem()] + [vmem()] * 4 + [anywhere()],
        out_specs=[vmem()] * 6,
        scratch_shapes=scratch(tokens, heads, blocks) + [pltpu.SemaphoreType.DMA(())],
        compiler_params=params(),
        cost_estimate=NO_COST,
        name="attend_own",
    )(meta, *quarters, buf)


def attend_near(meta, queries, norms, state, bufs, new_len, const):
    tokens, q_cols = queries.shape
    heads = q_cols // 128
    blocks = bufs[0].shape[0]
    return pl.pallas_call(
        lambda *refs: near_kernel(new_len, const, *refs),
        out_shape=state_shapes(tokens, q_cols),
        in_specs=[smem()] + [vmem()] * 5 + [anywhere()] * 2,
        out_specs=[vmem()] * 3,
        scratch_shapes=scratch(tokens, heads, blocks, (2,))
        + [pltpu.SemaphoreType.DMA((2,))],
        compiler_params=params(),
        cost_estimate=NO_COST,
        name="attend_near",
    )(meta, queries, norms, *state, *bufs)


def attend_last(meta, queries, norms, state, buf, new_len, const):
    tokens, q_cols = queries.shape
    heads = q_cols // 128
    blocks = buf.shape[0]
    pairs = blocks * 128 * tokens // 2 * heads
    return pl.pallas_call(
        lambda *refs: last_kernel(new_len, const, *refs),
        out_shape=[jax.ShapeDtypeStruct((tokens // CTX + 16, q_cols), BF16)] * CTX,
        in_specs=[smem()] + [vmem()] * 5 + [anywhere()],
        out_specs=[vmem()] * CTX,
        scratch_shapes=[pltpu.VMEM((tokens, q_cols), F32)]
        + scratch(tokens, heads, blocks, (1,))
        + [pltpu.SemaphoreType.DMA((1,))],
        compiler_params=params(),
        cost_estimate=pl.CostEstimate(
            flops=pairs * 512, bytes_accessed=8 << 20, transcendentals=pairs
        ),
        name="attend_last",
    )(meta, queries, norms, *state, buf)


def combine_kernel(*refs):
    in_refs, out_ref = refs[:CTX], refs[CTX]
    part, q_cols = out_ref.shape
    heads = q_cols // 128
    lines = []
    for c in range(CTX):
        tile = in_refs[c][part : part + 16, :].astype(F32)
        lines.append(tile[0:1] + tile[1:2] + tile[2:3])
    top = lines[0]
    for line in lines[1:]:
        top = jnp.maximum(top, line)
    shares = [jnp.exp2(line - top) for line in lines]
    total = shares[0] + shares[1] + shares[2] + shares[3]
    pieces = []
    for share in shares:
        share = share / total
        pieces += [share[:, h * 128 : h * 128 + 128] for h in range(heads)]
    pieces.append(jnp.zeros((128 - CTX * heads, 128), F32))
    turned = jnp.concatenate(pieces, axis=0).T
    for head in range(heads):
        cols = slice(head * 128, head * 128 + 128)
        mixed = jnp.zeros((part, 128), F32)
        for c in range(CTX):
            at = c * heads + head
            mixed = mixed + in_refs[c][:part, cols].astype(F32) * turned[:, at : at + 1]
        out_ref[:, cols] = mixed.astype(BF16)


def combine(arrived):
    rows, q_cols = arrived[0].shape
    return pl.pallas_call(
        combine_kernel,
        out_shape=jax.ShapeDtypeStruct((rows - 16, q_cols), BF16),
        in_specs=[vmem()] * CTX,
        out_specs=vmem(),
        compiler_params=params(),
        cost_estimate=NO_COST,
        name="combine",
    )(*arrived)


def out_kernel(
    meta_ref, place_ref, a, b, c, d, w_ref, new_a, new_b, new_c, new_d, pool_in,
    own_ref, send_ref, pool_out, rows_ref, sems,
):
    rank = meta_ref[0]
    core = meta_ref[1]
    part = a.shape[0]
    half = own_ref.shape[2]

    def place_blocks(act):
        count = new_a.shape[0]
        for n, ref in enumerate((new_a, new_b, new_c, new_d)):
            for i in range(count):
                at = n * count + i
                slot = place_ref[at]

                @pl.when(slot >= 0)
                def _(ref=ref, i=i, at=at, slot=slot):
                    act(pltpu.make_async_copy(ref.at[i], pool_out.at[slot], sems.at[at]))

    @pl.when(pl.program_id(0) == 0)
    def _():
        place_blocks(lambda copy: copy.start())
        for step, ref in enumerate((a, b, c, d)):
            place = lax.rem(rank + CTX - step, CTX)
            rows_ref[pl.ds(pl.multiple_of(place * part, part), part), :] = ref[...]

    product = jnp.dot(rows_ref[...], w_ref[...], preferred_element_type=F32)

    @pl.when(core == 0)
    def _():
        own_ref[0] = product[:, :half]
        send_ref[0] = product[:, half:].astype(BF16)

    @pl.when(core != 0)
    def _():
        own_ref[0] = product[:, half:]
        send_ref[0] = product[:, :half].astype(BF16)

    @pl.when(pl.program_id(0) == pl.num_programs(0) - 1)
    def _():
        place_blocks(lambda copy: copy.wait())


def project_out(meta, places, quarters, w_out, news, pool, planes):
    part, depth = quarters[0].shape
    tokens = part * CTX
    width = w_out.shape[1] // planes
    whole = pl.BlockSpec((part, depth), lambda i, *_: (0, 0))
    out = pl.BlockSpec((1, tokens, width // 2), lambda i, *_: (i, 0, 0))
    return pl.pallas_call(
        out_kernel,
        grid_spec=pltpu.PrefetchScalarGridSpec(
            num_scalar_prefetch=2,
            grid=(planes,),
            in_specs=[whole] * 4
            + [pl.BlockSpec((depth, width), lambda i, meta, _: (0, lax.rem(meta[2] + i, planes)))]
            + [anywhere()] * 5,
            out_specs=[out] * 2 + [anywhere()],
            scratch_shapes=[
                pltpu.VMEM((tokens, depth), BF16),
                pltpu.SemaphoreType.DMA((places.shape[0],)),
            ],
        ),
        out_shape=[
            jax.ShapeDtypeStruct((planes, tokens, width // 2), F32),
            jax.ShapeDtypeStruct((planes, tokens, width // 2), BF16),
            jax.ShapeDtypeStruct(pool.shape, BF16),
        ],
        input_output_aliases={11: 2},
        compiler_params=params(),
        cost_estimate=NO_COST,
        name="project_out",
    )(meta, places, *quarters, w_out, *news, pool)


def shifted(value, axis, step):
    size = lax.axis_size(axis)
    return lax.ppermute(value, axis, [(i, (i + step) % size) for i in range(size)])


def around(value, axis):
    return [value] + [shifted(value, axis, step) for step in (1, 2, 3)]


def local(
    tokens, norm_gain, w_query, w_key, w_value, w_out, kv_pool, block_table, prefix_len, write_slot
):
    groups = lax.axis_size("group")
    ranks = lax.axis_size("ctx")
    tp_size = lax.axis_size("tp")
    rank = lax.axis_index("ctx")
    group = lax.axis_index("group")
    core = lax.axis_index("tp") % 2
    plane = lax.axis_index("tp") // 2
    pool_size = kv_pool.shape[0]
    sessions, list_len = block_table.shape
    sess_here = sessions // groups
    per_pair = sess_here * list_len // (groups * ranks)
    new_len = tokens.shape[0] // sess_here
    head_dim = kv_pool.shape[4]
    const = head_dim**-0.5 * LOG2E
    device_id = group * ranks + rank
    pool = kv_pool.reshape(pool_size, 2, head_dim, head_dim)

    table = block_table.reshape(groups, sess_here * list_len)
    steps = jnp.arange(groups, dtype=jnp.int32)
    send_table = jnp.roll(table, -group, axis=0)
    here = send_table // pool_size == device_id
    upper = jnp.triu(jnp.ones((sess_here * list_len,) * 2, BF16))
    order = jnp.dot(here.astype(BF16), upper, preferred_element_type=F32).astype(jnp.int32)
    wanted = jnp.arange(1, per_pair + 1, dtype=jnp.int32)
    picked = here[:, None, :] & (order[:, None, :] == wanted[None, :, None])
    send_index = jnp.sum(jnp.where(picked, send_table[:, None, :] % pool_size, 0), axis=2)
    mine = lax.dynamic_index_in_dim(table, group, 0, keepdims=False).reshape(sess_here, list_len)
    lengths = lax.dynamic_slice_in_dim(prefix_len, group * sess_here, sess_here)
    source = ((group - steps) % groups) * ranks + rank
    from_there = mine[None] // pool_size == source[:, None, None]
    slots = jnp.arange(list_len, dtype=jnp.int32)
    keys_in = jnp.clip(lengths[:, None] - slots[None, :] * head_dim, 0, head_dim)
    live_keys = jnp.sum(jnp.where(from_there, keys_in[None], 0), axis=2)
    counts = jnp.sum(from_there.astype(jnp.int32), axis=2)
    starts = jnp.cumsum(counts, axis=1) - counts
    meta = jnp.stack([starts, live_keys], axis=2).reshape(groups, 2 * sess_here).astype(jnp.int32)

    rank_only = rank[None].astype(jnp.int32)
    begun = project(
        rank_only, jnp.stack([send_index[1], send_index[3]]), pool,
        tokens, norm_gain[None, :], w_query, w_key, w_value,
    )
    parts = begun[:ranks]
    near = [shifted(begun[ranks], "group", 1), shifted(begun[ranks + 1], "group", 3)]
    rest, _ = lax.optimization_barrier((jnp.stack([send_index[2], send_index[0]]), parts[0]))
    far, own_blocks, new_pool = pack(rest, pool)
    parts = [parts[0]] + [shifted(parts[step], "ctx", step) for step in (1, 3, 2)]
    parts, far, own_blocks = lax.optimization_barrier((parts, far, own_blocks))
    fresh = finish(parts, tokens.shape[1] * ranks)
    far, fresh = lax.optimization_barrier((far, fresh))
    far = shifted(far, "group", 2)
    quarters = around(fresh, "ctx")

    first_meta = jnp.concatenate([rank_only, meta[0]])
    queries, norms, *state, block = attend_own(
        first_meta, quarters, own_blocks, new_len, const
    )
    near_meta = jnp.concatenate([meta[1], meta[3]])
    state = attend_near(near_meta, queries, norms, state, near, new_len, const)
    last_meta = jnp.concatenate([meta[2], rank_only])
    partial = attend_last(last_meta, queries, norms, state, far, new_len, const)
    partial = [partial[0]] + [shifted(partial[step], "ctx", step) for step in (1, 2, 3)]
    attended = combine(partial)

    planes = tp_size // 2
    out_meta = jnp.stack([rank, core, plane]).astype(jnp.int32)
    news = around(block, "group")
    targets = jnp.roll(write_slot.reshape(groups, ranks)[::-1], group + 1, axis=0).reshape(-1)
    places = jnp.where(targets // pool_size == device_id, targets % pool_size, -1)
    own, send, new_pool = project_out(
        out_meta, places, around(attended, "ctx"), w_out, news, new_pool, planes
    )
    other = lax.ppermute(send, "tp", [(i, i ^ 1) for i in range(tp_size)])
    total = own[0] + other[0].astype(F32)
    for step in range(1, planes):
        pair = (own[step] + other[step].astype(F32)).astype(BF16)
        total = total + shifted(pair, "tp", 2 * step).astype(F32)
    return (total.astype(BF16), new_pool.reshape(kv_pool.shape))


def solution(mesh):
    placed = (
        P("group", "ctx"),
        P("ctx"),
        P("ctx", "tp"),
        P("ctx", "tp"),
        P("ctx", "tp"),
        P("tp", "ctx"),
        P(("group", "ctx"), None, "tp", None, None),
        P(),
        P(),
        P(),
    )
    return jax.shard_map(
        local,
        mesh=mesh,
        in_specs=placed,
        out_specs=(P("group", ("ctx", "tp")), P(("group", "ctx"), None, "tp", None, None)),
        check_vma=False,
    )
```

```python
import jax
import jax.numpy as jnp
from jax import lax
from jax.experimental import pallas as pl
from jax.experimental.pallas import tpu as pltpu
from jax.sharding import PartitionSpec as P

NEG_FILL = -1e30
LOG2E = 1.4426950408889634
F32 = jnp.float32
BF16 = jnp.bfloat16
VMEM_BYTES = 30 * 1024 * 1024
VMEM_MOST = 58 * 1024 * 1024
CHUNK = 4
TAIL = 2
ROOM = 60.0
NO_COST = pl.CostEstimate(flops=1, bytes_accessed=1, transcendentals=0)
CTX = 4
SEND = ((0, 1, 2, 3), (1, 0, 3, 2), (2, 3, 1, 0), (3, 2, 0, 1))
NT = (((1,), (1,)), ((), ()))


def params(size=VMEM_BYTES):
    return pltpu.CompilerParams(vmem_limit_bytes=size)


def vmem():
    return pl.BlockSpec(memory_space=pltpu.VMEM)


def smem():
    return pl.BlockSpec(memory_space=pltpu.SMEM)


def anywhere():
    return pl.BlockSpec(memory_space=pl.ANY)


def gather_blocks(index_ref, pool, held, outs, sems):
    copies = []
    for step in range(held.shape[0]):
        for n in range(held.shape[1]):
            held[step, n] = pool[index_ref[step, n]]
        copies.append(pltpu.make_async_copy(held.at[step], outs[step], sems.at[step]))
        copies[-1].start()
    return copies


def project_kernel(
    meta_ref, index_ref, pool_ref, tok_ref, gain_ref, wq_ref, wk_ref, wv_ref, *refs
):
    steps = index_ref.shape[0]
    out_refs, block_refs = refs[:CTX], refs[CTX : CTX + steps]
    pool, held, tok, wq, wkv, norm, total, in_sems, out_sems, block_sems = refs[CTX + steps :]
    rows, features = tok.shape
    q_cols = wq.shape[1]
    deep = features // 4
    part = rows // CTX
    rank = meta_ref[0]
    fetch_tok = pltpu.make_async_copy(tok_ref, tok, in_sems.at[0])
    fetch_w = [
        pltpu.make_async_copy(
            wq_ref.at[pl.ds(n * deep, deep)], wq.at[pl.ds(n * deep, deep)], in_sems.at[1 + n]
        )
        for n in range(4)
    ]
    fetch_kv = [
        pltpu.make_async_copy(ref, wkv.at[:, pl.ds(n * 128, 128)], in_sems.at[5 + n])
        for n, ref in enumerate((wk_ref, wv_ref))
    ]
    fetch_pool = pltpu.make_async_copy(pool_ref, pool, block_sems.at[steps])
    for copy in [fetch_pool, fetch_tok] + fetch_kv + fetch_w:
        copy.start()
    fetch_pool.wait()
    sent = gather_blocks(index_ref, pool, held, block_refs, block_sems)
    fetch_tok.wait()
    for first in range(0, rows, part):
        some = slice(first, first + part)
        wide = tok[some].astype(F32)
        norm[some] = (wide * gain_ref[...]).astype(BF16)
        squares = jnp.sum(wide * wide, axis=1, keepdims=True)
        total[some, q_cols + 256 :] = jnp.broadcast_to(squares, (part, 128))
    for copy in fetch_kv:
        copy.wait()
    total[:, q_cols : q_cols + 256] = jnp.dot(norm[...], wkv[...], preferred_element_type=F32)
    half = 2 * deep
    for n in range(2):
        fetch_w[2 * n].wait()
        fetch_w[2 * n + 1].wait()
        depth = slice(n * half, n * half + half)
        for first in range(0, q_cols, 256):
            cols = slice(first, first + 256)
            value = jnp.dot(norm[:, depth], wq[depth, cols], preferred_element_type=F32)
            if n == 0:
                total[:, cols] = value
            else:
                total[:, cols] += value
    copies = []
    for step in range(CTX):
        place = lax.rem(rank + step, CTX)
        source = total.at[pl.ds(pl.multiple_of(place * part, part), part)]
        copies.append(pltpu.make_async_copy(source, out_refs[step], out_sems.at[step]))
        copies[-1].start()
    for copy in sent + copies:
        copy.wait()


def project(meta, index, pool, tokens, gain, w_query, w_key, w_value):
    steps, count = index.shape
    block = pool.shape[1:]
    rows, features = tokens.shape
    q_cols = w_query.shape[1]
    cols = q_cols + 384
    return pl.pallas_call(
        project_kernel,
        out_shape=[jax.ShapeDtypeStruct((rows // CTX, cols), F32)] * CTX
        + [jax.ShapeDtypeStruct((count,) + block, BF16)] * steps,
        in_specs=[smem(), smem(), anywhere(), anywhere(), vmem()] + [anywhere()] * 3,
        out_specs=[anywhere()] * (CTX + steps),
        scratch_shapes=[
            pltpu.VMEM(pool.shape, BF16),
            pltpu.VMEM((steps, count) + block, BF16),
            pltpu.VMEM((rows, features), BF16),
            pltpu.VMEM((features, q_cols), BF16),
            pltpu.VMEM((features, 256), BF16),
            pltpu.VMEM((rows, features), BF16),
            pltpu.VMEM((rows, cols), F32),
            pltpu.SemaphoreType.DMA((7,)),
            pltpu.SemaphoreType.DMA((CTX,)),
            pltpu.SemaphoreType.DMA((steps + 1,)),
        ],
        compiler_params=params(VMEM_MOST),
        cost_estimate=NO_COST,
        name="project",
    )(meta, index, pool, tokens, gain, w_query, w_key, w_value)


def finish_kernel(features, *refs):
    part_refs, out_ref = refs[:CTX], refs[CTX]
    q_cols = out_ref.shape[1]
    total = part_refs[0][...]
    for ref in part_refs[1:]:
        total = total + ref[...]
    scale = lax.rsqrt(total[:, q_cols : q_cols + 1] / features + 1e-05)
    out_ref[...] = (total[:, :q_cols] * scale).astype(BF16)


def finish(parts, features):
    rows, cols = parts[0].shape
    return pl.pallas_call(
        lambda *refs: finish_kernel(features, *refs),
        out_shape=jax.ShapeDtypeStruct((rows, cols - 128), BF16),
        in_specs=[vmem()] * CTX,
        out_specs=vmem(),
        compiler_params=params(),
        cost_estimate=NO_COST,
        name="finish",
    )(*parts)


def pack_kernel(index_ref, pool_ref, *refs):
    steps = index_ref.shape[0]
    outs = refs[:steps]
    pool_out, pool, held, sems = refs[steps:]
    fetch = pltpu.make_async_copy(pool_ref, pool, sems.at[steps])
    fetch.start()
    fetch.wait()
    keep = pltpu.make_async_copy(pool, pool_out, sems.at[steps])
    keep.start()
    for copy in gather_blocks(index_ref, pool, held, outs, sems) + [keep]:
        copy.wait()


def pack(index, pool):
    steps, count = index.shape
    block = pool.shape[1:]
    return pl.pallas_call(
        pack_kernel,
        out_shape=[jax.ShapeDtypeStruct((count,) + block, BF16)] * steps
        + [jax.ShapeDtypeStruct(pool.shape, BF16)],
        in_specs=[smem(), anywhere()],
        out_specs=[anywhere()] * (steps + 1),
        scratch_shapes=[
            pltpu.VMEM(pool.shape, BF16),
            pltpu.VMEM((steps, count) + block, BF16),
            pltpu.SemaphoreType.DMA((steps + 1,)),
        ],
        compiler_params=params(VMEM_MOST),
        cost_estimate=NO_COST,
        name="pack",
    )(index, pool)


def pack_lanes(ref, rows):
    lane = lax.broadcasted_iota(jnp.int32, (ref.shape[1], 128), 1)[: ref[0, rows, :].shape[0]]
    packed = jnp.zeros(lane.shape, F32)
    for head in range(ref.shape[0]):
        packed = jnp.where(lane == head, ref[head, rows, :], packed)
    return packed


def sweep(q_ref, rows, heads, keys, finish_head):
    pending = None
    for head in range(heads):
        cols = slice(head * 128, head * 128 + 128)
        scores = lax.dot_general(q_ref[rows, cols], keys, NT, preferred_element_type=F32)
        if pending is not None:
            finish_head(*pending)
        pending = (head, cols, scores)
    finish_head(*pending)


def moving(q_ref, m_ref, l_ref, acc_ref, rows, keys, values_ext, mask, const, zero):
    def finish_head(head, cols, scores):
        scores = jnp.where(mask, scores, NEG_FILL)
        m_old = m_ref[head, rows, :]
        m_new = jnp.maximum(m_old, jnp.max(scores, axis=1, keepdims=True) * const)
        alpha = jnp.exp2(m_old - m_new)
        reps = scores.shape[1] // 128
        weights = jnp.exp2(scores * const - jnp.concatenate([m_new] * reps, axis=1))
        if zero:
            weights = jnp.where(mask, weights, 0.0)
        mixed = jnp.dot(weights.astype(BF16), values_ext, preferred_element_type=F32)
        m_ref[head, rows, :] = m_new
        l_ref[head, rows, :] = l_ref[head, rows, :] * alpha + mixed[:, 128:]
        acc_ref[rows, cols] = acc_ref[rows, cols] * alpha + mixed[:, :128]

    sweep(q_ref, rows, m_ref.shape[0], keys, finish_head)


def steady(q_ref, m_ref, l_ref, acc_ref, rows, keys, values_ext, mask, const):
    def finish_head(head, cols, scores):
        if mask is not None:
            scores = jnp.where(mask, scores, NEG_FILL)
        reps = scores.shape[1] // 128
        shift = jnp.concatenate([m_ref[head, rows, :]] * reps, axis=1)
        weights = jnp.exp2(scores * const - shift)
        mixed = jnp.dot(weights.astype(BF16), values_ext, preferred_element_type=F32)
        l_ref[head, rows, :] += mixed[:, 128:]
        acc_ref[rows, cols] += mixed[:, :128]

    sweep(q_ref, rows, m_ref.shape[0], keys, finish_head)


def prefix_part(meta_ref, base, q_ref, qn_ref, kv_ref, vx_ref, m_ref, l_ref, acc_ref, new_len, const):
    blocks = kv_ref.shape[0]
    state = (q_ref, m_ref, l_ref, acc_ref)
    all_keys = kv_ref[:, 0].reshape(blocks * 128, 128)
    vx_ref[:, :128] = kv_ref[:, 1].reshape(blocks * 128, 128)
    vx_ref[:, 128:] = jnp.ones((blocks * 128, 128), BF16)
    norms = jnp.dot(all_keys * all_keys, jnp.ones((128, 128), BF16), preferred_element_type=F32)
    reach = jnp.sqrt(jnp.max(norms)) * (1.05 * const)

    def session_body(session, carry):
        row0 = pl.multiple_of(session * new_len, new_len)
        rows = pl.ds(row0, new_len)
        first = meta_ref[base + 2 * session]
        keys_live = meta_ref[base + 2 * session + 1]
        high = first * 128 + keys_live
        total = (keys_live + 127) // 128

        def enough():
            room = qn_ref[rows, :] * reach - pack_lanes(m_ref, rows)
            return (jnp.max(room) <= ROOM).astype(jnp.int32)

        def piece(wanted, count, masked):
            span = count * 128
            begin = jnp.minimum(wanted, blocks - count)
            keys = kv_ref[pl.ds(begin, count), 0].reshape(span, 128)
            values_ext = vx_ref[pl.ds(pl.multiple_of(begin * 128, 128), span), :]
            if not masked:
                return keys, values_ext, None
            index = begin * 128 + lax.broadcasted_iota(jnp.int32, (1, span), 1)
            return keys, values_ext, (index >= wanted * 128) & (index < high)

        def slow_more(now):
            return (now[0] < total) & (now[1] == 0)

        def slow(now):
            moving(*state, rows, *piece(first + now[0], CHUNK, True), const, False)
            return now[0] + CHUNK, enough()

        done, _ = lax.while_loop(slow_more, slow, (0, enough()))
        full = jnp.maximum(keys_live - done * 128, 0) // (CHUNK * 128)

        def fast(step, carry):
            steady(*state, rows, *piece(first + done + step * CHUNK, CHUNK, False), const)
            return carry

        lax.fori_loop(0, full, fast, 0)
        done = done + full * CHUNK

        def tail(step, carry):
            steady(*state, rows, *piece(first + done + step * TAIL, TAIL, True), const)
            return carry

        lax.fori_loop(0, (jnp.maximum(total - done, 0) + TAIL - 1) // TAIL, tail, 0)
        return carry

    lax.fori_loop(0, q_ref.shape[0] // new_len, session_body, 0)


def first_kernel(
    new_len, const, meta_ref, a, b, c, d, buf,
    q_ref, qn_ref, acc_ref, mp_ref, lp_ref, new_ref, kv_ref, vx_ref, m_ref, l_ref, sem,
):
    fetch = pltpu.make_async_copy(buf, kv_ref, sem)
    fetch.start()
    tokens, q_cols = q_ref.shape
    part = a.shape[0]
    heads = m_ref.shape[0]
    rank = meta_ref[0]
    for step, ref in enumerate((a, b, c, d)):
        place = lax.rem(rank + CTX - step, CTX)
        q_ref[pl.ds(pl.multiple_of(place * part, part), part), :] = ref[:, :q_cols]
        new_ref[place, 0] = ref[:, q_cols : q_cols + 128]
        new_ref[place, 1] = ref[:, q_cols + 128 :]
    m_ref[...] = jnp.full(m_ref.shape, NEG_FILL, F32)
    l_ref[...] = jnp.zeros(l_ref.shape, F32)
    acc_ref[...] = jnp.zeros(acc_ref.shape, F32)
    lane = lax.broadcasted_iota(jnp.int32, (tokens, 128), 1)
    squares = jnp.zeros((tokens, 128), F32)
    for head in range(heads):
        wide = q_ref[:, head * 128 : head * 128 + 128].astype(F32)
        squares = jnp.where(lane == head, jnp.sum(wide * wide, axis=1, keepdims=True), squares)
    qn_ref[...] = jnp.sqrt(squares)
    keys = a[:, q_cols : q_cols + 128]
    values_ext = jnp.concatenate(
        [a[:, q_cols + 128 : q_cols + 256], jnp.ones((part, 128), BF16)], axis=1
    )
    per_session = new_len // part
    rows = pl.ds(pl.multiple_of(lax.div(rank, per_session) * new_len, new_len), new_len)
    offset = lax.rem(rank, per_session) * part
    token = lax.broadcasted_iota(jnp.int32, (new_len, part), 0)
    fresh = lax.broadcasted_iota(jnp.int32, (new_len, part), 1) + offset
    moving(q_ref, m_ref, l_ref, acc_ref, rows, keys, values_ext, fresh <= token, const, True)
    fetch.wait()
    prefix_part(
        meta_ref, 1, q_ref, qn_ref, kv_ref, vx_ref, m_ref, l_ref, acc_ref, new_len, const
    )
    mp_ref[...] = pack_lanes(m_ref, slice(None))
    lp_ref[...] = pack_lanes(l_ref, slice(None))


def load_state(mp_in, lp_in, m_ref, l_ref):
    shape = m_ref.shape[1:]
    for head in range(m_ref.shape[0]):
        m_ref[head] = jnp.broadcast_to(mp_in[:, head : head + 1], shape)
        l_ref[head] = jnp.broadcast_to(lp_in[:, head : head + 1], shape)


def sources(
    new_len, const, meta_ref, q_ref, qn_ref, bufs, acc_in, mp_in, lp_in,
    acc_ref, kv_ref, vx_ref, m_ref, l_ref, sems,
):
    copies = []
    for n, buf in enumerate(bufs):
        copies.append(pltpu.make_async_copy(buf, kv_ref.at[n], sems.at[n]))
        copies[-1].start()
    acc_ref[...] = acc_in[...]
    load_state(mp_in, lp_in, m_ref, l_ref)
    for n, copy in enumerate(copies):
        copy.wait()
        prefix_part(
            meta_ref, 4 * n, q_ref, qn_ref, kv_ref.at[n], vx_ref, m_ref, l_ref, acc_ref, new_len,
            const,
        )


def near_kernel(
    new_len, const, meta_ref, q_ref, qn_ref, acc_in, mp_in, lp_in, buf,
    acc_ref, mp_ref, lp_ref, kv_ref, vx_ref, m_ref, l_ref, sems,
):
    sources(
        new_len, const, meta_ref, q_ref, qn_ref, (buf,), acc_in, mp_in, lp_in,
        acc_ref, kv_ref, vx_ref, m_ref, l_ref, sems,
    )
    mp_ref[...] = pack_lanes(m_ref, slice(None))
    lp_ref[...] = pack_lanes(l_ref, slice(None))


def last_kernel(
    new_len, const, meta_ref, q_ref, qn_ref, acc_in, mp_in, lp_in, buf,
    out_a, out_b, out_c, out_d, acc_ref, kv_ref, vx_ref, m_ref, l_ref, sems,
):
    sources(
        new_len, const, meta_ref, q_ref, qn_ref, (buf,), acc_in, mp_in, lp_in,
        acc_ref, kv_ref, vx_ref, m_ref, l_ref, sems,
    )
    tokens = q_ref.shape[0]
    heads = m_ref.shape[0]
    part = tokens // CTX
    rank = meta_ref[4]
    row = lax.broadcasted_iota(jnp.int32, (16, heads * 128), 0)
    for step, out_ref in enumerate((out_a, out_b, out_c, out_d)):
        place = lax.rem(rank + step, CTX)
        rows = pl.ds(pl.multiple_of(place * part, part), part)
        for head in range(heads):
            cols = slice(head * 128, head * 128 + 128)
            total = l_ref[head, rows, :]
            empty = total == 0.0
            safe = jnp.where(empty, 1.0, total)
            out_ref[:part, cols] = (acc_ref[rows, cols] / safe).astype(BF16)
            m_ref[head, rows, :] = jnp.where(
                empty, NEG_FILL, m_ref[head, rows, :] + jnp.log2(safe)
            )
        turned = pack_lanes(m_ref, rows).T
        line = jnp.concatenate([turned[h : h + 1] for h in range(heads)], axis=1)
        high = line.astype(BF16).astype(F32)
        rest = line - high
        mid = rest.astype(BF16).astype(F32)
        low = rest - mid
        tile = jnp.where(row == 0, high, jnp.where(row == 1, mid, jnp.where(row == 2, low, 0.0)))
        out_ref[part : part + 16, :] = tile.astype(BF16)


def scratch(tokens, heads, blocks, lead=()):
    return [
        pltpu.VMEM(lead + (blocks, 2, 128, 128), BF16),
        pltpu.VMEM((blocks * 128, 256), BF16),
        pltpu.VMEM((heads, tokens, 128), F32),
        pltpu.VMEM((heads, tokens, 128), F32),
    ]


def state_shapes(tokens, q_cols):
    return [
        jax.ShapeDtypeStruct((tokens, q_cols), F32),
        jax.ShapeDtypeStruct((tokens, 128), F32),
        jax.ShapeDtypeStruct((tokens, 128), F32),
    ]


def attend_own(meta, quarters, buf, new_len, const):
    part = quarters[0].shape[0]
    q_cols = quarters[0].shape[1] - 256
    tokens = part * CTX
    heads = q_cols // 128
    blocks = buf.shape[0]
    return pl.pallas_call(
        lambda *refs: first_kernel(new_len, const, *refs),
        out_shape=[
            jax.ShapeDtypeStruct((tokens, q_cols), BF16),
            jax.ShapeDtypeStruct((tokens, 128), F32),
        ]
        + state_shapes(tokens, q_cols)
        + [jax.ShapeDtypeStruct((CTX, 2, part, 128), BF16)],
        in_specs=[smem()] + [vmem()] * 4 + [anywhere()],
        out_specs=[vmem()] * 6,
        scratch_shapes=scratch(tokens, heads, blocks) + [pltpu.SemaphoreType.DMA(())],
        compiler_params=params(),
        cost_estimate=NO_COST,
        name="attend_own",
    )(meta, *quarters, buf)


def attend_near(meta, queries, norms, state, bufs, new_len, const):
    tokens, q_cols = queries.shape
    heads = q_cols // 128
    blocks = bufs[0].shape[0]
    return pl.pallas_call(
        lambda *refs: near_kernel(new_len, const, *refs),
        out_shape=state_shapes(tokens, q_cols),
        in_specs=[smem()] + [vmem()] * 5 + [anywhere()] * len(bufs),
        out_specs=[vmem()] * 3,
        scratch_shapes=scratch(tokens, heads, blocks, (len(bufs),))
        + [pltpu.SemaphoreType.DMA((len(bufs),))],
        compiler_params=params(),
        cost_estimate=NO_COST,
        name="attend_near",
    )(meta, queries, norms, *state, *bufs)


def attend_last(meta, queries, norms, state, buf, new_len, const):
    tokens, q_cols = queries.shape
    heads = q_cols // 128
    blocks = buf.shape[0]
    pairs = blocks * 128 * tokens // 2 * heads
    return pl.pallas_call(
        lambda *refs: last_kernel(new_len, const, *refs),
        out_shape=[jax.ShapeDtypeStruct((tokens // CTX + 16, q_cols), BF16)] * CTX,
        in_specs=[smem()] + [vmem()] * 5 + [anywhere()],
        out_specs=[vmem()] * CTX,
        scratch_shapes=[pltpu.VMEM((tokens, q_cols), F32)]
        + scratch(tokens, heads, blocks, (1,))
        + [pltpu.SemaphoreType.DMA((1,))],
        compiler_params=params(),
        cost_estimate=pl.CostEstimate(
            flops=pairs * 512, bytes_accessed=8 << 20, transcendentals=pairs
        ),
        name="attend_last",
    )(meta, queries, norms, *state, buf)


def combine_kernel(*refs):
    in_refs, out_ref = refs[:CTX], refs[CTX]
    part, q_cols = out_ref.shape
    heads = q_cols // 128
    lines = []
    for c in range(CTX):
        tile = in_refs[c][part : part + 16, :].astype(F32)
        lines.append(tile[0:1] + tile[1:2] + tile[2:3])
    top = lines[0]
    for line in lines[1:]:
        top = jnp.maximum(top, line)
    shares = [jnp.exp2(line - top) for line in lines]
    total = shares[0] + shares[1] + shares[2] + shares[3]
    pieces = []
    for share in shares:
        share = share / total
        pieces += [share[:, h * 128 : h * 128 + 128] for h in range(heads)]
    pieces.append(jnp.zeros((128 - CTX * heads, 128), F32))
    turned = jnp.concatenate(pieces, axis=0).T
    for head in range(heads):
        cols = slice(head * 128, head * 128 + 128)
        mixed = jnp.zeros((part, 128), F32)
        for c in range(CTX):
            at = c * heads + head
            mixed = mixed + in_refs[c][:part, cols].astype(F32) * turned[:, at : at + 1]
        out_ref[:, cols] = mixed.astype(BF16)


def combine(arrived):
    rows, q_cols = arrived[0].shape
    return pl.pallas_call(
        combine_kernel,
        out_shape=jax.ShapeDtypeStruct((rows - 16, q_cols), BF16),
        in_specs=[vmem()] * CTX,
        out_specs=vmem(),
        compiler_params=params(),
        cost_estimate=NO_COST,
        name="combine",
    )(*arrived)


def out_kernel(
    meta_ref, place_ref, a, b, c, d, w_ref, new_a, new_b, new_c, new_d, pool_in,
    own_ref, send_ref, pool_out, rows_ref, sems,
):
    rank = meta_ref[0]
    core = meta_ref[1]
    part = a.shape[0]
    half = own_ref.shape[2]

    def place_blocks(act):
        count = new_a.shape[0]
        for n, ref in enumerate((new_a, new_b, new_c, new_d)):
            for i in range(count):
                at = n * count + i
                slot = place_ref[at]

                @pl.when(slot >= 0)
                def _(ref=ref, i=i, at=at, slot=slot):
                    act(pltpu.make_async_copy(ref.at[i], pool_out.at[slot], sems.at[at]))

    @pl.when(pl.program_id(0) == 0)
    def _():
        place_blocks(lambda copy: copy.start())
        for step, ref in enumerate((a, b, c, d)):
            place = lax.rem(rank + CTX - step, CTX)
            rows_ref[pl.ds(pl.multiple_of(place * part, part), part), :] = ref[...]

    product = jnp.dot(rows_ref[...], w_ref[...], preferred_element_type=F32)

    @pl.when(core == 0)
    def _():
        own_ref[0] = product[:, :half]
        send_ref[0] = product[:, half:].astype(BF16)

    @pl.when(core != 0)
    def _():
        own_ref[0] = product[:, half:]
        send_ref[0] = product[:, :half].astype(BF16)

    @pl.when(pl.program_id(0) == pl.num_programs(0) - 1)
    def _():
        place_blocks(lambda copy: copy.wait())


def project_out(meta, places, quarters, w_out, news, pool, planes):
    part, depth = quarters[0].shape
    tokens = part * CTX
    width = w_out.shape[1] // planes
    whole = pl.BlockSpec((part, depth), lambda i, *_: (0, 0))
    out = pl.BlockSpec((1, tokens, width // 2), lambda i, *_: (i, 0, 0))
    return pl.pallas_call(
        out_kernel,
        grid_spec=pltpu.PrefetchScalarGridSpec(
            num_scalar_prefetch=2,
            grid=(planes,),
            in_specs=[whole] * 4
            + [pl.BlockSpec((depth, width), lambda i, meta, _: (0, lax.rem(meta[2] + i, planes)))]
            + [anywhere()] * 5,
            out_specs=[out] * 2 + [anywhere()],
            scratch_shapes=[
                pltpu.VMEM((tokens, depth), BF16),
                pltpu.SemaphoreType.DMA((places.shape[0],)),
            ],
        ),
        out_shape=[
            jax.ShapeDtypeStruct((planes, tokens, width // 2), F32),
            jax.ShapeDtypeStruct((planes, tokens, width // 2), BF16),
            jax.ShapeDtypeStruct(pool.shape, BF16),
        ],
        input_output_aliases={11: 2},
        compiler_params=params(),
        cost_estimate=NO_COST,
        name="project_out",
    )(meta, places, *quarters, w_out, *news, pool)


def shifted(value, axis, step):
    size = lax.axis_size(axis)
    return lax.ppermute(value, axis, [(i, (i + step) % size) for i in range(size)])


def moved(value, step):
    return lax.ppermute(value, "group", list(enumerate(SEND[step])))


def around(value, axis):
    return [value] + [shifted(value, axis, step) for step in (1, 2, 3)]


def local(
    tokens, norm_gain, w_query, w_key, w_value, w_out, kv_pool, block_table, prefix_len, write_slot
):
    groups = lax.axis_size("group")
    ranks = lax.axis_size("ctx")
    tp_size = lax.axis_size("tp")
    rank = lax.axis_index("ctx")
    group = lax.axis_index("group")
    core = lax.axis_index("tp") % 2
    plane = lax.axis_index("tp") // 2
    pool_size = kv_pool.shape[0]
    sessions, list_len = block_table.shape
    sess_here = sessions // groups
    per_pair = sess_here * list_len // (groups * ranks)
    new_len = tokens.shape[0] // sess_here
    head_dim = kv_pool.shape[4]
    const = head_dim**-0.5 * LOG2E
    device_id = group * ranks + rank
    pool = kv_pool.reshape(pool_size, 2, head_dim, head_dim)

    table = block_table.reshape(groups, sess_here * list_len)
    send_to = jnp.array(SEND, jnp.int32)
    receive = jnp.array([[line.index(g) for g in range(groups)] for line in SEND], jnp.int32)
    send_table = table[lax.dynamic_index_in_dim(send_to, group, 1, keepdims=False)]
    here = send_table // pool_size == device_id
    upper = jnp.triu(jnp.ones((sess_here * list_len,) * 2, BF16))
    order = jnp.dot(here.astype(BF16), upper, preferred_element_type=F32).astype(jnp.int32)
    wanted = jnp.arange(1, per_pair + 1, dtype=jnp.int32)
    picked = here[:, None, :] & (order[:, None, :] == wanted[None, :, None])
    send_index = jnp.sum(jnp.where(picked, send_table[:, None, :] % pool_size, 0), axis=2)
    mine = lax.dynamic_index_in_dim(table, group, 0, keepdims=False).reshape(sess_here, list_len)
    lengths = lax.dynamic_slice_in_dim(prefix_len, group * sess_here, sess_here)
    source = lax.dynamic_index_in_dim(receive, group, 1, keepdims=False) * ranks + rank
    from_there = mine[None] // pool_size == source[:, None, None]
    slots = jnp.arange(list_len, dtype=jnp.int32)
    keys_in = jnp.clip(lengths[:, None] - slots[None, :] * head_dim, 0, head_dim)
    live_keys = jnp.sum(jnp.where(from_there, keys_in[None], 0), axis=2)
    counts = jnp.sum(from_there.astype(jnp.int32), axis=2)
    starts = jnp.cumsum(counts, axis=1) - counts
    meta = jnp.stack([starts, live_keys], axis=2).reshape(groups, 2 * sess_here).astype(jnp.int32)

    rank_only = rank[None].astype(jnp.int32)
    begun = project(
        rank_only, send_index[1:3], pool,
        tokens, norm_gain[None, :], w_query, w_key, w_value,
    )
    parts = begun[:ranks]
    early = [moved(begun[ranks], 1), moved(begun[ranks + 1], 2)]
    rest, _ = lax.optimization_barrier((jnp.stack([send_index[3], send_index[0]]), parts[0]))
    far, own_blocks, new_pool = pack(rest, pool)
    parts = [parts[0]] + [shifted(parts[step], "ctx", step) for step in (1, 3, 2)]
    parts, far, own_blocks = lax.optimization_barrier((parts, far, own_blocks))
    fresh = finish(parts, tokens.shape[1] * ranks)
    far, fresh = lax.optimization_barrier((far, fresh))
    far = moved(far, 3)
    quarters = around(fresh, "ctx")

    first_meta = jnp.concatenate([rank_only, meta[0]])
    queries, norms, *state, block = attend_own(
        first_meta, quarters, own_blocks, new_len, const
    )
    for step in (1, 2):
        state = attend_near(
            meta[step], queries, norms, state, [early[step - 1]], new_len, const
        )
    last_meta = jnp.concatenate([meta[3], rank_only])
    partial = attend_last(last_meta, queries, norms, state, far, new_len, const)
    partial = [partial[0]] + [shifted(partial[step], "ctx", step) for step in (1, 2, 3)]
    attended = combine(partial)

    planes = tp_size // 2
    out_meta = jnp.stack([rank, core, plane]).astype(jnp.int32)
    news = around(block, "group")
    targets = jnp.roll(write_slot.reshape(groups, ranks)[::-1], group + 1, axis=0).reshape(-1)
    places = jnp.where(targets // pool_size == device_id, targets % pool_size, -1)
    own, send, new_pool = project_out(
        out_meta, places, around(attended, "ctx"), w_out, news, new_pool, planes
    )
    other = lax.ppermute(send, "tp", [(i, i ^ 1) for i in range(tp_size)])
    total = own[0] + other[0].astype(F32)
    for step in range(1, planes):
        pair = (own[step] + other[step].astype(F32)).astype(BF16)
        total = total + shifted(pair, "tp", 2 * step).astype(F32)
    return (total.astype(BF16), new_pool.reshape(kv_pool.shape))


def solution(mesh):
    placed = (
        P("group", "ctx"),
        P("ctx"),
        P("ctx", "tp"),
        P("ctx", "tp"),
        P("ctx", "tp"),
        P("tp", "ctx"),
        P(("group", "ctx"), None, "tp", None, None),
        P(),
        P(),
        P(),
    )
    return jax.shard_map(
        local,
        mesh=mesh,
        in_specs=placed,
        out_specs=(P("group", ("ctx", "tp")), P(("group", "ctx"), None, "tp", None, None)),
        check_vma=False,
    )
```

```python
import jax
import jax.numpy as jnp
from jax import lax
from jax.experimental import pallas as pl
from jax.experimental.pallas import tpu as pltpu
from jax.sharding import PartitionSpec as P

NEG_FILL = -1e30
LOG2E = 1.4426950408889634
F32 = jnp.float32
BF16 = jnp.bfloat16
VMEM_BYTES = 30 * 1024 * 1024
VMEM_MOST = 58 * 1024 * 1024
CHUNK = 4
TAIL = 2
ROOM = 60.0
NO_COST = pl.CostEstimate(flops=1, bytes_accessed=1, transcendentals=0)
CTX = 4
NT = (((1,), (1,)), ((), ()))


def params(size=VMEM_BYTES):
    return pltpu.CompilerParams(vmem_limit_bytes=size)


def vmem():
    return pl.BlockSpec(memory_space=pltpu.VMEM)


def smem():
    return pl.BlockSpec(memory_space=pltpu.SMEM)


def anywhere():
    return pl.BlockSpec(memory_space=pl.ANY)


def gather_blocks(index_ref, pool, held, outs, sems):
    copies = []
    for step in range(held.shape[0]):
        for n in range(held.shape[1]):
            held[step, n] = pool[index_ref[step, n]]
        copies.append(pltpu.make_async_copy(held.at[step], outs[step], sems.at[step]))
        copies[-1].start()
    return copies


def project_kernel(
    meta_ref, index_ref, pool_ref, tok_ref, gain_ref, wq_ref, wk_ref, wv_ref, *refs
):
    steps = index_ref.shape[0]
    out_refs, block_refs = refs[:CTX], refs[CTX : CTX + steps]
    pool, held, tok, wq, wkv, norm, total, in_sems, out_sems, block_sems = refs[CTX + steps :]
    rows, features = tok.shape
    q_cols = wq.shape[1]
    deep = features // 4
    part = rows // CTX
    rank = meta_ref[0]
    fetch_tok = pltpu.make_async_copy(tok_ref, tok, in_sems.at[0])
    fetch_w = [
        pltpu.make_async_copy(
            wq_ref.at[pl.ds(n * deep, deep)], wq.at[pl.ds(n * deep, deep)], in_sems.at[1 + n]
        )
        for n in range(4)
    ]
    fetch_kv = [
        pltpu.make_async_copy(ref, wkv.at[:, pl.ds(n * 128, 128)], in_sems.at[5 + n])
        for n, ref in enumerate((wk_ref, wv_ref))
    ]
    fetch_pool = pltpu.make_async_copy(pool_ref, pool, block_sems.at[steps])
    for copy in [fetch_pool, fetch_tok] + fetch_kv + fetch_w:
        copy.start()
    fetch_pool.wait()
    sent = gather_blocks(index_ref, pool, held, block_refs, block_sems)
    fetch_tok.wait()
    for first in range(0, rows, part):
        some = slice(first, first + part)
        wide = tok[some].astype(F32)
        norm[some] = (wide * gain_ref[...]).astype(BF16)
        squares = jnp.sum(wide * wide, axis=1, keepdims=True)
        total[some, q_cols + 256 :] = jnp.broadcast_to(squares, (part, 128))
    for copy in fetch_kv:
        copy.wait()
    total[:, q_cols : q_cols + 256] = jnp.dot(norm[...], wkv[...], preferred_element_type=F32)
    half = 2 * deep
    for n in range(2):
        fetch_w[2 * n].wait()
        fetch_w[2 * n + 1].wait()
        depth = slice(n * half, n * half + half)
        for first in range(0, q_cols, 256):
            cols = slice(first, first + 256)
            value = jnp.dot(norm[:, depth], wq[depth, cols], preferred_element_type=F32)
            if n == 0:
                total[:, cols] = value
            else:
                total[:, cols] += value
    copies = []
    for step in range(CTX):
        place = lax.rem(rank + step, CTX)
        source = total.at[pl.ds(pl.multiple_of(place * part, part), part)]
        copies.append(pltpu.make_async_copy(source, out_refs[step], out_sems.at[step]))
        copies[-1].start()
    for copy in sent + copies:
        copy.wait()


def project(meta, index, pool, tokens, gain, w_query, w_key, w_value):
    steps, count = index.shape
    block = pool.shape[1:]
    rows, features = tokens.shape
    q_cols = w_query.shape[1]
    cols = q_cols + 384
    return pl.pallas_call(
        project_kernel,
        out_shape=[jax.ShapeDtypeStruct((rows // CTX, cols), F32)] * CTX
        + [jax.ShapeDtypeStruct((count,) + block, BF16)] * steps,
        in_specs=[smem(), smem(), anywhere(), anywhere(), vmem()] + [anywhere()] * 3,
        out_specs=[anywhere()] * (CTX + steps),
        scratch_shapes=[
            pltpu.VMEM(pool.shape, BF16),
            pltpu.VMEM((steps, count) + block, BF16),
            pltpu.VMEM((rows, features), BF16),
            pltpu.VMEM((features, q_cols), BF16),
            pltpu.VMEM((features, 256), BF16),
            pltpu.VMEM((rows, features), BF16),
            pltpu.VMEM((rows, cols), F32),
            pltpu.SemaphoreType.DMA((7,)),
            pltpu.SemaphoreType.DMA((CTX,)),
            pltpu.SemaphoreType.DMA((steps + 1,)),
        ],
        compiler_params=params(VMEM_MOST),
        cost_estimate=NO_COST,
        name="project",
    )(meta, index, pool, tokens, gain, w_query, w_key, w_value)


def finish_kernel(features, *refs):
    part_refs, out_ref = refs[:CTX], refs[CTX]
    q_cols = out_ref.shape[1]
    total = part_refs[0][...]
    for ref in part_refs[1:]:
        total = total + ref[...]
    scale = lax.rsqrt(total[:, q_cols : q_cols + 1] / features + 1e-05)
    out_ref[...] = (total[:, :q_cols] * scale).astype(BF16)


def finish(parts, features):
    rows, cols = parts[0].shape
    return pl.pallas_call(
        lambda *refs: finish_kernel(features, *refs),
        out_shape=jax.ShapeDtypeStruct((rows, cols - 128), BF16),
        in_specs=[vmem()] * CTX,
        out_specs=vmem(),
        compiler_params=params(),
        cost_estimate=NO_COST,
        name="finish",
    )(*parts)


def pack_kernel(index_ref, pool_ref, *refs):
    steps = index_ref.shape[0]
    outs = refs[:steps]
    pool_out, pool, held, sems = refs[steps:]
    fetch = pltpu.make_async_copy(pool_ref, pool, sems.at[steps])
    fetch.start()
    fetch.wait()
    keep = pltpu.make_async_copy(pool, pool_out, sems.at[steps])
    keep.start()
    for copy in gather_blocks(index_ref, pool, held, outs, sems) + [keep]:
        copy.wait()


def pack(index, pool):
    steps, count = index.shape
    block = pool.shape[1:]
    return pl.pallas_call(
        pack_kernel,
        out_shape=[jax.ShapeDtypeStruct((count,) + block, BF16)] * steps
        + [jax.ShapeDtypeStruct(pool.shape, BF16)],
        in_specs=[smem(), anywhere()],
        out_specs=[anywhere()] * (steps + 1),
        scratch_shapes=[
            pltpu.VMEM(pool.shape, BF16),
            pltpu.VMEM((steps, count) + block, BF16),
            pltpu.SemaphoreType.DMA((steps + 1,)),
        ],
        compiler_params=params(VMEM_MOST),
        cost_estimate=NO_COST,
        name="pack",
    )(index, pool)


def pack_lanes(ref, rows):
    lane = lax.broadcasted_iota(jnp.int32, (ref.shape[1], 128), 1)[: ref[0, rows, :].shape[0]]
    packed = jnp.zeros(lane.shape, F32)
    for head in range(ref.shape[0]):
        packed = jnp.where(lane == head, ref[head, rows, :], packed)
    return packed


def sweep(q_ref, rows, heads, keys, finish_head):
    pending = None
    for head in range(heads):
        cols = slice(head * 128, head * 128 + 128)
        scores = lax.dot_general(q_ref[rows, cols], keys, NT, preferred_element_type=F32)
        if pending is not None:
            finish_head(*pending)
        pending = (head, cols, scores)
    finish_head(*pending)


def moving(q_ref, m_ref, l_ref, acc_ref, rows, keys, values_ext, mask, const, zero):
    def finish_head(head, cols, scores):
        scores = jnp.where(mask, scores, NEG_FILL)
        m_old = m_ref[head, rows, :]
        m_new = jnp.maximum(m_old, jnp.max(scores, axis=1, keepdims=True) * const)
        alpha = jnp.exp2(m_old - m_new)
        reps = scores.shape[1] // 128
        weights = jnp.exp2(scores * const - jnp.concatenate([m_new] * reps, axis=1))
        if zero:
            weights = jnp.where(mask, weights, 0.0)
        mixed = jnp.dot(weights.astype(BF16), values_ext, preferred_element_type=F32)
        m_ref[head, rows, :] = m_new
        l_ref[head, rows, :] = l_ref[head, rows, :] * alpha + mixed[:, 128:]
        acc_ref[rows, cols] = acc_ref[rows, cols] * alpha + mixed[:, :128]

    sweep(q_ref, rows, m_ref.shape[0], keys, finish_head)


def steady(q_ref, m_ref, l_ref, acc_ref, rows, keys, values_ext, mask, const):
    def finish_head(head, cols, scores):
        if mask is not None:
            scores = jnp.where(mask, scores, NEG_FILL)
        reps = scores.shape[1] // 128
        shift = jnp.concatenate([m_ref[head, rows, :]] * reps, axis=1)
        weights = jnp.exp2(scores * const - shift)
        mixed = jnp.dot(weights.astype(BF16), values_ext, preferred_element_type=F32)
        l_ref[head, rows, :] += mixed[:, 128:]
        acc_ref[rows, cols] += mixed[:, :128]

    sweep(q_ref, rows, m_ref.shape[0], keys, finish_head)


def prefix_part(meta_ref, base, q_ref, qn_ref, kv_ref, vx_ref, m_ref, l_ref, acc_ref, new_len, const):
    blocks = kv_ref.shape[0]
    state = (q_ref, m_ref, l_ref, acc_ref)
    all_keys = kv_ref[:, 0].reshape(blocks * 128, 128)
    vx_ref[:, :128] = kv_ref[:, 1].reshape(blocks * 128, 128)
    vx_ref[:, 128:] = jnp.ones((blocks * 128, 128), BF16)
    norms = jnp.dot(all_keys * all_keys, jnp.ones((128, 128), BF16), preferred_element_type=F32)
    reach = jnp.sqrt(jnp.max(norms)) * (1.05 * const)

    def session_body(session, carry):
        row0 = pl.multiple_of(session * new_len, new_len)
        rows = pl.ds(row0, new_len)
        first = meta_ref[base + 2 * session]
        keys_live = meta_ref[base + 2 * session + 1]
        high = first * 128 + keys_live
        total = (keys_live + 127) // 128

        def enough():
            room = qn_ref[rows, :] * reach - pack_lanes(m_ref, rows)
            return (jnp.max(room) <= ROOM).astype(jnp.int32)

        def piece(wanted, count, masked):
            span = count * 128
            begin = jnp.minimum(wanted, blocks - count)
            keys = kv_ref[pl.ds(begin, count), 0].reshape(span, 128)
            values_ext = vx_ref[pl.ds(pl.multiple_of(begin * 128, 128), span), :]
            if not masked:
                return keys, values_ext, None
            index = begin * 128 + lax.broadcasted_iota(jnp.int32, (1, span), 1)
            return keys, values_ext, (index >= wanted * 128) & (index < high)

        def slow_more(now):
            return (now[0] < total) & (now[1] == 0)

        def slow(now):
            moving(*state, rows, *piece(first + now[0], CHUNK, True), const, False)
            return now[0] + CHUNK, enough()

        done, _ = lax.while_loop(slow_more, slow, (0, enough()))
        full = jnp.maximum(keys_live - done * 128, 0) // (CHUNK * 128)

        def fast(step, carry):
            steady(*state, rows, *piece(first + done + step * CHUNK, CHUNK, False), const)
            return carry

        lax.fori_loop(0, full, fast, 0)
        done = done + full * CHUNK

        def tail(step, carry):
            steady(*state, rows, *piece(first + done + step * TAIL, TAIL, True), const)
            return carry

        lax.fori_loop(0, (jnp.maximum(total - done, 0) + TAIL - 1) // TAIL, tail, 0)
        return carry

    lax.fori_loop(0, q_ref.shape[0] // new_len, session_body, 0)


def first_kernel(
    new_len, const, meta_ref, a, b, c, d, buf,
    q_ref, qn_ref, acc_ref, mp_ref, lp_ref, new_ref, kv_ref, vx_ref, m_ref, l_ref, sem,
):
    fetch = pltpu.make_async_copy(buf, kv_ref, sem)
    fetch.start()
    tokens, q_cols = q_ref.shape
    part = a.shape[0]
    heads = m_ref.shape[0]
    rank = meta_ref[0]
    for step, ref in enumerate((a, b, c, d)):
        place = lax.rem(rank + CTX - step, CTX)
        q_ref[pl.ds(pl.multiple_of(place * part, part), part), :] = ref[:, :q_cols]
        new_ref[place, 0] = ref[:, q_cols : q_cols + 128]
        new_ref[place, 1] = ref[:, q_cols + 128 :]
    m_ref[...] = jnp.full(m_ref.shape, NEG_FILL, F32)
    l_ref[...] = jnp.zeros(l_ref.shape, F32)
    acc_ref[...] = jnp.zeros(acc_ref.shape, F32)
    lane = lax.broadcasted_iota(jnp.int32, (tokens, 128), 1)
    squares = jnp.zeros((tokens, 128), F32)
    for head in range(heads):
        wide = q_ref[:, head * 128 : head * 128 + 128].astype(F32)
        squares = jnp.where(lane == head, jnp.sum(wide * wide, axis=1, keepdims=True), squares)
    qn_ref[...] = jnp.sqrt(squares)
    keys = a[:, q_cols : q_cols + 128]
    values_ext = jnp.concatenate(
        [a[:, q_cols + 128 : q_cols + 256], jnp.ones((part, 128), BF16)], axis=1
    )
    per_session = new_len // part
    rows = pl.ds(pl.multiple_of(lax.div(rank, per_session) * new_len, new_len), new_len)
    offset = lax.rem(rank, per_session) * part
    token = lax.broadcasted_iota(jnp.int32, (new_len, part), 0)
    fresh = lax.broadcasted_iota(jnp.int32, (new_len, part), 1) + offset
    moving(q_ref, m_ref, l_ref, acc_ref, rows, keys, values_ext, fresh <= token, const, True)
    fetch.wait()
    prefix_part(
        meta_ref, 1, q_ref, qn_ref, kv_ref, vx_ref, m_ref, l_ref, acc_ref, new_len, const
    )
    mp_ref[...] = pack_lanes(m_ref, slice(None))
    lp_ref[...] = pack_lanes(l_ref, slice(None))


def load_state(mp_in, lp_in, m_ref, l_ref):
    shape = m_ref.shape[1:]
    for head in range(m_ref.shape[0]):
        m_ref[head] = jnp.broadcast_to(mp_in[:, head : head + 1], shape)
        l_ref[head] = jnp.broadcast_to(lp_in[:, head : head + 1], shape)


def sources(
    new_len, const, meta_ref, q_ref, qn_ref, bufs, acc_in, mp_in, lp_in,
    acc_ref, kv_ref, vx_ref, m_ref, l_ref, sems,
):
    copies = []
    for n, buf in enumerate(bufs):
        copies.append(pltpu.make_async_copy(buf, kv_ref.at[n], sems.at[n]))
        copies[-1].start()
    acc_ref[...] = acc_in[...]
    load_state(mp_in, lp_in, m_ref, l_ref)
    for n, copy in enumerate(copies):
        copy.wait()
        prefix_part(
            meta_ref, 4 * n, q_ref, qn_ref, kv_ref.at[n], vx_ref, m_ref, l_ref, acc_ref, new_len,
            const,
        )


def near_kernel(
    new_len, const, meta_ref, q_ref, qn_ref, acc_in, mp_in, lp_in, buf_a, buf_b,
    acc_ref, mp_ref, lp_ref, kv_ref, vx_ref, m_ref, l_ref, sems,
):
    sources(
        new_len, const, meta_ref, q_ref, qn_ref, (buf_a, buf_b), acc_in, mp_in, lp_in,
        acc_ref, kv_ref, vx_ref, m_ref, l_ref, sems,
    )
    mp_ref[...] = pack_lanes(m_ref, slice(None))
    lp_ref[...] = pack_lanes(l_ref, slice(None))


def last_kernel(
    new_len, const, meta_ref, q_ref, qn_ref, acc_in, mp_in, lp_in, buf,
    out_a, out_b, out_c, out_d, acc_ref, kv_ref, vx_ref, m_ref, l_ref, sems,
):
    sources(
        new_len, const, meta_ref, q_ref, qn_ref, (buf,), acc_in, mp_in, lp_in,
        acc_ref, kv_ref, vx_ref, m_ref, l_ref, sems,
    )
    tokens = q_ref.shape[0]
    heads = m_ref.shape[0]
    part = tokens // CTX
    rank = meta_ref[4]
    row = lax.broadcasted_iota(jnp.int32, (16, heads * 128), 0)
    for step, out_ref in enumerate((out_a, out_b, out_c, out_d)):
        place = lax.rem(rank + step, CTX)
        rows = pl.ds(pl.multiple_of(place * part, part), part)
        for head in range(heads):
            cols = slice(head * 128, head * 128 + 128)
            total = l_ref[head, rows, :]
            empty = total == 0.0
            safe = jnp.where(empty, 1.0, total)
            out_ref[:part, cols] = (acc_ref[rows, cols] / safe).astype(BF16)
            m_ref[head, rows, :] = jnp.where(
                empty, NEG_FILL, m_ref[head, rows, :] + jnp.log2(safe)
            )
        turned = pack_lanes(m_ref, rows).T
        line = jnp.concatenate([turned[h : h + 1] for h in range(heads)], axis=1)
        high = line.astype(BF16).astype(F32)
        rest = line - high
        mid = rest.astype(BF16).astype(F32)
        low = rest - mid
        tile = jnp.where(row == 0, high, jnp.where(row == 1, mid, jnp.where(row == 2, low, 0.0)))
        out_ref[part : part + 16, :] = tile.astype(BF16)


def scratch(tokens, heads, blocks, lead=()):
    return [
        pltpu.VMEM(lead + (blocks, 2, 128, 128), BF16),
        pltpu.VMEM((blocks * 128, 256), BF16),
        pltpu.VMEM((heads, tokens, 128), F32),
        pltpu.VMEM((heads, tokens, 128), F32),
    ]


def state_shapes(tokens, q_cols):
    return [
        jax.ShapeDtypeStruct((tokens, q_cols), F32),
        jax.ShapeDtypeStruct((tokens, 128), F32),
        jax.ShapeDtypeStruct((tokens, 128), F32),
    ]


def attend_own(meta, quarters, buf, new_len, const):
    part = quarters[0].shape[0]
    q_cols = quarters[0].shape[1] - 256
    tokens = part * CTX
    heads = q_cols // 128
    blocks = buf.shape[0]
    return pl.pallas_call(
        lambda *refs: first_kernel(new_len, const, *refs),
        out_shape=[
            jax.ShapeDtypeStruct((tokens, q_cols), BF16),
            jax.ShapeDtypeStruct((tokens, 128), F32),
        ]
        + state_shapes(tokens, q_cols)
        + [jax.ShapeDtypeStruct((CTX, 2, part, 128), BF16)],
        in_specs=[smem()] + [vmem()] * 4 + [anywhere()],
        out_specs=[vmem()] * 6,
        scratch_shapes=scratch(tokens, heads, blocks) + [pltpu.SemaphoreType.DMA(())],
        compiler_params=params(),
        cost_estimate=NO_COST,
        name="attend_own",
    )(meta, *quarters, buf)


def attend_near(meta, queries, norms, state, bufs, new_len, const):
    tokens, q_cols = queries.shape
    heads = q_cols // 128
    blocks = bufs[0].shape[0]
    return pl.pallas_call(
        lambda *refs: near_kernel(new_len, const, *refs),
        out_shape=state_shapes(tokens, q_cols),
        in_specs=[smem()] + [vmem()] * 5 + [anywhere()] * 2,
        out_specs=[vmem()] * 3,
        scratch_shapes=scratch(tokens, heads, blocks, (2,))
        + [pltpu.SemaphoreType.DMA((2,))],
        compiler_params=params(),
        cost_estimate=NO_COST,
        name="attend_near",
    )(meta, queries, norms, *state, *bufs)


def attend_last(meta, queries, norms, state, buf, new_len, const):
    tokens, q_cols = queries.shape
    heads = q_cols // 128
    blocks = buf.shape[0]
    pairs = blocks * 128 * tokens // 2 * heads
    return pl.pallas_call(
        lambda *refs: last_kernel(new_len, const, *refs),
        out_shape=[jax.ShapeDtypeStruct((tokens // CTX + 16, q_cols), BF16)] * CTX,
        in_specs=[smem()] + [vmem()] * 5 + [anywhere()],
        out_specs=[vmem()] * CTX,
        scratch_shapes=[pltpu.VMEM((tokens, q_cols), F32)]
        + scratch(tokens, heads, blocks, (1,))
        + [pltpu.SemaphoreType.DMA((1,))],
        compiler_params=params(),
        cost_estimate=pl.CostEstimate(
            flops=pairs * 512, bytes_accessed=8 << 20, transcendentals=pairs
        ),
        name="attend_last",
    )(meta, queries, norms, *state, buf)


def combine_kernel(*refs):
    in_refs, out_ref = refs[:CTX], refs[CTX]
    part, q_cols = out_ref.shape
    heads = q_cols // 128
    lines = []
    for c in range(CTX):
        tile = in_refs[c][part : part + 16, :].astype(F32)
        lines.append(tile[0:1] + tile[1:2] + tile[2:3])
    top = lines[0]
    for line in lines[1:]:
        top = jnp.maximum(top, line)
    shares = [jnp.exp2(line - top) for line in lines]
    total = shares[0] + shares[1] + shares[2] + shares[3]
    pieces = []
    for share in shares:
        share = share / total
        pieces += [share[:, h * 128 : h * 128 + 128] for h in range(heads)]
    pieces.append(jnp.zeros((128 - CTX * heads, 128), F32))
    turned = jnp.concatenate(pieces, axis=0).T
    for head in range(heads):
        cols = slice(head * 128, head * 128 + 128)
        mixed = jnp.zeros((part, 128), F32)
        for c in range(CTX):
            at = c * heads + head
            mixed = mixed + in_refs[c][:part, cols].astype(F32) * turned[:, at : at + 1]
        out_ref[:, cols] = mixed.astype(BF16)


def combine(arrived):
    rows, q_cols = arrived[0].shape
    return pl.pallas_call(
        combine_kernel,
        out_shape=jax.ShapeDtypeStruct((rows - 16, q_cols), BF16),
        in_specs=[vmem()] * CTX,
        out_specs=vmem(),
        compiler_params=params(),
        cost_estimate=NO_COST,
        name="combine",
    )(*arrived)


def out_kernel(
    meta_ref, place_ref, a, b, c, d, w_ref, new_a, new_b, new_c, new_d, pool_in,
    own_ref, send_ref, pool_out, rows_ref, sems,
):
    rank = meta_ref[0]
    core = meta_ref[1]
    part = a.shape[0]
    half = own_ref.shape[2]

    def place_blocks(act):
        count = new_a.shape[0]
        for n, ref in enumerate((new_a, new_b, new_c, new_d)):
            for i in range(count):
                at = n * count + i
                slot = place_ref[at]

                @pl.when(slot >= 0)
                def _(ref=ref, i=i, at=at, slot=slot):
                    act(pltpu.make_async_copy(ref.at[i], pool_out.at[slot], sems.at[at]))

    @pl.when(pl.program_id(0) == 0)
    def _():
        place_blocks(lambda copy: copy.start())
        for step, ref in enumerate((a, b, c, d)):
            place = lax.rem(rank + CTX - step, CTX)
            rows_ref[pl.ds(pl.multiple_of(place * part, part), part), :] = ref[...]

    product = jnp.dot(rows_ref[...], w_ref[...], preferred_element_type=F32)

    @pl.when(core == 0)
    def _():
        own_ref[0] = product[:, :half]
        send_ref[0] = product[:, half:].astype(BF16)

    @pl.when(core != 0)
    def _():
        own_ref[0] = product[:, half:]
        send_ref[0] = product[:, :half].astype(BF16)

    @pl.when(pl.program_id(0) == pl.num_programs(0) - 1)
    def _():
        place_blocks(lambda copy: copy.wait())


def project_out(meta, places, quarters, w_out, news, pool, planes):
    part, depth = quarters[0].shape
    tokens = part * CTX
    width = w_out.shape[1] // planes
    whole = pl.BlockSpec((part, depth), lambda i, *_: (0, 0))
    out = pl.BlockSpec((1, tokens, width // 2), lambda i, *_: (i, 0, 0))
    return pl.pallas_call(
        out_kernel,
        grid_spec=pltpu.PrefetchScalarGridSpec(
            num_scalar_prefetch=2,
            grid=(planes,),
            in_specs=[whole] * 4
            + [pl.BlockSpec((depth, width), lambda i, meta, _: (0, lax.rem(meta[2] + i, planes)))]
            + [anywhere()] * 5,
            out_specs=[out] * 2 + [anywhere()],
            scratch_shapes=[
                pltpu.VMEM((tokens, depth), BF16),
                pltpu.SemaphoreType.DMA((places.shape[0],)),
            ],
        ),
        out_shape=[
            jax.ShapeDtypeStruct((planes, tokens, width // 2), F32),
            jax.ShapeDtypeStruct((planes, tokens, width // 2), BF16),
            jax.ShapeDtypeStruct(pool.shape, BF16),
        ],
        input_output_aliases={11: 2},
        compiler_params=params(),
        cost_estimate=NO_COST,
        name="project_out",
    )(meta, places, *quarters, w_out, *news, pool)


def shifted(value, axis, step):
    size = lax.axis_size(axis)
    return lax.ppermute(value, axis, [(i, (i + step) % size) for i in range(size)])


def around(value, axis):
    return [value] + [shifted(value, axis, step) for step in (1, 2, 3)]


def local(
    tokens, norm_gain, w_query, w_key, w_value, w_out, kv_pool, block_table, prefix_len, write_slot
):
    groups = lax.axis_size("group")
    ranks = lax.axis_size("ctx")
    tp_size = lax.axis_size("tp")
    rank = lax.axis_index("ctx")
    group = lax.axis_index("group")
    core = lax.axis_index("tp") % 2
    plane = lax.axis_index("tp") // 2
    pool_size = kv_pool.shape[0]
    sessions, list_len = block_table.shape
    sess_here = sessions // groups
    per_pair = sess_here * list_len // (groups * ranks)
    new_len = tokens.shape[0] // sess_here
    head_dim = kv_pool.shape[4]
    const = head_dim**-0.5 * LOG2E
    device_id = group * ranks + rank
    pool = kv_pool.reshape(pool_size, 2, head_dim, head_dim)

    table = block_table.reshape(groups, sess_here * list_len)
    steps = jnp.arange(groups, dtype=jnp.int32)
    send_table = jnp.roll(table, -group, axis=0)
    here = send_table // pool_size == device_id
    upper = jnp.triu(jnp.ones((sess_here * list_len,) * 2, BF16))
    order = jnp.dot(here.astype(BF16), upper, preferred_element_type=F32).astype(jnp.int32)
    wanted = jnp.arange(1, per_pair + 1, dtype=jnp.int32)
    picked = here[:, None, :] & (order[:, None, :] == wanted[None, :, None])
    send_index = jnp.sum(jnp.where(picked, send_table[:, None, :] % pool_size, 0), axis=2)
    mine = lax.dynamic_index_in_dim(table, group, 0, keepdims=False).reshape(sess_here, list_len)
    lengths = lax.dynamic_slice_in_dim(prefix_len, group * sess_here, sess_here)
    source = ((group - steps) % groups) * ranks + rank
    from_there = mine[None] // pool_size == source[:, None, None]
    slots = jnp.arange(list_len, dtype=jnp.int32)
    keys_in = jnp.clip(lengths[:, None] - slots[None, :] * head_dim, 0, head_dim)
    live_keys = jnp.sum(jnp.where(from_there, keys_in[None], 0), axis=2)
    counts = jnp.sum(from_there.astype(jnp.int32), axis=2)
    starts = jnp.cumsum(counts, axis=1) - counts
    meta = jnp.stack([starts, live_keys], axis=2).reshape(groups, 2 * sess_here).astype(jnp.int32)

    rank_only = rank[None].astype(jnp.int32)
    begun = project(
        rank_only, jnp.stack([send_index[1], send_index[3], send_index[2]]), pool,
        tokens, norm_gain[None, :], w_query, w_key, w_value,
    )
    parts = begun[:ranks]
    near = [shifted(begun[ranks], "group", 1), shifted(begun[ranks + 1], "group", 3)]
    far = shifted(begun[ranks + 2], "group", 2)
    rest, _ = lax.optimization_barrier((send_index[:1], parts[0]))
    own_blocks, new_pool = pack(rest, pool)
    parts = [parts[0]] + [shifted(parts[step], "ctx", step) for step in (1, 3, 2)]
    parts, own_blocks = lax.optimization_barrier((parts, own_blocks))
    fresh = finish(parts, tokens.shape[1] * ranks)
    quarters = around(fresh, "ctx")

    first_meta = jnp.concatenate([rank_only, meta[0]])
    queries, norms, *state, block = attend_own(
        first_meta, quarters, own_blocks, new_len, const
    )
    near_meta = jnp.concatenate([meta[1], meta[3]])
    state = attend_near(near_meta, queries, norms, state, near, new_len, const)
    last_meta = jnp.concatenate([meta[2], rank_only])
    partial = attend_last(last_meta, queries, norms, state, far, new_len, const)
    partial = [partial[0]] + [shifted(partial[step], "ctx", step) for step in (1, 2, 3)]
    attended = combine(partial)

    planes = tp_size // 2
    out_meta = jnp.stack([rank, core, plane]).astype(jnp.int32)
    news = around(block, "group")
    targets = jnp.roll(write_slot.reshape(groups, ranks)[::-1], group + 1, axis=0).reshape(-1)
    places = jnp.where(targets // pool_size == device_id, targets % pool_size, -1)
    own, send, new_pool = project_out(
        out_meta, places, around(attended, "ctx"), w_out, news, new_pool, planes
    )
    other = lax.ppermute(send, "tp", [(i, i ^ 1) for i in range(tp_size)])
    total = own[0] + other[0].astype(F32)
    for step in range(1, planes):
        pair = (own[step] + other[step].astype(F32)).astype(BF16)
        total = total + shifted(pair, "tp", 2 * step).astype(F32)
    return (total.astype(BF16), new_pool.reshape(kv_pool.shape))


def solution(mesh):
    placed = (
        P("group", "ctx"),
        P("ctx"),
        P("ctx", "tp"),
        P("ctx", "tp"),
        P("ctx", "tp"),
        P("tp", "ctx"),
        P(("group", "ctx"), None, "tp", None, None),
        P(),
        P(),
        P(),
    )
    return jax.shard_map(
        local,
        mesh=mesh,
        in_specs=placed,
        out_specs=(P("group", ("ctx", "tp")), P(("group", "ctx"), None, "tp", None, None)),
        check_vma=False,
    )
```

```python
import jax
import jax.numpy as jnp
from jax import lax
from jax.experimental import pallas as pl
from jax.experimental.pallas import tpu as pltpu
from jax.sharding import PartitionSpec as P

NEG_FILL = -1e30
LOG2E = 1.4426950408889634
F32 = jnp.float32
BF16 = jnp.bfloat16
VMEM_BYTES = 30 * 1024 * 1024
VMEM_MOST = 58 * 1024 * 1024
CHUNK = 4
TAIL = 2
ROOM = 60.0
NO_COST = pl.CostEstimate(flops=1, bytes_accessed=1, transcendentals=0)
CTX = 4
SEND = ((0, 1, 2, 3), (1, 0, 3, 2), (3, 2, 1, 0), (2, 3, 0, 1))
NT = (((1,), (1,)), ((), ()))


def params(size=VMEM_BYTES):
    return pltpu.CompilerParams(vmem_limit_bytes=size)


def vmem():
    return pl.BlockSpec(memory_space=pltpu.VMEM)


def smem():
    return pl.BlockSpec(memory_space=pltpu.SMEM)


def anywhere():
    return pl.BlockSpec(memory_space=pl.ANY)


def gather_blocks(index_ref, pool, held, outs, sems):
    copies = []
    for step in range(held.shape[0]):
        for n in range(held.shape[1]):
            held[step, n] = pool[index_ref[step, n]]
        copies.append(pltpu.make_async_copy(held.at[step], outs[step], sems.at[step]))
        copies[-1].start()
    return copies


def project_kernel(
    meta_ref, index_ref, pool_ref, tok_ref, gain_ref, wq_ref, wk_ref, wv_ref, *refs
):
    steps = index_ref.shape[0]
    out_refs, block_refs = refs[:CTX], refs[CTX : CTX + steps]
    pool, held, tok, wq, wkv, norm, total, in_sems, out_sems, block_sems = refs[CTX + steps :]
    rows, features = tok.shape
    q_cols = wq.shape[1]
    deep = features // 4
    part = rows // CTX
    rank = meta_ref[0]
    fetch_tok = pltpu.make_async_copy(tok_ref, tok, in_sems.at[0])
    fetch_w = [
        pltpu.make_async_copy(
            wq_ref.at[pl.ds(n * deep, deep)], wq.at[pl.ds(n * deep, deep)], in_sems.at[1 + n]
        )
        for n in range(4)
    ]
    fetch_kv = [
        pltpu.make_async_copy(ref, wkv.at[:, pl.ds(n * 128, 128)], in_sems.at[5 + n])
        for n, ref in enumerate((wk_ref, wv_ref))
    ]
    fetch_pool = pltpu.make_async_copy(pool_ref, pool, block_sems.at[steps])
    for copy in [fetch_pool, fetch_tok] + fetch_kv + fetch_w:
        copy.start()
    fetch_pool.wait()
    sent = gather_blocks(index_ref, pool, held, block_refs, block_sems)
    fetch_tok.wait()
    for first in range(0, rows, part):
        some = slice(first, first + part)
        wide = tok[some].astype(F32)
        norm[some] = (wide * gain_ref[...]).astype(BF16)
        squares = jnp.sum(wide * wide, axis=1, keepdims=True)
        total[some, q_cols + 256 :] = jnp.broadcast_to(squares, (part, 128))
    for copy in fetch_kv:
        copy.wait()
    total[:, q_cols : q_cols + 256] = jnp.dot(norm[...], wkv[...], preferred_element_type=F32)
    half = 2 * deep
    for n in range(2):
        fetch_w[2 * n].wait()
        fetch_w[2 * n + 1].wait()
        depth = slice(n * half, n * half + half)
        for first in range(0, q_cols, 256):
            cols = slice(first, first + 256)
            value = jnp.dot(norm[:, depth], wq[depth, cols], preferred_element_type=F32)
            if n == 0:
                total[:, cols] = value
            else:
                total[:, cols] += value
    copies = []
    for step in range(CTX):
        place = lax.rem(rank + step, CTX)
        source = total.at[pl.ds(pl.multiple_of(place * part, part), part)]
        copies.append(pltpu.make_async_copy(source, out_refs[step], out_sems.at[step]))
        copies[-1].start()
    for copy in sent + copies:
        copy.wait()


def project(meta, index, pool, tokens, gain, w_query, w_key, w_value):
    steps, count = index.shape
    block = pool.shape[1:]
    rows, features = tokens.shape
    q_cols = w_query.shape[1]
    cols = q_cols + 384
    return pl.pallas_call(
        project_kernel,
        out_shape=[jax.ShapeDtypeStruct((rows // CTX, cols), F32)] * CTX
        + [jax.ShapeDtypeStruct((count,) + block, BF16)] * steps,
        in_specs=[smem(), smem(), anywhere(), anywhere(), vmem()] + [anywhere()] * 3,
        out_specs=[anywhere()] * (CTX + steps),
        scratch_shapes=[
            pltpu.VMEM(pool.shape, BF16),
            pltpu.VMEM((steps, count) + block, BF16),
            pltpu.VMEM((rows, features), BF16),
            pltpu.VMEM((features, q_cols), BF16),
            pltpu.VMEM((features, 256), BF16),
            pltpu.VMEM((rows, features), BF16),
            pltpu.VMEM((rows, cols), F32),
            pltpu.SemaphoreType.DMA((7,)),
            pltpu.SemaphoreType.DMA((CTX,)),
            pltpu.SemaphoreType.DMA((steps + 1,)),
        ],
        compiler_params=params(VMEM_MOST),
        cost_estimate=NO_COST,
        name="project",
    )(meta, index, pool, tokens, gain, w_query, w_key, w_value)


def finish_kernel(features, *refs):
    part_refs, out_ref = refs[:CTX], refs[CTX]
    q_cols = out_ref.shape[1]
    total = part_refs[0][...]
    for ref in part_refs[1:]:
        total = total + ref[...]
    scale = lax.rsqrt(total[:, q_cols : q_cols + 1] / features + 1e-05)
    out_ref[...] = (total[:, :q_cols] * scale).astype(BF16)


def finish(parts, features):
    rows, cols = parts[0].shape
    return pl.pallas_call(
        lambda *refs: finish_kernel(features, *refs),
        out_shape=jax.ShapeDtypeStruct((rows, cols - 128), BF16),
        in_specs=[vmem()] * CTX,
        out_specs=vmem(),
        compiler_params=params(),
        cost_estimate=NO_COST,
        name="finish",
    )(*parts)


def pack_kernel(index_ref, pool_ref, *refs):
    steps = index_ref.shape[0]
    outs = refs[:steps]
    pool_out, pool, held, sems = refs[steps:]
    fetch = pltpu.make_async_copy(pool_ref, pool, sems.at[steps])
    fetch.start()
    fetch.wait()
    keep = pltpu.make_async_copy(pool, pool_out, sems.at[steps])
    keep.start()
    for copy in gather_blocks(index_ref, pool, held, outs, sems) + [keep]:
        copy.wait()


def pack(index, pool):
    steps, count = index.shape
    block = pool.shape[1:]
    return pl.pallas_call(
        pack_kernel,
        out_shape=[jax.ShapeDtypeStruct((count,) + block, BF16)] * steps
        + [jax.ShapeDtypeStruct(pool.shape, BF16)],
        in_specs=[smem(), anywhere()],
        out_specs=[anywhere()] * (steps + 1),
        scratch_shapes=[
            pltpu.VMEM(pool.shape, BF16),
            pltpu.VMEM((steps, count) + block, BF16),
            pltpu.SemaphoreType.DMA((steps + 1,)),
        ],
        compiler_params=params(VMEM_MOST),
        cost_estimate=NO_COST,
        name="pack",
    )(index, pool)


def pack_lanes(ref, rows):
    lane = lax.broadcasted_iota(jnp.int32, (ref.shape[1], 128), 1)[: ref[0, rows, :].shape[0]]
    packed = jnp.zeros(lane.shape, F32)
    for head in range(ref.shape[0]):
        packed = jnp.where(lane == head, ref[head, rows, :], packed)
    return packed


def sweep(q_ref, rows, heads, keys, finish_head):
    pending = None
    for head in range(heads):
        cols = slice(head * 128, head * 128 + 128)
        scores = lax.dot_general(q_ref[rows, cols], keys, NT, preferred_element_type=F32)
        if pending is not None:
            finish_head(*pending)
        pending = (head, cols, scores)
    finish_head(*pending)


def moving(q_ref, m_ref, l_ref, acc_ref, rows, keys, values_ext, mask, const, zero):
    def finish_head(head, cols, scores):
        scores = jnp.where(mask, scores, NEG_FILL)
        m_old = m_ref[head, rows, :]
        m_new = jnp.maximum(m_old, jnp.max(scores, axis=1, keepdims=True) * const)
        alpha = jnp.exp2(m_old - m_new)
        reps = scores.shape[1] // 128
        weights = jnp.exp2(scores * const - jnp.concatenate([m_new] * reps, axis=1))
        if zero:
            weights = jnp.where(mask, weights, 0.0)
        mixed = jnp.dot(weights.astype(BF16), values_ext, preferred_element_type=F32)
        m_ref[head, rows, :] = m_new
        l_ref[head, rows, :] = l_ref[head, rows, :] * alpha + mixed[:, 128:]
        acc_ref[rows, cols] = acc_ref[rows, cols] * alpha + mixed[:, :128]

    sweep(q_ref, rows, m_ref.shape[0], keys, finish_head)


def steady(q_ref, m_ref, l_ref, acc_ref, rows, keys, values_ext, mask, const):
    def finish_head(head, cols, scores):
        if mask is not None:
            scores = jnp.where(mask, scores, NEG_FILL)
        reps = scores.shape[1] // 128
        shift = jnp.concatenate([m_ref[head, rows, :]] * reps, axis=1)
        weights = jnp.exp2(scores * const - shift)
        mixed = jnp.dot(weights.astype(BF16), values_ext, preferred_element_type=F32)
        l_ref[head, rows, :] += mixed[:, 128:]
        acc_ref[rows, cols] += mixed[:, :128]

    sweep(q_ref, rows, m_ref.shape[0], keys, finish_head)


def prefix_part(meta_ref, base, q_ref, qn_ref, kv_ref, vx_ref, m_ref, l_ref, acc_ref, new_len, const):
    blocks = kv_ref.shape[0]
    state = (q_ref, m_ref, l_ref, acc_ref)
    all_keys = kv_ref[:, 0].reshape(blocks * 128, 128)
    vx_ref[:, :128] = kv_ref[:, 1].reshape(blocks * 128, 128)
    vx_ref[:, 128:] = jnp.ones((blocks * 128, 128), BF16)
    norms = jnp.dot(all_keys * all_keys, jnp.ones((128, 128), BF16), preferred_element_type=F32)
    reach = jnp.sqrt(jnp.max(norms)) * (1.05 * const)

    def session_body(session, carry):
        row0 = pl.multiple_of(session * new_len, new_len)
        rows = pl.ds(row0, new_len)
        first = meta_ref[base + 2 * session]
        keys_live = meta_ref[base + 2 * session + 1]
        high = first * 128 + keys_live
        total = (keys_live + 127) // 128

        def enough():
            room = qn_ref[rows, :] * reach - pack_lanes(m_ref, rows)
            return (jnp.max(room) <= ROOM).astype(jnp.int32)

        def piece(wanted, count, masked):
            span = count * 128
            begin = jnp.minimum(wanted, blocks - count)
            keys = kv_ref[pl.ds(begin, count), 0].reshape(span, 128)
            values_ext = vx_ref[pl.ds(pl.multiple_of(begin * 128, 128), span), :]
            if not masked:
                return keys, values_ext, None
            index = begin * 128 + lax.broadcasted_iota(jnp.int32, (1, span), 1)
            return keys, values_ext, (index >= wanted * 128) & (index < high)

        def slow_more(now):
            return (now[0] < total) & (now[1] == 0)

        def slow(now):
            moving(*state, rows, *piece(first + now[0], CHUNK, True), const, False)
            return now[0] + CHUNK, enough()

        done, _ = lax.while_loop(slow_more, slow, (0, enough()))
        full = jnp.maximum(keys_live - done * 128, 0) // (CHUNK * 128)

        def fast(step, carry):
            steady(*state, rows, *piece(first + done + step * CHUNK, CHUNK, False), const)
            return carry

        lax.fori_loop(0, full, fast, 0)
        done = done + full * CHUNK

        def tail(step, carry):
            steady(*state, rows, *piece(first + done + step * TAIL, TAIL, True), const)
            return carry

        lax.fori_loop(0, (jnp.maximum(total - done, 0) + TAIL - 1) // TAIL, tail, 0)
        return carry

    lax.fori_loop(0, q_ref.shape[0] // new_len, session_body, 0)


def first_kernel(
    new_len, const, meta_ref, a, b, c, d, buf,
    q_ref, qn_ref, acc_ref, mp_ref, lp_ref, new_ref, kv_ref, vx_ref, m_ref, l_ref, sem,
):
    fetch = pltpu.make_async_copy(buf, kv_ref, sem)
    fetch.start()
    tokens, q_cols = q_ref.shape
    part = a.shape[0]
    heads = m_ref.shape[0]
    rank = meta_ref[0]
    for step, ref in enumerate((a, b, c, d)):
        place = lax.rem(rank + CTX - step, CTX)
        q_ref[pl.ds(pl.multiple_of(place * part, part), part), :] = ref[:, :q_cols]
        new_ref[place, 0] = ref[:, q_cols : q_cols + 128]
        new_ref[place, 1] = ref[:, q_cols + 128 :]
    m_ref[...] = jnp.full(m_ref.shape, NEG_FILL, F32)
    l_ref[...] = jnp.zeros(l_ref.shape, F32)
    acc_ref[...] = jnp.zeros(acc_ref.shape, F32)
    lane = lax.broadcasted_iota(jnp.int32, (tokens, 128), 1)
    squares = jnp.zeros((tokens, 128), F32)
    for head in range(heads):
        wide = q_ref[:, head * 128 : head * 128 + 128].astype(F32)
        squares = jnp.where(lane == head, jnp.sum(wide * wide, axis=1, keepdims=True), squares)
    qn_ref[...] = jnp.sqrt(squares)
    keys = a[:, q_cols : q_cols + 128]
    values_ext = jnp.concatenate(
        [a[:, q_cols + 128 : q_cols + 256], jnp.ones((part, 128), BF16)], axis=1
    )
    per_session = new_len // part
    rows = pl.ds(pl.multiple_of(lax.div(rank, per_session) * new_len, new_len), new_len)
    offset = lax.rem(rank, per_session) * part
    token = lax.broadcasted_iota(jnp.int32, (new_len, part), 0)
    fresh = lax.broadcasted_iota(jnp.int32, (new_len, part), 1) + offset
    moving(q_ref, m_ref, l_ref, acc_ref, rows, keys, values_ext, fresh <= token, const, True)
    fetch.wait()
    prefix_part(
        meta_ref, 1, q_ref, qn_ref, kv_ref, vx_ref, m_ref, l_ref, acc_ref, new_len, const
    )
    mp_ref[...] = pack_lanes(m_ref, slice(None))
    lp_ref[...] = pack_lanes(l_ref, slice(None))


def load_state(mp_in, lp_in, m_ref, l_ref):
    shape = m_ref.shape[1:]
    for head in range(m_ref.shape[0]):
        m_ref[head] = jnp.broadcast_to(mp_in[:, head : head + 1], shape)
        l_ref[head] = jnp.broadcast_to(lp_in[:, head : head + 1], shape)


def sources(
    new_len, const, meta_ref, q_ref, qn_ref, bufs, acc_in, mp_in, lp_in,
    acc_ref, kv_ref, vx_ref, m_ref, l_ref, sems,
):
    copies = []
    for n, buf in enumerate(bufs):
        copies.append(pltpu.make_async_copy(buf, kv_ref.at[n], sems.at[n]))
        copies[-1].start()
    acc_ref[...] = acc_in[...]
    load_state(mp_in, lp_in, m_ref, l_ref)
    for n, copy in enumerate(copies):
        copy.wait()
        prefix_part(
            meta_ref, 4 * n, q_ref, qn_ref, kv_ref.at[n], vx_ref, m_ref, l_ref, acc_ref, new_len,
            const,
        )


def near_kernel(
    new_len, const, meta_ref, q_ref, qn_ref, acc_in, mp_in, lp_in, buf,
    acc_ref, mp_ref, lp_ref, kv_ref, vx_ref, m_ref, l_ref, sems,
):
    sources(
        new_len, const, meta_ref, q_ref, qn_ref, (buf,), acc_in, mp_in, lp_in,
        acc_ref, kv_ref, vx_ref, m_ref, l_ref, sems,
    )
    mp_ref[...] = pack_lanes(m_ref, slice(None))
    lp_ref[...] = pack_lanes(l_ref, slice(None))


def last_kernel(
    new_len, const, meta_ref, q_ref, qn_ref, acc_in, mp_in, lp_in, buf,
    out_a, out_b, out_c, out_d, acc_ref, kv_ref, vx_ref, m_ref, l_ref, sems,
):
    sources(
        new_len, const, meta_ref, q_ref, qn_ref, (buf,), acc_in, mp_in, lp_in,
        acc_ref, kv_ref, vx_ref, m_ref, l_ref, sems,
    )
    tokens = q_ref.shape[0]
    heads = m_ref.shape[0]
    part = tokens // CTX
    rank = meta_ref[4]
    row = lax.broadcasted_iota(jnp.int32, (16, heads * 128), 0)
    for step, out_ref in enumerate((out_a, out_b, out_c, out_d)):
        place = lax.rem(rank + step, CTX)
        rows = pl.ds(pl.multiple_of(place * part, part), part)
        for head in range(heads):
            cols = slice(head * 128, head * 128 + 128)
            total = l_ref[head, rows, :]
            empty = total == 0.0
            safe = jnp.where(empty, 1.0, total)
            out_ref[:part, cols] = (acc_ref[rows, cols] / safe).astype(BF16)
            m_ref[head, rows, :] = jnp.where(
                empty, NEG_FILL, m_ref[head, rows, :] + jnp.log2(safe)
            )
        turned = pack_lanes(m_ref, rows).T
        line = jnp.concatenate([turned[h : h + 1] for h in range(heads)], axis=1)
        high = line.astype(BF16).astype(F32)
        rest = line - high
        mid = rest.astype(BF16).astype(F32)
        low = rest - mid
        tile = jnp.where(row == 0, high, jnp.where(row == 1, mid, jnp.where(row == 2, low, 0.0)))
        out_ref[part : part + 16, :] = tile.astype(BF16)


def scratch(tokens, heads, blocks, lead=()):
    return [
        pltpu.VMEM(lead + (blocks, 2, 128, 128), BF16),
        pltpu.VMEM((blocks * 128, 256), BF16),
        pltpu.VMEM((heads, tokens, 128), F32),
        pltpu.VMEM((heads, tokens, 128), F32),
    ]


def state_shapes(tokens, q_cols):
    return [
        jax.ShapeDtypeStruct((tokens, q_cols), F32),
        jax.ShapeDtypeStruct((tokens, 128), F32),
        jax.ShapeDtypeStruct((tokens, 128), F32),
    ]


def attend_own(meta, quarters, buf, new_len, const):
    part = quarters[0].shape[0]
    q_cols = quarters[0].shape[1] - 256
    tokens = part * CTX
    heads = q_cols // 128
    blocks = buf.shape[0]
    return pl.pallas_call(
        lambda *refs: first_kernel(new_len, const, *refs),
        out_shape=[
            jax.ShapeDtypeStruct((tokens, q_cols), BF16),
            jax.ShapeDtypeStruct((tokens, 128), F32),
        ]
        + state_shapes(tokens, q_cols)
        + [jax.ShapeDtypeStruct((CTX, 2, part, 128), BF16)],
        in_specs=[smem()] + [vmem()] * 4 + [anywhere()],
        out_specs=[vmem()] * 6,
        scratch_shapes=scratch(tokens, heads, blocks) + [pltpu.SemaphoreType.DMA(())],
        compiler_params=params(),
        cost_estimate=NO_COST,
        name="attend_own",
    )(meta, *quarters, buf)


def attend_near(meta, queries, norms, state, bufs, new_len, const):
    tokens, q_cols = queries.shape
    heads = q_cols // 128
    blocks = bufs[0].shape[0]
    return pl.pallas_call(
        lambda *refs: near_kernel(new_len, const, *refs),
        out_shape=state_shapes(tokens, q_cols),
        in_specs=[smem()] + [vmem()] * 5 + [anywhere()] * len(bufs),
        out_specs=[vmem()] * 3,
        scratch_shapes=scratch(tokens, heads, blocks, (len(bufs),))
        + [pltpu.SemaphoreType.DMA((len(bufs),))],
        compiler_params=params(),
        cost_estimate=NO_COST,
        name="attend_near",
    )(meta, queries, norms, *state, *bufs)


def attend_last(meta, queries, norms, state, buf, new_len, const):
    tokens, q_cols = queries.shape
    heads = q_cols // 128
    blocks = buf.shape[0]
    pairs = blocks * 128 * tokens // 2 * heads
    return pl.pallas_call(
        lambda *refs: last_kernel(new_len, const, *refs),
        out_shape=[jax.ShapeDtypeStruct((tokens // CTX + 16, q_cols), BF16)] * CTX,
        in_specs=[smem()] + [vmem()] * 5 + [anywhere()],
        out_specs=[vmem()] * CTX,
        scratch_shapes=[pltpu.VMEM((tokens, q_cols), F32)]
        + scratch(tokens, heads, blocks, (1,))
        + [pltpu.SemaphoreType.DMA((1,))],
        compiler_params=params(),
        cost_estimate=pl.CostEstimate(
            flops=pairs * 512, bytes_accessed=8 << 20, transcendentals=pairs
        ),
        name="attend_last",
    )(meta, queries, norms, *state, buf)


def combine_kernel(*refs):
    in_refs, out_ref = refs[:CTX], refs[CTX]
    part, q_cols = out_ref.shape
    heads = q_cols // 128
    lines = []
    for c in range(CTX):
        tile = in_refs[c][part : part + 16, :].astype(F32)
        lines.append(tile[0:1] + tile[1:2] + tile[2:3])
    top = lines[0]
    for line in lines[1:]:
        top = jnp.maximum(top, line)
    shares = [jnp.exp2(line - top) for line in lines]
    total = shares[0] + shares[1] + shares[2] + shares[3]
    pieces = []
    for share in shares:
        share = share / total
        pieces += [share[:, h * 128 : h * 128 + 128] for h in range(heads)]
    pieces.append(jnp.zeros((128 - CTX * heads, 128), F32))
    turned = jnp.concatenate(pieces, axis=0).T
    for head in range(heads):
        cols = slice(head * 128, head * 128 + 128)
        mixed = jnp.zeros((part, 128), F32)
        for c in range(CTX):
            at = c * heads + head
            mixed = mixed + in_refs[c][:part, cols].astype(F32) * turned[:, at : at + 1]
        out_ref[:, cols] = mixed.astype(BF16)


def combine(arrived):
    rows, q_cols = arrived[0].shape
    return pl.pallas_call(
        combine_kernel,
        out_shape=jax.ShapeDtypeStruct((rows - 16, q_cols), BF16),
        in_specs=[vmem()] * CTX,
        out_specs=vmem(),
        compiler_params=params(),
        cost_estimate=NO_COST,
        name="combine",
    )(*arrived)


def out_kernel(
    meta_ref, place_ref, a, b, c, d, w_ref, new_a, new_b, new_c, new_d, pool_in,
    own_ref, send_ref, pool_out, rows_ref, sems,
):
    rank = meta_ref[0]
    core = meta_ref[1]
    part = a.shape[0]
    half = own_ref.shape[2]

    def place_blocks(act):
        count = new_a.shape[0]
        for n, ref in enumerate((new_a, new_b, new_c, new_d)):
            for i in range(count):
                at = n * count + i
                slot = place_ref[at]

                @pl.when(slot >= 0)
                def _(ref=ref, i=i, at=at, slot=slot):
                    act(pltpu.make_async_copy(ref.at[i], pool_out.at[slot], sems.at[at]))

    @pl.when(pl.program_id(0) == 0)
    def _():
        place_blocks(lambda copy: copy.start())
        for step, ref in enumerate((a, b, c, d)):
            place = lax.rem(rank + CTX - step, CTX)
            rows_ref[pl.ds(pl.multiple_of(place * part, part), part), :] = ref[...]

    product = jnp.dot(rows_ref[...], w_ref[...], preferred_element_type=F32)

    @pl.when(core == 0)
    def _():
        own_ref[0] = product[:, :half]
        send_ref[0] = product[:, half:].astype(BF16)

    @pl.when(core != 0)
    def _():
        own_ref[0] = product[:, half:]
        send_ref[0] = product[:, :half].astype(BF16)

    @pl.when(pl.program_id(0) == pl.num_programs(0) - 1)
    def _():
        place_blocks(lambda copy: copy.wait())


def project_out(meta, places, quarters, w_out, news, pool, planes):
    part, depth = quarters[0].shape
    tokens = part * CTX
    width = w_out.shape[1] // planes
    whole = pl.BlockSpec((part, depth), lambda i, *_: (0, 0))
    out = pl.BlockSpec((1, tokens, width // 2), lambda i, *_: (i, 0, 0))
    return pl.pallas_call(
        out_kernel,
        grid_spec=pltpu.PrefetchScalarGridSpec(
            num_scalar_prefetch=2,
            grid=(planes,),
            in_specs=[whole] * 4
            + [pl.BlockSpec((depth, width), lambda i, meta, _: (0, lax.rem(meta[2] + i, planes)))]
            + [anywhere()] * 5,
            out_specs=[out] * 2 + [anywhere()],
            scratch_shapes=[
                pltpu.VMEM((tokens, depth), BF16),
                pltpu.SemaphoreType.DMA((places.shape[0],)),
            ],
        ),
        out_shape=[
            jax.ShapeDtypeStruct((planes, tokens, width // 2), F32),
            jax.ShapeDtypeStruct((planes, tokens, width // 2), BF16),
            jax.ShapeDtypeStruct(pool.shape, BF16),
        ],
        input_output_aliases={11: 2},
        compiler_params=params(),
        cost_estimate=NO_COST,
        name="project_out",
    )(meta, places, *quarters, w_out, *news, pool)


def shifted(value, axis, step):
    size = lax.axis_size(axis)
    return lax.ppermute(value, axis, [(i, (i + step) % size) for i in range(size)])


def moved(value, step):
    return lax.ppermute(value, "group", list(enumerate(SEND[step])))


def around(value, axis):
    return [value] + [shifted(value, axis, step) for step in (1, 2, 3)]


def local(
    tokens, norm_gain, w_query, w_key, w_value, w_out, kv_pool, block_table, prefix_len, write_slot
):
    groups = lax.axis_size("group")
    ranks = lax.axis_size("ctx")
    tp_size = lax.axis_size("tp")
    rank = lax.axis_index("ctx")
    group = lax.axis_index("group")
    core = lax.axis_index("tp") % 2
    plane = lax.axis_index("tp") // 2
    pool_size = kv_pool.shape[0]
    sessions, list_len = block_table.shape
    sess_here = sessions // groups
    per_pair = sess_here * list_len // (groups * ranks)
    new_len = tokens.shape[0] // sess_here
    head_dim = kv_pool.shape[4]
    const = head_dim**-0.5 * LOG2E
    device_id = group * ranks + rank
    pool = kv_pool.reshape(pool_size, 2, head_dim, head_dim)

    table = block_table.reshape(groups, sess_here * list_len)
    send_to = jnp.array(SEND, jnp.int32)
    receive = jnp.array([[line.index(g) for g in range(groups)] for line in SEND], jnp.int32)
    send_table = table[lax.dynamic_index_in_dim(send_to, group, 1, keepdims=False)]
    here = send_table // pool_size == device_id
    upper = jnp.triu(jnp.ones((sess_here * list_len,) * 2, BF16))
    order = jnp.dot(here.astype(BF16), upper, preferred_element_type=F32).astype(jnp.int32)
    wanted = jnp.arange(1, per_pair + 1, dtype=jnp.int32)
    picked = here[:, None, :] & (order[:, None, :] == wanted[None, :, None])
    send_index = jnp.sum(jnp.where(picked, send_table[:, None, :] % pool_size, 0), axis=2)
    mine = lax.dynamic_index_in_dim(table, group, 0, keepdims=False).reshape(sess_here, list_len)
    lengths = lax.dynamic_slice_in_dim(prefix_len, group * sess_here, sess_here)
    source = lax.dynamic_index_in_dim(receive, group, 1, keepdims=False) * ranks + rank
    from_there = mine[None] // pool_size == source[:, None, None]
    slots = jnp.arange(list_len, dtype=jnp.int32)
    keys_in = jnp.clip(lengths[:, None] - slots[None, :] * head_dim, 0, head_dim)
    live_keys = jnp.sum(jnp.where(from_there, keys_in[None], 0), axis=2)
    counts = jnp.sum(from_there.astype(jnp.int32), axis=2)
    starts = jnp.cumsum(counts, axis=1) - counts
    meta = jnp.stack([starts, live_keys], axis=2).reshape(groups, 2 * sess_here).astype(jnp.int32)

    rank_only = rank[None].astype(jnp.int32)
    begun = project(
        rank_only, send_index[1:], pool,
        tokens, norm_gain[None, :], w_query, w_key, w_value,
    )
    parts = begun[:ranks]
    early = [moved(begun[ranks], 1), moved(begun[ranks + 1], 2)]
    far = moved(begun[ranks + 2], 3)
    rest, _ = lax.optimization_barrier((send_index[:1], parts[0]))
    own_blocks, new_pool = pack(rest, pool)
    parts = [parts[0]] + [shifted(parts[step], "ctx", step) for step in (1, 3, 2)]
    parts, own_blocks = lax.optimization_barrier((parts, own_blocks))
    fresh = finish(parts, tokens.shape[1] * ranks)
    quarters = around(fresh, "ctx")

    first_meta = jnp.concatenate([rank_only, meta[0]])
    queries, norms, *state, block = attend_own(
        first_meta, quarters, own_blocks, new_len, const
    )
    for step in (1, 2):
        state = attend_near(
            meta[step], queries, norms, state, [early[step - 1]], new_len, const
        )
    last_meta = jnp.concatenate([meta[3], rank_only])
    partial = attend_last(last_meta, queries, norms, state, far, new_len, const)
    partial = [partial[0]] + [shifted(partial[step], "ctx", step) for step in (1, 2, 3)]
    attended = combine(partial)

    planes = tp_size // 2
    out_meta = jnp.stack([rank, core, plane]).astype(jnp.int32)
    news = around(block, "group")
    targets = jnp.roll(write_slot.reshape(groups, ranks)[::-1], group + 1, axis=0).reshape(-1)
    places = jnp.where(targets // pool_size == device_id, targets % pool_size, -1)
    own, send, new_pool = project_out(
        out_meta, places, around(attended, "ctx"), w_out, news, new_pool, planes
    )
    other = lax.ppermute(send, "tp", [(i, i ^ 1) for i in range(tp_size)])
    total = own[0] + other[0].astype(F32)
    for step in range(1, planes):
        pair = (own[step] + other[step].astype(F32)).astype(BF16)
        total = total + shifted(pair, "tp", 2 * step).astype(F32)
    return (total.astype(BF16), new_pool.reshape(kv_pool.shape))


def solution(mesh):
    placed = (
        P("group", "ctx"),
        P("ctx"),
        P("ctx", "tp"),
        P("ctx", "tp"),
        P("ctx", "tp"),
        P("tp", "ctx"),
        P(("group", "ctx"), None, "tp", None, None),
        P(),
        P(),
        P(),
    )
    return jax.shard_map(
        local,
        mesh=mesh,
        in_specs=placed,
        out_specs=(P("group", ("ctx", "tp")), P(("group", "ctx"), None, "tp", None, None)),
        check_vma=False,
    )
```

```python
import jax
import jax.numpy as jnp
from jax import lax
from jax.experimental import pallas as pl
from jax.experimental.pallas import tpu as pltpu
from jax.sharding import PartitionSpec as P

NEG_FILL = -1e30
LOG2E = 1.4426950408889634
F32 = jnp.float32
BF16 = jnp.bfloat16
VMEM_BYTES = 30 * 1024 * 1024
VMEM_MOST = 58 * 1024 * 1024
CHUNK = 4
TAIL = 2
ROOM = 60.0
NO_COST = pl.CostEstimate(flops=1, bytes_accessed=1, transcendentals=0)
CTX = 4
SEND = ((0, 1, 2, 3), (1, 0, 3, 2), (3, 2, 1, 0), (2, 3, 0, 1))
NT = (((1,), (1,)), ((), ()))


def params(size=VMEM_BYTES):
    return pltpu.CompilerParams(vmem_limit_bytes=size)


def vmem():
    return pl.BlockSpec(memory_space=pltpu.VMEM)


def smem():
    return pl.BlockSpec(memory_space=pltpu.SMEM)


def anywhere():
    return pl.BlockSpec(memory_space=pl.ANY)


def gather_blocks(index_ref, pool, held, outs, sems):
    copies = []
    for step in range(held.shape[0]):
        for n in range(held.shape[1]):
            held[step, n] = pool[index_ref[step, n]]
        copies.append(pltpu.make_async_copy(held.at[step], outs[step], sems.at[step]))
        copies[-1].start()
    return copies


def project_kernel(
    meta_ref, index_ref, pool_ref, tok_ref, gain_ref, wq_ref, wk_ref, wv_ref, *refs
):
    steps = index_ref.shape[0]
    out_refs, block_refs = refs[:CTX], refs[CTX : CTX + steps]
    pool, held, tok, wq, wkv, norm, total, in_sems, out_sems, block_sems = refs[CTX + steps :]
    rows, features = tok.shape
    q_cols = wq.shape[1]
    deep = features // 4
    part = rows // CTX
    rank = meta_ref[0]
    fetch_tok = pltpu.make_async_copy(tok_ref, tok, in_sems.at[0])
    fetch_w = [
        pltpu.make_async_copy(
            wq_ref.at[pl.ds(n * deep, deep)], wq.at[pl.ds(n * deep, deep)], in_sems.at[1 + n]
        )
        for n in range(4)
    ]
    fetch_kv = [
        pltpu.make_async_copy(ref, wkv.at[:, pl.ds(n * 128, 128)], in_sems.at[5 + n])
        for n, ref in enumerate((wk_ref, wv_ref))
    ]
    fetch_pool = pltpu.make_async_copy(pool_ref, pool, block_sems.at[steps])
    for copy in [fetch_pool, fetch_tok] + fetch_kv + fetch_w:
        copy.start()
    fetch_pool.wait()
    sent = gather_blocks(index_ref, pool, held, block_refs, block_sems)
    fetch_tok.wait()
    for first in range(0, rows, part):
        some = slice(first, first + part)
        wide = tok[some].astype(F32)
        norm[some] = (wide * gain_ref[...]).astype(BF16)
        squares = jnp.sum(wide * wide, axis=1, keepdims=True)
        total[some, q_cols + 256 :] = jnp.broadcast_to(squares, (part, 128))
    for copy in fetch_kv:
        copy.wait()
    total[:, q_cols : q_cols + 256] = jnp.dot(norm[...], wkv[...], preferred_element_type=F32)
    half = 2 * deep
    for n in range(2):
        fetch_w[2 * n].wait()
        fetch_w[2 * n + 1].wait()
        depth = slice(n * half, n * half + half)
        for first in range(0, q_cols, 256):
            cols = slice(first, first + 256)
            value = jnp.dot(norm[:, depth], wq[depth, cols], preferred_element_type=F32)
            if n == 0:
                total[:, cols] = value
            else:
                total[:, cols] += value
    copies = []
    for step in range(CTX):
        place = lax.rem(rank + step, CTX)
        source = total.at[pl.ds(pl.multiple_of(place * part, part), part)]
        copies.append(pltpu.make_async_copy(source, out_refs[step], out_sems.at[step]))
        copies[-1].start()
    for copy in sent + copies:
        copy.wait()


def project(meta, index, pool, tokens, gain, w_query, w_key, w_value):
    steps, count = index.shape
    block = pool.shape[1:]
    rows, features = tokens.shape
    q_cols = w_query.shape[1]
    cols = q_cols + 384
    return pl.pallas_call(
        project_kernel,
        out_shape=[jax.ShapeDtypeStruct((rows // CTX, cols), F32)] * CTX
        + [jax.ShapeDtypeStruct((count,) + block, BF16)] * steps,
        in_specs=[smem(), smem(), anywhere(), anywhere(), vmem()] + [anywhere()] * 3,
        out_specs=[anywhere()] * (CTX + steps),
        scratch_shapes=[
            pltpu.VMEM(pool.shape, BF16),
            pltpu.VMEM((steps, count) + block, BF16),
            pltpu.VMEM((rows, features), BF16),
            pltpu.VMEM((features, q_cols), BF16),
            pltpu.VMEM((features, 256), BF16),
            pltpu.VMEM((rows, features), BF16),
            pltpu.VMEM((rows, cols), F32),
            pltpu.SemaphoreType.DMA((7,)),
            pltpu.SemaphoreType.DMA((CTX,)),
            pltpu.SemaphoreType.DMA((steps + 1,)),
        ],
        compiler_params=params(VMEM_MOST),
        cost_estimate=NO_COST,
        name="project",
    )(meta, index, pool, tokens, gain, w_query, w_key, w_value)


def finish_kernel(features, *refs):
    part_refs, out_ref = refs[:CTX], refs[CTX]
    q_cols = out_ref.shape[1]
    total = part_refs[0][...]
    for ref in part_refs[1:]:
        total = total + ref[...]
    scale = lax.rsqrt(total[:, q_cols : q_cols + 1] / features + 1e-05)
    out_ref[...] = (total[:, :q_cols] * scale).astype(BF16)


def finish(parts, features):
    rows, cols = parts[0].shape
    return pl.pallas_call(
        lambda *refs: finish_kernel(features, *refs),
        out_shape=jax.ShapeDtypeStruct((rows, cols - 128), BF16),
        in_specs=[vmem()] * CTX,
        out_specs=vmem(),
        compiler_params=params(),
        cost_estimate=NO_COST,
        name="finish",
    )(*parts)


def pack_kernel(index_ref, pool_ref, *refs):
    steps = index_ref.shape[0]
    outs = refs[:steps]
    pool_out, pool, held, sems = refs[steps:]
    fetch = pltpu.make_async_copy(pool_ref, pool, sems.at[steps])
    fetch.start()
    fetch.wait()
    keep = pltpu.make_async_copy(pool, pool_out, sems.at[steps])
    keep.start()
    for copy in gather_blocks(index_ref, pool, held, outs, sems) + [keep]:
        copy.wait()


def pack(index, pool):
    steps, count = index.shape
    block = pool.shape[1:]
    return pl.pallas_call(
        pack_kernel,
        out_shape=[jax.ShapeDtypeStruct((count,) + block, BF16)] * steps
        + [jax.ShapeDtypeStruct(pool.shape, BF16)],
        in_specs=[smem(), anywhere()],
        out_specs=[anywhere()] * (steps + 1),
        scratch_shapes=[
            pltpu.VMEM(pool.shape, BF16),
            pltpu.VMEM((steps, count) + block, BF16),
            pltpu.SemaphoreType.DMA((steps + 1,)),
        ],
        compiler_params=params(VMEM_MOST),
        cost_estimate=NO_COST,
        name="pack",
    )(index, pool)


def pack_lanes(ref, rows):
    lane = lax.broadcasted_iota(jnp.int32, (ref.shape[1], 128), 1)[: ref[0, rows, :].shape[0]]
    packed = jnp.zeros(lane.shape, F32)
    for head in range(ref.shape[0]):
        packed = jnp.where(lane == head, ref[head, rows, :], packed)
    return packed


def sweep(q_ref, rows, heads, keys, finish_head):
    pending = None
    for head in range(heads):
        cols = slice(head * 128, head * 128 + 128)
        scores = lax.dot_general(q_ref[rows, cols], keys, NT, preferred_element_type=F32)
        if pending is not None:
            finish_head(*pending)
        pending = (head, cols, scores)
    finish_head(*pending)


def moving(q_ref, m_ref, l_ref, acc_ref, rows, keys, values_ext, mask, const, zero):
    def finish_head(head, cols, scores):
        scores = jnp.where(mask, scores, NEG_FILL)
        m_old = m_ref[head, rows, :]
        m_new = jnp.maximum(m_old, jnp.max(scores, axis=1, keepdims=True) * const)
        alpha = jnp.exp2(m_old - m_new)
        reps = scores.shape[1] // 128
        weights = jnp.exp2(scores * const - jnp.concatenate([m_new] * reps, axis=1))
        if zero:
            weights = jnp.where(mask, weights, 0.0)
        mixed = jnp.dot(weights.astype(BF16), values_ext, preferred_element_type=F32)
        m_ref[head, rows, :] = m_new
        l_ref[head, rows, :] = l_ref[head, rows, :] * alpha + mixed[:, 128:]
        acc_ref[rows, cols] = acc_ref[rows, cols] * alpha + mixed[:, :128]

    sweep(q_ref, rows, m_ref.shape[0], keys, finish_head)


def steady(q_ref, m_ref, l_ref, acc_ref, rows, keys, values_ext, mask, const):
    def finish_head(head, cols, scores):
        if mask is not None:
            scores = jnp.where(mask, scores, NEG_FILL)
        reps = scores.shape[1] // 128
        shift = jnp.concatenate([m_ref[head, rows, :]] * reps, axis=1)
        weights = jnp.exp2(scores * const - shift)
        mixed = jnp.dot(weights.astype(BF16), values_ext, preferred_element_type=F32)
        l_ref[head, rows, :] += mixed[:, 128:]
        acc_ref[rows, cols] += mixed[:, :128]

    sweep(q_ref, rows, m_ref.shape[0], keys, finish_head)


def prefix_part(meta_ref, base, q_ref, qn_ref, kv_ref, vx_ref, m_ref, l_ref, acc_ref, new_len, const):
    blocks = kv_ref.shape[0]
    state = (q_ref, m_ref, l_ref, acc_ref)
    all_keys = kv_ref[:, 0].reshape(blocks * 128, 128)
    vx_ref[:, :128] = kv_ref[:, 1].reshape(blocks * 128, 128)
    vx_ref[:, 128:] = jnp.ones((blocks * 128, 128), BF16)
    norms = jnp.dot(all_keys * all_keys, jnp.ones((128, 128), BF16), preferred_element_type=F32)
    reach = jnp.sqrt(jnp.max(norms)) * (1.05 * const)

    def session_body(session, carry):
        row0 = pl.multiple_of(session * new_len, new_len)
        rows = pl.ds(row0, new_len)
        first = meta_ref[base + 2 * session]
        keys_live = meta_ref[base + 2 * session + 1]
        high = first * 128 + keys_live
        total = (keys_live + 127) // 128

        def enough():
            room = qn_ref[rows, :] * reach - pack_lanes(m_ref, rows)
            return (jnp.max(room) <= ROOM).astype(jnp.int32)

        def piece(wanted, count, masked):
            span = count * 128
            begin = jnp.minimum(wanted, blocks - count)
            keys = kv_ref[pl.ds(begin, count), 0].reshape(span, 128)
            values_ext = vx_ref[pl.ds(pl.multiple_of(begin * 128, 128), span), :]
            if not masked:
                return keys, values_ext, None
            index = begin * 128 + lax.broadcasted_iota(jnp.int32, (1, span), 1)
            return keys, values_ext, (index >= wanted * 128) & (index < high)

        def slow_more(now):
            return (now[0] < total) & (now[1] == 0)

        def slow(now):
            moving(*state, rows, *piece(first + now[0], CHUNK, True), const, False)
            return now[0] + CHUNK, enough()

        done, _ = lax.while_loop(slow_more, slow, (0, enough()))
        full = jnp.maximum(keys_live - done * 128, 0) // (CHUNK * 128)

        def fast(step, carry):
            steady(*state, rows, *piece(first + done + step * CHUNK, CHUNK, False), const)
            return carry

        lax.fori_loop(0, full, fast, 0)
        done = done + full * CHUNK

        def tail(step, carry):
            steady(*state, rows, *piece(first + done + step * TAIL, TAIL, True), const)
            return carry

        lax.fori_loop(0, (jnp.maximum(total - done, 0) + TAIL - 1) // TAIL, tail, 0)
        return carry

    lax.fori_loop(0, q_ref.shape[0] // new_len, session_body, 0)


def first_kernel(
    new_len, const, meta_ref, a, b, c, d, buf,
    q_ref, qn_ref, acc_ref, mp_ref, lp_ref, new_ref, kv_ref, vx_ref, m_ref, l_ref, sem,
):
    fetch = pltpu.make_async_copy(buf, kv_ref, sem)
    fetch.start()
    tokens, q_cols = q_ref.shape
    part = a.shape[0]
    heads = m_ref.shape[0]
    rank = meta_ref[0]
    for step, ref in enumerate((a, b, c, d)):
        place = lax.rem(rank + CTX - step, CTX)
        q_ref[pl.ds(pl.multiple_of(place * part, part), part), :] = ref[:, :q_cols]
        new_ref[place, 0] = ref[:, q_cols : q_cols + 128]
        new_ref[place, 1] = ref[:, q_cols + 128 :]
    m_ref[...] = jnp.full(m_ref.shape, NEG_FILL, F32)
    l_ref[...] = jnp.zeros(l_ref.shape, F32)
    acc_ref[...] = jnp.zeros(acc_ref.shape, F32)
    lane = lax.broadcasted_iota(jnp.int32, (tokens, 128), 1)
    squares = jnp.zeros((tokens, 128), F32)
    for head in range(heads):
        wide = q_ref[:, head * 128 : head * 128 + 128].astype(F32)
        squares = jnp.where(lane == head, jnp.sum(wide * wide, axis=1, keepdims=True), squares)
    qn_ref[...] = jnp.sqrt(squares)
    keys = a[:, q_cols : q_cols + 128]
    values_ext = jnp.concatenate(
        [a[:, q_cols + 128 : q_cols + 256], jnp.ones((part, 128), BF16)], axis=1
    )
    per_session = new_len // part
    rows = pl.ds(pl.multiple_of(lax.div(rank, per_session) * new_len, new_len), new_len)
    offset = lax.rem(rank, per_session) * part
    token = lax.broadcasted_iota(jnp.int32, (new_len, part), 0)
    fresh = lax.broadcasted_iota(jnp.int32, (new_len, part), 1) + offset
    moving(q_ref, m_ref, l_ref, acc_ref, rows, keys, values_ext, fresh <= token, const, True)
    fetch.wait()
    prefix_part(
        meta_ref, 1, q_ref, qn_ref, kv_ref, vx_ref, m_ref, l_ref, acc_ref, new_len, const
    )
    mp_ref[...] = pack_lanes(m_ref, slice(None))
    lp_ref[...] = pack_lanes(l_ref, slice(None))


def load_state(mp_in, lp_in, m_ref, l_ref):
    shape = m_ref.shape[1:]
    for head in range(m_ref.shape[0]):
        m_ref[head] = jnp.broadcast_to(mp_in[:, head : head + 1], shape)
        l_ref[head] = jnp.broadcast_to(lp_in[:, head : head + 1], shape)


def sources(
    new_len, const, meta_ref, q_ref, qn_ref, bufs, acc_in, mp_in, lp_in,
    acc_ref, kv_ref, vx_ref, m_ref, l_ref, sems,
):
    copies = []
    for n, buf in enumerate(bufs):
        copies.append(pltpu.make_async_copy(buf, kv_ref.at[n], sems.at[n]))
        copies[-1].start()
    acc_ref[...] = acc_in[...]
    load_state(mp_in, lp_in, m_ref, l_ref)
    for n, copy in enumerate(copies):
        copy.wait()
        prefix_part(
            meta_ref, 4 * n, q_ref, qn_ref, kv_ref.at[n], vx_ref, m_ref, l_ref, acc_ref, new_len,
            const,
        )


def near_kernel(
    new_len, const, meta_ref, q_ref, qn_ref, acc_in, mp_in, lp_in, buf,
    acc_ref, mp_ref, lp_ref, kv_ref, vx_ref, m_ref, l_ref, sems,
):
    sources(
        new_len, const, meta_ref, q_ref, qn_ref, (buf,), acc_in, mp_in, lp_in,
        acc_ref, kv_ref, vx_ref, m_ref, l_ref, sems,
    )
    mp_ref[...] = pack_lanes(m_ref, slice(None))
    lp_ref[...] = pack_lanes(l_ref, slice(None))


def last_kernel(
    new_len, const, meta_ref, q_ref, qn_ref, acc_in, mp_in, lp_in, buf_a, buf_b,
    out_a, out_b, out_c, out_d, acc_ref, kv_ref, vx_ref, m_ref, l_ref, sems,
):
    sources(
        new_len, const, meta_ref, q_ref, qn_ref, (buf_a, buf_b), acc_in, mp_in, lp_in,
        acc_ref, kv_ref, vx_ref, m_ref, l_ref, sems,
    )
    tokens = q_ref.shape[0]
    heads = m_ref.shape[0]
    part = tokens // CTX
    rank = meta_ref[8]
    row = lax.broadcasted_iota(jnp.int32, (16, heads * 128), 0)
    for step, out_ref in enumerate((out_a, out_b, out_c, out_d)):
        place = lax.rem(rank + step, CTX)
        rows = pl.ds(pl.multiple_of(place * part, part), part)
        for head in range(heads):
            cols = slice(head * 128, head * 128 + 128)
            total = l_ref[head, rows, :]
            empty = total == 0.0
            safe = jnp.where(empty, 1.0, total)
            out_ref[:part, cols] = (acc_ref[rows, cols] / safe).astype(BF16)
            m_ref[head, rows, :] = jnp.where(
                empty, NEG_FILL, m_ref[head, rows, :] + jnp.log2(safe)
            )
        turned = pack_lanes(m_ref, rows).T
        line = jnp.concatenate([turned[h : h + 1] for h in range(heads)], axis=1)
        high = line.astype(BF16).astype(F32)
        rest = line - high
        mid = rest.astype(BF16).astype(F32)
        low = rest - mid
        tile = jnp.where(row == 0, high, jnp.where(row == 1, mid, jnp.where(row == 2, low, 0.0)))
        out_ref[part : part + 16, :] = tile.astype(BF16)


def scratch(tokens, heads, blocks, lead=()):
    return [
        pltpu.VMEM(lead + (blocks, 2, 128, 128), BF16),
        pltpu.VMEM((blocks * 128, 256), BF16),
        pltpu.VMEM((heads, tokens, 128), F32),
        pltpu.VMEM((heads, tokens, 128), F32),
    ]


def state_shapes(tokens, q_cols):
    return [
        jax.ShapeDtypeStruct((tokens, q_cols), F32),
        jax.ShapeDtypeStruct((tokens, 128), F32),
        jax.ShapeDtypeStruct((tokens, 128), F32),
    ]


def attend_own(meta, quarters, buf, new_len, const):
    part = quarters[0].shape[0]
    q_cols = quarters[0].shape[1] - 256
    tokens = part * CTX
    heads = q_cols // 128
    blocks = buf.shape[0]
    return pl.pallas_call(
        lambda *refs: first_kernel(new_len, const, *refs),
        out_shape=[
            jax.ShapeDtypeStruct((tokens, q_cols), BF16),
            jax.ShapeDtypeStruct((tokens, 128), F32),
        ]
        + state_shapes(tokens, q_cols)
        + [jax.ShapeDtypeStruct((CTX, 2, part, 128), BF16)],
        in_specs=[smem()] + [vmem()] * 4 + [anywhere()],
        out_specs=[vmem()] * 6,
        scratch_shapes=scratch(tokens, heads, blocks) + [pltpu.SemaphoreType.DMA(())],
        compiler_params=params(),
        cost_estimate=NO_COST,
        name="attend_own",
    )(meta, *quarters, buf)


def attend_near(meta, queries, norms, state, bufs, new_len, const):
    tokens, q_cols = queries.shape
    heads = q_cols // 128
    blocks = bufs[0].shape[0]
    return pl.pallas_call(
        lambda *refs: near_kernel(new_len, const, *refs),
        out_shape=state_shapes(tokens, q_cols),
        in_specs=[smem()] + [vmem()] * 5 + [anywhere()] * len(bufs),
        out_specs=[vmem()] * 3,
        scratch_shapes=scratch(tokens, heads, blocks, (len(bufs),))
        + [pltpu.SemaphoreType.DMA((len(bufs),))],
        compiler_params=params(),
        cost_estimate=NO_COST,
        name="attend_near",
    )(meta, queries, norms, *state, *bufs)


def attend_last(meta, queries, norms, state, bufs, new_len, const):
    tokens, q_cols = queries.shape
    heads = q_cols // 128
    blocks = bufs[0].shape[0]
    pairs = blocks * 128 * tokens // 2 * heads
    return pl.pallas_call(
        lambda *refs: last_kernel(new_len, const, *refs),
        out_shape=[jax.ShapeDtypeStruct((tokens // CTX + 16, q_cols), BF16)] * CTX,
        in_specs=[smem()] + [vmem()] * 5 + [anywhere()] * len(bufs),
        out_specs=[vmem()] * CTX,
        scratch_shapes=[pltpu.VMEM((tokens, q_cols), F32)]
        + scratch(tokens, heads, blocks, (len(bufs),))
        + [pltpu.SemaphoreType.DMA((len(bufs),))],
        compiler_params=params(),
        cost_estimate=pl.CostEstimate(
            flops=pairs * 512, bytes_accessed=8 << 20, transcendentals=pairs
        ),
        name="attend_last",
    )(meta, queries, norms, *state, *bufs)


def combine_kernel(*refs):
    in_refs, out_ref = refs[:CTX], refs[CTX]
    part, q_cols = out_ref.shape
    heads = q_cols // 128
    lines = []
    for c in range(CTX):
        tile = in_refs[c][part : part + 16, :].astype(F32)
        lines.append(tile[0:1] + tile[1:2] + tile[2:3])
    top = lines[0]
    for line in lines[1:]:
        top = jnp.maximum(top, line)
    shares = [jnp.exp2(line - top) for line in lines]
    total = shares[0] + shares[1] + shares[2] + shares[3]
    pieces = []
    for share in shares:
        share = share / total
        pieces += [share[:, h * 128 : h * 128 + 128] for h in range(heads)]
    pieces.append(jnp.zeros((128 - CTX * heads, 128), F32))
    turned = jnp.concatenate(pieces, axis=0).T
    for head in range(heads):
        cols = slice(head * 128, head * 128 + 128)
        mixed = jnp.zeros((part, 128), F32)
        for c in range(CTX):
            at = c * heads + head
            mixed = mixed + in_refs[c][:part, cols].astype(F32) * turned[:, at : at + 1]
        out_ref[:, cols] = mixed.astype(BF16)


def combine(arrived):
    rows, q_cols = arrived[0].shape
    return pl.pallas_call(
        combine_kernel,
        out_shape=jax.ShapeDtypeStruct((rows - 16, q_cols), BF16),
        in_specs=[vmem()] * CTX,
        out_specs=vmem(),
        compiler_params=params(),
        cost_estimate=NO_COST,
        name="combine",
    )(*arrived)


def out_kernel(
    meta_ref, place_ref, a, b, c, d, w_ref, new_a, new_b, new_c, new_d, pool_in,
    own_ref, send_ref, pool_out, rows_ref, sems,
):
    rank = meta_ref[0]
    core = meta_ref[1]
    part = a.shape[0]
    half = own_ref.shape[2]

    def place_blocks(act):
        count = new_a.shape[0]
        for n, ref in enumerate((new_a, new_b, new_c, new_d)):
            for i in range(count):
                at = n * count + i
                slot = place_ref[at]

                @pl.when(slot >= 0)
                def _(ref=ref, i=i, at=at, slot=slot):
                    act(pltpu.make_async_copy(ref.at[i], pool_out.at[slot], sems.at[at]))

    @pl.when(pl.program_id(0) == 0)
    def _():
        place_blocks(lambda copy: copy.start())
        for step, ref in enumerate((a, b, c, d)):
            place = lax.rem(rank + CTX - step, CTX)
            rows_ref[pl.ds(pl.multiple_of(place * part, part), part), :] = ref[...]

    product = jnp.dot(rows_ref[...], w_ref[...], preferred_element_type=F32)

    @pl.when(core == 0)
    def _():
        own_ref[0] = product[:, :half]
        send_ref[0] = product[:, half:].astype(BF16)

    @pl.when(core != 0)
    def _():
        own_ref[0] = product[:, half:]
        send_ref[0] = product[:, :half].astype(BF16)

    @pl.when(pl.program_id(0) == pl.num_programs(0) - 1)
    def _():
        place_blocks(lambda copy: copy.wait())


def project_out(meta, places, quarters, w_out, news, pool, planes):
    part, depth = quarters[0].shape
    tokens = part * CTX
    width = w_out.shape[1] // planes
    whole = pl.BlockSpec((part, depth), lambda i, *_: (0, 0))
    out = pl.BlockSpec((1, tokens, width // 2), lambda i, *_: (i, 0, 0))
    return pl.pallas_call(
        out_kernel,
        grid_spec=pltpu.PrefetchScalarGridSpec(
            num_scalar_prefetch=2,
            grid=(planes,),
            in_specs=[whole] * 4
            + [pl.BlockSpec((depth, width), lambda i, meta, _: (0, lax.rem(meta[2] + i, planes)))]
            + [anywhere()] * 5,
            out_specs=[out] * 2 + [anywhere()],
            scratch_shapes=[
                pltpu.VMEM((tokens, depth), BF16),
                pltpu.SemaphoreType.DMA((places.shape[0],)),
            ],
        ),
        out_shape=[
            jax.ShapeDtypeStruct((planes, tokens, width // 2), F32),
            jax.ShapeDtypeStruct((planes, tokens, width // 2), BF16),
            jax.ShapeDtypeStruct(pool.shape, BF16),
        ],
        input_output_aliases={11: 2},
        compiler_params=params(),
        cost_estimate=NO_COST,
        name="project_out",
    )(meta, places, *quarters, w_out, *news, pool)


def shifted(value, axis, step):
    size = lax.axis_size(axis)
    return lax.ppermute(value, axis, [(i, (i + step) % size) for i in range(size)])


def moved(value, step):
    return lax.ppermute(value, "group", list(enumerate(SEND[step])))


def around(value, axis):
    return [value] + [shifted(value, axis, step) for step in (1, 2, 3)]


def local(
    tokens, norm_gain, w_query, w_key, w_value, w_out, kv_pool, block_table, prefix_len, write_slot
):
    groups = lax.axis_size("group")
    ranks = lax.axis_size("ctx")
    tp_size = lax.axis_size("tp")
    rank = lax.axis_index("ctx")
    group = lax.axis_index("group")
    core = lax.axis_index("tp") % 2
    plane = lax.axis_index("tp") // 2
    pool_size = kv_pool.shape[0]
    sessions, list_len = block_table.shape
    sess_here = sessions // groups
    per_pair = sess_here * list_len // (groups * ranks)
    new_len = tokens.shape[0] // sess_here
    head_dim = kv_pool.shape[4]
    const = head_dim**-0.5 * LOG2E
    device_id = group * ranks + rank
    pool = kv_pool.reshape(pool_size, 2, head_dim, head_dim)

    table = block_table.reshape(groups, sess_here * list_len)
    send_to = jnp.array(SEND, jnp.int32)
    receive = jnp.array([[line.index(g) for g in range(groups)] for line in SEND], jnp.int32)
    send_table = table[lax.dynamic_index_in_dim(send_to, group, 1, keepdims=False)]
    here = send_table // pool_size == device_id
    upper = jnp.triu(jnp.ones((sess_here * list_len,) * 2, BF16))
    order = jnp.dot(here.astype(BF16), upper, preferred_element_type=F32).astype(jnp.int32)
    wanted = jnp.arange(1, per_pair + 1, dtype=jnp.int32)
    picked = here[:, None, :] & (order[:, None, :] == wanted[None, :, None])
    send_index = jnp.sum(jnp.where(picked, send_table[:, None, :] % pool_size, 0), axis=2)
    mine = lax.dynamic_index_in_dim(table, group, 0, keepdims=False).reshape(sess_here, list_len)
    lengths = lax.dynamic_slice_in_dim(prefix_len, group * sess_here, sess_here)
    source = lax.dynamic_index_in_dim(receive, group, 1, keepdims=False) * ranks + rank
    from_there = mine[None] // pool_size == source[:, None, None]
    slots = jnp.arange(list_len, dtype=jnp.int32)
    keys_in = jnp.clip(lengths[:, None] - slots[None, :] * head_dim, 0, head_dim)
    live_keys = jnp.sum(jnp.where(from_there, keys_in[None], 0), axis=2)
    counts = jnp.sum(from_there.astype(jnp.int32), axis=2)
    starts = jnp.cumsum(counts, axis=1) - counts
    meta = jnp.stack([starts, live_keys], axis=2).reshape(groups, 2 * sess_here).astype(jnp.int32)

    rank_only = rank[None].astype(jnp.int32)
    begun = project(
        rank_only, send_index[1:], pool,
        tokens, norm_gain[None, :], w_query, w_key, w_value,
    )
    parts = begun[:ranks]
    early = [moved(begun[ranks], 1), moved(begun[ranks + 1], 2)]
    far = moved(begun[ranks + 2], 3)
    rest, _ = lax.optimization_barrier((send_index[:1], parts[0]))
    own_blocks, new_pool = pack(rest, pool)
    parts = [parts[0]] + [shifted(parts[step], "ctx", step) for step in (1, 3, 2)]
    parts, own_blocks = lax.optimization_barrier((parts, own_blocks))
    fresh = finish(parts, tokens.shape[1] * ranks)
    quarters = around(fresh, "ctx")

    first_meta = jnp.concatenate([rank_only, meta[0]])
    queries, norms, *state, block = attend_own(
        first_meta, quarters, own_blocks, new_len, const
    )
    state = attend_near(meta[1], queries, norms, state, [early[0]], new_len, const)
    last_meta = jnp.concatenate([meta[2], meta[3], rank_only])
    partial = attend_last(last_meta, queries, norms, state, [early[1], far], new_len, const)
    partial = [partial[0]] + [shifted(partial[step], "ctx", step) for step in (1, 2, 3)]
    attended = combine(partial)

    planes = tp_size // 2
    out_meta = jnp.stack([rank, core, plane]).astype(jnp.int32)
    news = around(block, "group")
    targets = jnp.roll(write_slot.reshape(groups, ranks)[::-1], group + 1, axis=0).reshape(-1)
    places = jnp.where(targets // pool_size == device_id, targets % pool_size, -1)
    own, send, new_pool = project_out(
        out_meta, places, around(attended, "ctx"), w_out, news, new_pool, planes
    )
    other = lax.ppermute(send, "tp", [(i, i ^ 1) for i in range(tp_size)])
    total = own[0] + other[0].astype(F32)
    for step in range(1, planes):
        pair = (own[step] + other[step].astype(F32)).astype(BF16)
        total = total + shifted(pair, "tp", 2 * step).astype(F32)
    return (total.astype(BF16), new_pool.reshape(kv_pool.shape))


def solution(mesh):
    placed = (
        P("group", "ctx"),
        P("ctx"),
        P("ctx", "tp"),
        P("ctx", "tp"),
        P("ctx", "tp"),
        P("tp", "ctx"),
        P(("group", "ctx"), None, "tp", None, None),
        P(),
        P(),
        P(),
    )
    return jax.shard_map(
        local,
        mesh=mesh,
        in_specs=placed,
        out_specs=(P("group", ("ctx", "tp")), P(("group", "ctx"), None, "tp", None, None)),
        check_vma=False,
    )
```
